32 devices in a mesh: img: 8 (over y, x, core), blk: 4 (over z).
Axes of the slice: x: 2, y: 2, z: 4, core: 2. Of those that a mesh axis runs over, the one named last changes fastest.
Arguments:
- inputs: bfloat16 [16384, 1152], P(('img', 'blk')), may hold values from -6 to 6
- token_image: int32 [16384], P(('img', 'blk')), may hold values from 0 to 7, as said below
- image_time: int32 [64], replicated, may hold values from 0 to 999
- image_class: int32 [64], replicated, may hold values from 0 to 1000
- targets: bfloat16 [16384, 768], P(('img', 'blk')), may hold values from -6 to 6
- cotangent: bfloat16 [16384, 1152], P(('img', 'blk')), may hold values from -6 to 6
- class_table: bfloat16 [1001, 1152], P(None, 'img'), may hold values from -6 to 6
- modulate_weight: bfloat16 [1152, 6912], P('img'), may hold values from -0.1875 to 0.1875
- modulate_bias: bfloat16 [6912], replicated, may hold values from -4 to 4
- attend_weight: bfloat16 [1152, 3456], P('img'), may hold values from -0.1875 to 0.1875
- attend_bias: bfloat16 [2304], P('img'), may hold values from -3 to 3
- output_weight: bfloat16 [1152, 1152], P('img'), may hold values from -1.5 to 1.5
- output_bias: bfloat16 [1152], P('img'), may hold values from -3 to 3
- expand_weight: bfloat16 [1152, 4608], P('img'), may hold values from -0.1875 to 0.1875
- expand_bias: bfloat16 [4608], P('img'), may hold values from -3 to 3
- shrink_weight: bfloat16 [4608, 1152], P('img'), may hold values from -0.09375 to 0.09375
- shrink_bias: bfloat16 [1152], P('img'), may hold values from -3 to 3
- inner_weight: bfloat16 [1152, 2048], P('img'), may hold values from -0.1875 to 0.1875
- inner_bias: bfloat16 [2048], P('img'), may hold values from -3 to 3
- middle_weight: bfloat16 [2048, 2048], P('img'), may hold values from -0.125 to 0.125
- middle_bias: bfloat16 [2048], P('img'), may hold values from -3 to 3
- outer_weight: bfloat16 [2048, 768], P('img'), may hold values from -0.125 to 0.125
- outer_bias: bfloat16 [768], P('img'), may hold values from -4 to 4
Outputs:
- block_output: bfloat16 [16384, 1152], P(('img', 'blk'))
- input_gradient: bfloat16 [16384, 1152], P(('img', 'blk'))
- table_gradient: float32 [1001, 1152], P(None, 'img')
- modulate_weight_gradient: float32 [1152, 6912], P('img')
- modulate_bias_gradient: float32 [6912], replicated
- attend_weight_gradient: float32 [1152, 3456], P('img')
- attend_bias_gradient: float32 [2304], P('img')
- output_weight_gradient: float32 [1152, 1152], P('img')
- output_bias_gradient: float32 [1152], P('img')
- expand_weight_gradient: float32 [1152, 4608], P('img')
- expand_bias_gradient: float32 [4608], P('img')
- shrink_weight_gradient: float32 [4608, 1152], P('img')
- shrink_bias_gradient: float32 [1152], P('img')
- inner_weight_gradient: float32 [1152, 2048], P('img')
- inner_bias_gradient: float32 [2048], P('img')
- middle_weight_gradient: float32 [2048, 2048], P('img')
- middle_bias_gradient: float32 [2048], P('img')
- outer_weight_gradient: float32 [2048, 768], P('img')
- outer_bias_gradient: float32 [768], P('img')
The draws below stay inside these ranges and needn't reach their ends.
Inputs may be any that keep to these rules, and one draw needn't show every extreme that they name: `token_image`: within an image group every device of blk holds the same layout: each of the group's images (of 1024 or 256 tokens) owns one run of consecutive rows, an equal share of its tokens on every device of the group; slots are numbered 0, 1, ... in row order, every row belongs to an image, and slots past a group's count of images are unused.
All inputs are finite; a program needn't handle non-finite values.
Results may differ from the reference program's by a relative error of at most 0.025.
Values may be sent and summed in bfloat16 or wider, within the bound.
A program may use at most 384 MiB of HBM per device.

```python
import math
import jax
import jax.numpy as jnp
from jax import lax

D = 1152
HEADS = 16
HEAD_DIM = 72
FF = 4608
CLASSES = 1001
PROJ = 2048
EMBED = 768
LONG = 1024
SHORT = 256
TOK_DEV = 512
GROUP = 2048
SLOTS = 8
IMAGES = 64
TOKENS = 16384
N_IMG = 8
N_BLK = 4


def group_layout(key, longs):
    units = TOK_DEV * N_BLK // SHORT
    ratio = LONG // SHORT
    total = longs + units - ratio * longs
    position = jnp.arange(units)
    real = position < total
    scores = jnp.where(real, jax.random.randint(key, (units,), 0, 1 << 20) * units + position, (1 << 30) + position)
    order = jnp.argsort(scores, stable=True)
    kinds = jnp.where(order < longs, ratio, jnp.where(order < total, 1, 0))
    starts = jnp.cumsum(kinds) - kinds
    unit_of_row = jnp.arange(TOK_DEV) // (SHORT // N_BLK)
    image = jnp.sum(((starts[None, :] <= unit_of_row[:, None]) & real[None, :]).astype(jnp.int32), axis=1) - 1
    return jnp.tile(image[None, :], (N_BLK, 1)).reshape(-1)


def draw_token_image(key, part):
    key = jax.random.fold_in(key, 11)
    most_long = TOK_DEV * N_BLK // LONG
    key_count, key_pick, key_other, key_order = jax.random.split(key, 4)
    longs = jax.random.randint(key_count, (N_IMG,), 0, most_long + 1)
    empty_group = jax.random.randint(key_pick, (), 0, N_IMG)
    full_group = (empty_group + 1 + jax.random.randint(key_other, (), 0, N_IMG - 1)) % N_IMG
    group_ids = jnp.arange(N_IMG)
    longs = jnp.where(group_ids == empty_group, 0, longs)
    longs = jnp.where(group_ids == full_group, most_long, longs)
    keys = jax.random.split(key_order, N_IMG)
    return jax.vmap(group_layout)(keys, longs).reshape(-1).astype(jnp.int32)


def draw_targets(key, part):
    key = jax.random.fold_in(key, 21)
    values = jnp.clip(jax.random.normal(key, (TOKENS, EMBED), jnp.float32), -6.0, 6.0)
    return values.astype(jnp.bfloat16)


def draw_outer_bias(key, part):
    key = jax.random.fold_in(key, 22)
    values = 0.4 * jnp.clip(jax.random.normal(key, (EMBED,), jnp.float32), -4.0, 4.0)
    return values.astype(jnp.bfloat16)


def touch_ends(result, rng, least, top_value):
    longest = result.shape.index(max(result.shape))
    spots = []
    for shift in (0, 1):
        where = [jax.random.randint(jax.random.fold_in(rng, axis), (), 0, length) for axis, length in enumerate(result.shape)]
        where[longest] = (where[longest] + shift) % result.shape[longest]
        spots.append(tuple(where))
    return result.at[spots[0]].set(least).at[spots[1]].set(top_value)


def block_scale(key, shape, shards, smallest, largest):
    factor_of = 1.0
    for dim, parts in shards:
        steps = jax.random.uniform(jax.random.fold_in(jax.random.fold_in(key, 6), dim), (parts,), jnp.float32, smallest / len(shards), largest / len(shards))
        factor_of = factor_of * jnp.repeat(jnp.exp(steps), shape[dim] // parts).reshape((-1,) + (1,) * (len(shape) - 1 - dim))
    return factor_of


def noise(stream_key, shape, scale, most, cuts=(), dtype=jnp.bfloat16):
    array = jax.random.normal(stream_key, shape, jnp.float32) * scale
    if len(cuts) > 0:
        array = block_scale(stream_key, shape, cuts, -0.22, 0.18) * array
    return jnp.clip(array, min=-most, max=most).astype(dtype)


def setup_inputs(seed: int = 0) -> dict:
    splits = jax.random.split(jax.random.key(seed), 24)
    return {
        "inputs": noise(splits[0], (TOKENS, D), 1.0, 6.0, ((0, 32),)),
        "token_image": draw_token_image(jax.random.fold_in(splits[23], 71), 0),
        "image_time": touch_ends(jax.random.randint(splits[2], (IMAGES,), 0, 1000), jax.random.fold_in(splits[2], 1), 0, 999).astype(jnp.int32),
        "image_class": touch_ends(jax.random.randint(splits[3], (IMAGES,), 0, CLASSES), jax.random.fold_in(splits[3], 1), 0, CLASSES - 1).astype(jnp.int32),
        "targets": draw_targets(jax.random.fold_in(splits[23], 71), 0),
        "cotangent": noise(splits[5], (TOKENS, D), 1.0, 6.0, ((0, 32),)),
        "class_table": noise(splits[6], (CLASSES, D), 1.0, 6.0, ((1, 8),)),
        "modulate_weight": noise(splits[7], (D, 6 * D), D ** -0.5, 0.1875, ((0, 8),)),
        "modulate_bias": noise(splits[8], (6 * D,), 0.3, 4.0),
        "attend_weight": noise(splits[9], (D, 3 * D), D ** -0.5, 0.1875, ((0, 8),)),
        "attend_bias": noise(splits[10], (2 * D,), 0.2, 3.0, ((0, 8),)),
        "output_weight": noise(splits[11], (D, D), (D // 64) ** -0.5, 1.5, ((0, 8),)),
        "output_bias": noise(splits[12], (D,), 0.2, 3.0, ((0, 8),)),
        "expand_weight": noise(splits[13], (D, FF), D ** -0.5, 0.1875, ((0, 8),)),
        "expand_bias": noise(splits[14], (FF,), 0.2, 3.0, ((0, 8),)),
        "shrink_weight": noise(splits[15], (FF, D), FF ** -0.5, 0.09375, ((0, 8),)),
        "shrink_bias": noise(splits[16], (D,), 0.2, 3.0, ((0, 8),)),
        "inner_weight": noise(splits[17], (D, PROJ), D ** -0.5, 0.1875, ((0, 8),)),
        "inner_bias": noise(splits[18], (PROJ,), 0.2, 3.0, ((0, 8),)),
        "middle_weight": noise(splits[19], (PROJ, PROJ), PROJ ** -0.5, 0.125, ((0, 8),)),
        "middle_bias": noise(splits[20], (PROJ,), 0.2, 3.0, ((0, 8),)),
        "outer_weight": noise(splits[21], (PROJ, EMBED), PROJ ** -0.5, 0.125, ((0, 8),)),
        "outer_bias": draw_outer_bias(jax.random.fold_in(splits[23], 71), 0),
    }


HIGH = lax.Precision.HIGHEST
EPSILON = 1e-06
NEGATIVE = -1e+30

@jax.custom_vjp
def low(v):
    return lax.optimization_barrier(v.astype(jnp.bfloat16)).astype(jnp.float32)

@jax.custom_vjp
def low_back(v):
    return v

def low_keep(v):
    return (low(v), None)

def low_pass(kept, grad):
    return (grad,)

def back_keep(v):
    return (v, None)

def back_low(kept, grad):
    return (low(grad),)
low.defvjp(low_keep, low_pass)
low_back.defvjp(back_keep, back_low)

def layer_norm(values):
    mean = lax.optimization_barrier(jnp.mean(values, axis=-1, keepdims=True))
    centered = values - mean
    variance = lax.optimization_barrier(jnp.mean(centered * centered, axis=-1, keepdims=True))
    return centered * lax.rsqrt(variance + EPSILON)

def matmul(left, right):
    return jnp.dot(left, right, precision=HIGH)

def time_embedding(steps, width):
    half = width // 2
    index = jnp.arange(half).astype(jnp.float32)
    frequency = jnp.exp(-math.log(10000.0) * index / half)
    angle = steps.astype(jnp.float32)[:, None] * frequency[None, :]
    return jnp.concatenate([jnp.cos(angle), jnp.sin(angle)], axis=1)

def attend_group(pieces):
    query, key, value, labels = pieces
    count = query.shape[0]
    query_heads = query.reshape(count, HEADS, HEAD_DIM)
    key_heads = key.reshape(count, HEADS, HEAD_DIM)
    value_heads = value.reshape(count, HEADS, HEAD_DIM)
    scale = 1.0 / math.sqrt(HEAD_DIM)
    scores = low_back(jnp.einsum('qhd,khd->hqk', query_heads, key_heads, precision=HIGH) * scale)
    mask = (labels[:, None] == labels[None, :])[None]
    masked = jnp.where(mask, scores, NEGATIVE)
    top = lax.optimization_barrier(jnp.max(masked, axis=2, keepdims=True))
    raised = jnp.where(mask, jnp.exp(masked - top), 0.0)
    weights = low(raised / lax.optimization_barrier(jnp.sum(raised, axis=2, keepdims=True)))
    attended = jnp.einsum('hqk,khd->qhd', weights, value_heads, precision=HIGH)
    return attended.reshape(count, HEADS * HEAD_DIM)

def forward(floats, token_image, image_time, image_class):
    inputs, targets, class_table, modulate_weight, modulate_bias, attend_weight, attend_bias, output_weight, output_bias, expand_weight, expand_bias, shrink_weight, shrink_bias, inner_weight, inner_bias, middle_weight, middle_bias, outer_weight, outer_bias = floats
    condition = jnp.take(class_table, image_class, axis=0) + time_embedding(image_time, D)
    silu_condition = low(jax.nn.silu(condition))
    modulation = matmul(silu_condition, modulate_weight) + modulate_bias
    image_of_row = jnp.arange(TOKENS) // GROUP * SLOTS + token_image
    row_modulation = jnp.take(modulation, image_of_row, axis=0)
    shift_one, scale_one, gate_one, shift_two, scale_two, gate_two = jnp.split(row_modulation, 6, axis=1)
    modulated1 = low(layer_norm(inputs) * (1.0 + scale_one) + shift_one)
    bias_full = jnp.concatenate([attend_bias[:D], jnp.zeros((D,), jnp.float32), attend_bias[D:]])
    projected = low(low_back(matmul(modulated1, attend_weight) + bias_full))
    query = projected[:, :D].reshape(N_IMG, GROUP, D)
    key = projected[:, D:2 * D].reshape(N_IMG, GROUP, D)
    value = projected[:, 2 * D:].reshape(N_IMG, GROUP, D)
    labels = token_image.reshape(N_IMG, GROUP)
    attended = lax.map(jax.checkpoint(attend_group), (query, key, value, labels)).reshape(TOKENS, D)
    attended = low(low_back(attended))
    branch1 = low_back(matmul(attended, output_weight) + output_bias)
    middle = inputs + gate_one * branch1
    modulated2 = low(layer_norm(middle) * (1.0 + scale_two) + shift_two)
    expanded = low_back(matmul(modulated2, expand_weight) + expand_bias)
    activated = low(jax.nn.gelu(expanded, approximate=True))
    branch2 = low_back(matmul(activated, shrink_weight) + shrink_bias)
    whole = middle + gate_two * branch2
    carried = low(whole)
    first = low(jax.nn.silu(low_back(matmul(carried, inner_weight) + inner_bias)))
    second = low(jax.nn.silu(low_back(matmul(first, middle_weight) + middle_bias)))
    aligned = low_back(matmul(second, outer_weight) + outer_bias)
    cross = lax.optimization_barrier(jnp.sum(aligned * targets, axis=1))
    aligned_inverse = lax.rsqrt(lax.optimization_barrier(jnp.sum(aligned * aligned, axis=1)) + EPSILON)
    target_inverse = lax.rsqrt(lax.optimization_barrier(jnp.sum(targets * targets, axis=1)) + EPSILON)
    cosine = cross * aligned_inverse * target_inverse
    loss = 0.5 * jnp.sum(1.0 - cosine)
    return (whole, loss)

def reference(inputs, token_image, image_time, image_class, targets, cotangent, class_table, modulate_weight, modulate_bias, attend_weight, attend_bias, output_weight, output_bias, expand_weight, expand_bias, shrink_weight, shrink_bias, inner_weight, inner_bias, middle_weight, middle_bias, outer_weight, outer_bias):
    floats = tuple((value.astype(jnp.float32) for value in (inputs, targets, class_table, modulate_weight, modulate_bias, attend_weight, attend_bias, output_weight, output_bias, expand_weight, expand_bias, shrink_weight, shrink_bias, inner_weight, inner_bias, middle_weight, middle_bias, outer_weight, outer_bias)))

    def run(*values):
        return forward(values, token_image, image_time, image_class)
    (whole, loss), pullback = jax.vjp(run, *floats)
    grads = pullback((cotangent.astype(jnp.float32), jnp.ones((), jnp.float32)))
    return (whole.astype(jnp.bfloat16), grads[0].astype(jnp.bfloat16), grads[2], grads[3], grads[4], grads[5], grads[6], grads[7], grads[8], grads[9], grads[10], grads[11], grads[12], grads[13], grads[14], grads[15], grads[16], grads[17], grads[18])
```

```python
from functools import partial
import math

import jax
import jax.numpy as jnp
from jax import lax
from jax.experimental import pallas as pl
from jax.experimental.pallas import tpu as pltpu
from jax.sharding import PartitionSpec as P

HEADS = 16
SHORT = 256
RATIO = 4
LANES = 128

EPSILON = 1e-06
HIGH = lax.Precision.HIGHEST
BF = jnp.bfloat16
F32 = jnp.float32


def layer_norm(values):
    mean = jnp.mean(values, axis=-1, keepdims=True)
    centered = values - mean
    variance = jnp.mean(centered * centered, axis=-1, keepdims=True)
    inverse = lax.rsqrt(variance + EPSILON)
    return (centered * inverse, inverse)


def norm_back(grad, normal, inverse):
    mean_grad = jnp.mean(grad, axis=-1, keepdims=True)
    mean_cross = jnp.mean(grad * normal, axis=-1, keepdims=True)
    return inverse * (grad - mean_grad - normal * mean_cross)


def local_back(function, point, grad):
    return jax.vjp(function, point)[1](grad)[0]


def left_product(left, right):
    return jnp.einsum("ti,to->io", left, right, preferred_element_type=F32).astype(BF)


def right_product(grad, weight):
    return jnp.einsum("to,io->ti", grad, weight, preferred_element_type=F32)


def column_sum(values):
    return jnp.sum(values.astype(F32), axis=0)


def dot(left, right):
    return jnp.dot(left, right, preferred_element_type=F32)


def dot_general(left, right, contract):
    return lax.dot_general(left, right, ((contract[:1], contract[1:]), ((), ())), preferred_element_type=F32)


def softmax_keys(keys, queries, scale):
    scores = dot_general(keys, queries, (1, 1)) * scale
    raised = jnp.exp(scores - jnp.max(scores, axis=0, keepdims=True))
    return raised * (1.0 / jnp.sum(raised, axis=0, keepdims=True))


def attend_forward_kernel(heads, scale, start_ref, length_ref, qkv_ref, pick_ref, out_ref):
    parts, _, unit, _ = qkv_ref.shape
    u = pl.program_id(0)
    first = start_ref[u]

    def work(span):
        outs = []
        for h in range(heads):

            def head(which, lo, n):
                at = (which * heads + h) * LANES
                return qkv_ref[:, pl.ds(lo, n), :, at : at + LANES].reshape(parts * n * unit, LANES)

            chance = softmax_keys(head(1, first, span), head(0, u, 1), scale).astype(BF)
            outs.append(dot_general(chance, head(2, first, span), (0, 0)).astype(BF))
        packed = dot(jnp.concatenate(outs, axis=1), pick_ref[...]).astype(BF)
        out_ref[...] = packed.reshape(out_ref.shape)

    pl.when(length_ref[u] == 1)(lambda: work(1))
    pl.when(length_ref[u] != 1)(lambda: work(RATIO))


def attend_backward_kernel(
    heads, scale, start_ref, length_ref, qkv_ref, grad_ref, spread_ref, pick_ref, out_ref, dq, dk, dv
):
    parts, units, unit, _ = qkv_ref.shape
    u = pl.program_id(0)
    first = start_ref[u]

    @pl.when(u == 0)
    def _():
        dk[...] = jnp.zeros_like(dk)
        dv[...] = jnp.zeros_like(dv)

    def work(span):
        grads = dot(grad_ref[...].reshape(parts * unit, -1), spread_ref[...]).astype(BF)
        for h in range(heads):

            def head(which, lo, n):
                at = (which * heads + h) * LANES
                return qkv_ref[:, pl.ds(lo, n), :, at : at + LANES].reshape(parts * n * unit, LANES)

            at = slice(h * LANES, (h + 1) * LANES)
            grad = grads[:, at]
            query, key, value = head(0, u, 1), head(1, first, span), head(2, first, span)
            chance = softmax_keys(key, query, scale)
            chance_grad = dot_general(value, grad, (1, 1))
            offset = jnp.sum(chance * chance_grad, axis=0, keepdims=True)
            score_grad = (chance * (chance_grad - offset)).astype(BF)
            into = (parts, span, unit, LANES)
            dv[:, pl.ds(first, span), :, at] += dot(chance.astype(BF), grad).reshape(into)
            dk[:, pl.ds(first, span), :, at] += (dot(score_grad, query) * scale).reshape(into)
            dq[:, pl.ds(u, 1), :, at] = (
                (dot_general(score_grad, key, (0, 0)) * scale).astype(BF).reshape(parts, 1, unit, LANES)
            )

    pl.when(length_ref[u] == 1)(lambda: work(1))
    pl.when(length_ref[u] != 1)(lambda: work(RATIO))

    @pl.when(u == units - 1)
    def _():
        def pack(i, carry):
            rows = [ref[:, pl.ds(i, 1)].astype(BF).reshape(parts * unit, -1) for ref in (dq, dk, dv)]
            packed = dot(jnp.concatenate(rows, axis=1), pick_ref[...]).astype(BF)
            out_ref[:, pl.ds(i, 1)] = packed.reshape(parts, 1, unit, -1)
            return carry

        lax.fori_loop(0, units, pack, 0)


def picker(heads, head_dim, dtype):
    row = jnp.arange(heads * LANES)[:, None]
    col = jnp.arange(heads * head_dim)[None, :]
    return ((row // LANES == col // head_dim) & (row % LANES == col % head_dim)).astype(dtype)


def attend_forward(start, length, qkv, heads, head_dim):
    parts, units, unit, lanes = qkv.shape
    width = heads * head_dim
    whole = lambda *shape: pl.BlockSpec(shape, lambda u, *_: (0,) * len(shape))
    return pl.pallas_call(
        partial(attend_forward_kernel, heads, 1.0 / math.sqrt(head_dim)),
        grid_spec=pltpu.PrefetchScalarGridSpec(
            num_scalar_prefetch=2,
            grid=(units,),
            in_specs=[whole(parts, units, unit, lanes), whole(heads * LANES, width)],
            out_specs=pl.BlockSpec((parts, 1, unit, width), lambda u, *_: (0, u, 0, 0)),
        ),
        out_shape=jax.ShapeDtypeStruct((parts, units, unit, width), BF),
        compiler_params=pltpu.CompilerParams(vmem_limit_bytes=48 * 2**20),
        cost_estimate=pl.CostEstimate(flops=10 * 2**30, bytes_accessed=16 * 2**20, transcendentals=2**23),
        name="attend_forward",
    )(start, length, qkv, picker(heads, head_dim, BF))


def attend_backward(start, length, qkv, grad, heads, head_dim):
    parts, units, unit, lanes = qkv.shape
    width = heads * head_dim
    whole = lambda *shape: pl.BlockSpec(shape, lambda u, *_: (0,) * len(shape))
    pick = picker(heads, head_dim, BF)
    return pl.pallas_call(
        partial(attend_backward_kernel, heads, 1.0 / math.sqrt(head_dim)),
        grid_spec=pltpu.PrefetchScalarGridSpec(
            num_scalar_prefetch=2,
            grid=(units,),
            in_specs=[
                whole(parts, units, unit, lanes),
                pl.BlockSpec((parts, 1, unit, width), lambda u, *_: (0, u, 0, 0)),
                whole(width, heads * LANES),
                whole(3 * heads * LANES, 3 * width),
            ],
            out_specs=whole(parts, units, unit, 3 * width),
            scratch_shapes=[
                pltpu.VMEM((parts, units, unit, heads * LANES), BF),
                pltpu.VMEM((parts, units, unit, heads * LANES), F32),
                pltpu.VMEM((parts, units, unit, heads * LANES), F32),
            ],
        ),
        out_shape=jax.ShapeDtypeStruct((parts, units, unit, 3 * width), BF),
        compiler_params=pltpu.CompilerParams(vmem_limit_bytes=56 * 2**20),
        cost_estimate=pl.CostEstimate(flops=40 * 2**30, bytes_accessed=16 * 2**20, transcendentals=2**23),
        name="attend_backward",
    )(start, length, qkv, grad, pick.T, picker(3 * heads, head_dim, BF))


def flips(n, bit):
    return [(i, i ^ bit) for i in range(n)]


def scatter_steps(left, right):
    devices = lax.axis_size("img")
    place = lax.axis_index("img")
    count, depth = left.shape
    columns = right.shape[1]
    blocks = left.reshape(count, devices, depth // devices)

    def of(*masks):
        picked = [lax.dynamic_index_in_dim(blocks, place ^ m, axis=1, keepdims=False) for m in masks]
        return jnp.concatenate(picked, axis=1)

    rows = depth // devices
    sent = left_product(of(1, 3, 5, 7), right)
    got = lax.ppermute(sent, "img", flips(devices, 1))
    own = jnp.einsum("ti,to->io", of(0, 2, 4, 6), right, preferred_element_type=F32) + got.astype(F32)
    own = own.astype(BF).reshape(4, rows, columns)
    half = columns // 2 // LANES * LANES
    one, two = own[:, :, :half], own[:, :, half:]
    got_x = lax.ppermute(jnp.stack([one[1], one[3]]), "img", flips(devices, 2)).astype(F32)
    got_y = lax.ppermute(jnp.stack([two[2], two[3]]), "img", flips(devices, 4)).astype(F32)
    next_y = (one[2].astype(F32) + got_x[1]).astype(BF)
    next_x = (two[1].astype(F32) + got_y[1]).astype(BF)
    got_y2 = lax.ppermute(next_y, "img", flips(devices, 4)).astype(F32)
    got_x2 = lax.ppermute(next_x, "img", flips(devices, 2)).astype(F32)
    first = one[0].astype(F32) + got_x[0] + got_y2
    second = two[0].astype(F32) + got_y[0] + got_x2
    return jnp.concatenate([first, second], axis=1).astype(BF)


def line_sum(values):
    place = lax.axis_index("blk")
    inner = (place == 1) | (place == 2)
    values = (values.astype(F32) + lax.ppermute(values, "blk", [(0, 1), (3, 2)]).astype(F32)).astype(BF)
    total = (values.astype(F32) + lax.ppermute(values, "blk", [(1, 2), (2, 1)]).astype(F32)).astype(BF)
    back = lax.ppermute(total, "blk", [(1, 0), (2, 3)])
    return jnp.where(inner, total, back)


def per_device(
    inputs,
    token_image,
    image_time,
    image_class,
    targets,
    cotangent,
    class_table,
    modulate_weight,
    modulate_bias,
    attend_weight,
    attend_bias,
    output_weight,
    output_bias,
    expand_weight,
    expand_bias,
    shrink_weight,
    shrink_bias,
    inner_weight,
    inner_bias,
    middle_weight,
    middle_bias,
    outer_weight,
    outer_bias,
):
    count, width = inputs.shape
    head_dim = width // HEADS
    columns = class_table.shape[1]
    devices, parts = lax.axis_size("img"), lax.axis_size("blk")
    place_img, place_blk = lax.axis_index("img"), lax.axis_index("blk")
    slots = image_class.shape[0] // devices
    unit = SHORT // parts
    units = count // unit
    heads = HEADS // parts
    mine = heads * head_dim
    half = width // 2

    class_hot = (image_class[:, None] == jnp.arange(class_table.shape[0])[None, :]).astype(BF)
    column = place_img * columns + jnp.arange(columns)
    frequency = jnp.exp(-math.log(10000.0) * (column % half).astype(F32) / half)
    angle = image_time.astype(F32)[:, None] * frequency[None, :]
    condition = dot(class_hot, class_table) + jnp.where(column[None, :] < half, jnp.cos(angle), jnp.sin(angle))
    silu_condition = jax.nn.silu(condition).astype(BF)
    shares = dot(silu_condition, modulate_weight)
    biases = (attend_bias, output_bias, expand_bias, shrink_bias, inner_bias, middle_bias, outer_bias)
    bias_row = jnp.concatenate(biases).astype(F32)
    wide = shares.shape[1]
    tail = jnp.broadcast_to(jnp.pad(bias_row, (0, wide - bias_row.shape[0])), (devices, 1, wide))
    sent = jnp.concatenate([shares.reshape(devices, slots, wide), tail], axis=1)
    got = lax.all_to_all(sent, "img", split_axis=0, concat_axis=0, tiled=True)
    modulation = jnp.sum(got[:, :slots], axis=0) + modulate_bias.astype(F32)[None, :]
    full_biases = []
    at = 0
    for bias in biases:
        full_biases.append(got[:, slots, at : at + bias.shape[0]].reshape(-1))
        at += bias.shape[0]
    (
        attend_bias_full,
        output_bias_full,
        expand_bias_full,
        shrink_bias_full,
        inner_bias_full,
        middle_bias_full,
        outer_bias_full,
    ) = full_biases

    labels = token_image[::unit]
    same = labels[:, None] == labels[None, :]
    start = jnp.argmax(same, axis=1).astype(jnp.int32)
    length = jnp.sum(same, axis=1).astype(jnp.int32)
    unit_hot = (labels[:, None] == jnp.arange(slots)[None, :]).astype(F32)
    unit_modulation = jnp.dot(unit_hot, modulation, precision=HIGH)
    shift_one, scale_one, gate_one, shift_two, scale_two, gate_two = (
        block[:, None, :] for block in jnp.split(unit_modulation, 6, axis=1)
    )

    def by_unit(values):
        return values.reshape(units, unit, width)

    def by_row(values):
        return values.reshape(count, width)

    attend_mine = lax.dynamic_slice_in_dim(
        attend_weight.reshape(-1, 3, parts, mine), place_blk, 1, axis=2
    ).reshape(-1, 3 * mine)
    attend_full = lax.all_gather(attend_mine, "img", axis=0, tiled=True)
    output_full = lax.all_gather(output_weight, "img", axis=0, tiled=True)
    expand_full = lax.all_gather(expand_weight, "img", axis=0, tiled=True)
    shrink_full = lax.all_gather(shrink_weight, "img", axis=0, tiled=True)
    inner_full = lax.all_gather(inner_weight, "img", axis=0, tiled=True)
    middle_full = lax.all_gather(middle_weight, "img", axis=0, tiled=True)
    outer_full = lax.all_gather(outer_weight, "img", axis=0, tiled=True)

    source = by_unit(inputs.astype(F32))
    normal_one, inverse_one = layer_norm(source)
    modulated_one = by_row((normal_one * (1.0 + scale_one) + shift_one).astype(BF))
    modulated_group = lax.all_to_all(
        jnp.broadcast_to(modulated_one, (parts, count, width)), "blk", split_axis=0, concat_axis=0, tiled=True
    ).reshape(parts * count, width)

    def pad_heads(values):
        lead = values.shape[:-1]
        values = values.reshape(*lead, 3 * heads, head_dim)
        values = jnp.pad(values, ((0, 0),) * len(lead) + ((0, 0), (0, LANES - head_dim)))
        return values.reshape(*lead, 3 * heads * LANES)

    bias_mine = lax.dynamic_slice_in_dim(attend_bias_full.reshape(2, parts, mine), place_blk, 1, axis=1)
    bias_mine = jnp.concatenate([bias_mine[0, 0], jnp.zeros((mine,), F32), bias_mine[1, 0]])
    projected = dot(modulated_group, pad_heads(attend_full)) + pad_heads(bias_mine)[None, :]
    qkv = projected.astype(BF).reshape(parts, units, unit, 3 * heads * LANES)
    attended_heads = attend_forward(start, length, qkv, heads, head_dim)
    attended = lax.all_to_all(
        attended_heads.reshape(parts, count, mine), "blk", split_axis=0, concat_axis=0, tiled=True
    )
    output_heads = output_full.reshape(parts, mine, width)
    branch_one = by_unit(
        jnp.einsum("pti,pio->to", attended, output_heads, preferred_element_type=F32) + output_bias_full
    )
    middle = source + gate_one * branch_one
    normal_two, inverse_two = layer_norm(middle)
    modulated_two = by_row((normal_two * (1.0 + scale_two) + shift_two).astype(BF))
    expanded = dot(modulated_two, expand_full) + expand_bias_full
    gelu_tanh = partial(jax.nn.gelu, approximate=True)
    activated = gelu_tanh(expanded).astype(BF)
    branch_two = by_unit(dot(activated, shrink_full) + shrink_bias_full)
    whole = middle + gate_two * branch_two
    whole_low = by_row(whole.astype(BF))
    pre_one = dot(whole_low, inner_full) + inner_bias_full
    first = jax.nn.silu(pre_one).astype(BF)
    pre_two = dot(first, middle_full) + middle_bias_full
    second = jax.nn.silu(pre_two).astype(BF)
    aligned = dot(second, outer_full) + outer_bias_full
    target = targets.astype(F32)
    cross = jnp.sum(aligned * target, axis=1)
    aligned_inverse = lax.rsqrt(jnp.sum(aligned * aligned, axis=1) + EPSILON)
    target_inverse = lax.rsqrt(jnp.sum(target * target, axis=1) + EPSILON)
    cosine = cross * aligned_inverse * target_inverse
    grad_aligned = (
        -0.5
        * (
            target * (aligned_inverse * target_inverse)[:, None]
            - (cosine * aligned_inverse * aligned_inverse)[:, None] * aligned
        )
    ).astype(BF)

    def scatter(left, right):
        if devices == 8:
            return scatter_steps(left, right)
        return lax.psum_scatter(left_product(left, right), "img", scatter_dimension=0, tiled=True)

    def total(part):
        return line_sum(part) if parts == 4 else lax.psum(part, "blk")

    outer_sum = total(scatter(second, grad_aligned))
    grad_outer_bias = column_sum(grad_aligned)
    grad_pre_two = local_back(jax.nn.silu, pre_two, right_product(grad_aligned, outer_full)).astype(BF)
    middle_sum = total(scatter(first, grad_pre_two))
    grad_middle_bias = column_sum(grad_pre_two)
    grad_pre_one = local_back(jax.nn.silu, pre_one, right_product(grad_pre_two, middle_full)).astype(BF)
    inner_sum = total(scatter(whole_low, grad_pre_one))
    grad_inner_bias = column_sum(grad_pre_one)
    grad_whole = by_unit(cotangent.astype(F32)) + by_unit(right_product(grad_pre_one, inner_full))
    grad_gate_two = grad_whole * branch_two
    grad_branch_two = by_row((grad_whole * gate_two).astype(BF))
    shrink_sum = total(scatter(activated, grad_branch_two))
    grad_shrink_bias = column_sum(grad_branch_two)
    grad_expanded = local_back(gelu_tanh, expanded, right_product(grad_branch_two, shrink_full)).astype(BF)
    expand_sum = total(scatter(modulated_two, grad_expanded))
    grad_expand_bias = column_sum(grad_expanded)
    grad_mod_two = by_unit(right_product(grad_expanded, expand_full))
    grad_scale_two = grad_mod_two * normal_two
    grad_middle = grad_whole + norm_back(grad_mod_two * (1.0 + scale_two), normal_two, inverse_two)
    grad_gate_one = grad_middle * branch_one
    grad_branch_one = by_row((grad_middle * gate_one).astype(BF))
    attended_rows = jnp.transpose(attended, (1, 0, 2)).reshape(count, width)
    output_sum = total(scatter(attended_rows, grad_branch_one))
    grad_output_bias = column_sum(grad_branch_one)
    grad_attended = jnp.einsum("to,pio->pti", grad_branch_one, output_heads, preferred_element_type=F32)
    grad_heads = lax.all_to_all(grad_attended.astype(BF), "blk", split_axis=0, concat_axis=0, tiled=True)
    grad_qkv = attend_backward(
        start, length, qkv, grad_heads.reshape(parts, units, unit, mine), heads, head_dim
    ).reshape(parts * count, 3 * mine)
    attend_part = scatter(modulated_group, grad_qkv)
    attend_parts = lax.all_gather(attend_part, "blk", axis=0, tiled=False)
    attend_sum = jnp.transpose(attend_parts.reshape(parts, -1, 3, mine), (1, 2, 0, 3)).reshape(
        attend_part.shape[0], 3 * width
    )
    partial_mod_one = right_product(grad_qkv, attend_full).astype(BF)
    grad_mod_one = by_unit(
        lax.psum_scatter(partial_mod_one, "blk", scatter_dimension=0, tiled=True).astype(F32)
    )
    grad_scale_one = grad_mod_one * normal_one
    grad_source = grad_middle + norm_back(grad_mod_one * (1.0 + scale_one), normal_one, inverse_one)

    def slot_sum(*values):
        rows = jnp.concatenate([jnp.sum(v, axis=1) for v in values], axis=1)
        return jnp.dot(unit_hot.T, rows, precision=HIGH)

    early_biases = (
        grad_output_bias,
        grad_expand_bias,
        grad_shrink_bias,
        grad_inner_bias,
        grad_middle_bias,
        grad_outer_bias,
    )
    early_sizes = [b.shape[0] // devices for b in early_biases]
    early_bias_rows = jnp.concatenate([b.reshape(devices, -1) for b in early_biases], axis=1)
    early_bias = lax.psum_scatter(early_bias_rows, "img", scatter_dimension=0, tiled=True)
    early_slots = slot_sum(grad_gate_one, grad_mod_two, grad_scale_two, grad_gate_two)
    early_slots, early_bias = lax.psum((early_slots, early_bias), "blk")
    early_grad = lax.all_gather(early_slots, "img", axis=0, tiled=True)
    early_bias = early_bias.reshape(-1)
    (
        output_bias_sum,
        expand_bias_sum,
        shrink_bias_sum,
        inner_bias_sum,
        middle_bias_sum,
        outer_bias_sum,
    ) = (early_bias[sum(early_sizes[:i]) : sum(early_sizes[: i + 1])] for i in range(len(early_sizes)))

    qkv_bias = column_sum(grad_qkv).reshape(3, mine)
    late_slots = slot_sum(grad_mod_one, grad_scale_one)
    late_rows = jnp.concatenate(
        [late_slots, jnp.pad(qkv_bias, ((0, slots - 3), (0, 2 * width - mine)))], axis=0
    )
    late = lax.all_gather(late_rows, ("img", "blk"), axis=0, tiled=False)
    late = late.reshape(devices, parts, 2 * slots, 2 * width)
    late_grad = jnp.sum(late[:, :, :slots], axis=1).reshape(devices * slots, 2 * width)
    bias_all = jnp.sum(late[:, :, slots : slots + 3, :mine], axis=0)
    attend_bias_whole = jnp.concatenate([bias_all[:, 0].reshape(-1), bias_all[:, 2].reshape(-1)])
    attend_bias_sum = lax.dynamic_slice_in_dim(
        attend_bias_whole, place_img * attend_bias.shape[0], attend_bias.shape[0]
    )
    modulation_grad = jnp.concatenate([late_grad, early_grad], axis=1)
    modulate_sum = jnp.dot(silu_condition.astype(F32).T, modulation_grad, precision=HIGH)
    modulate_bias_sum = jnp.sum(modulation_grad, axis=0)
    silu_grad = jnp.dot(modulation_grad, modulate_weight.astype(F32).T, precision=HIGH)
    condition_grad = local_back(jax.nn.silu, condition, silu_grad)
    table_sum = jnp.dot(class_hot.astype(F32).T, condition_grad, precision=HIGH)
    return (
        whole_low,
        by_row(grad_source.astype(BF)),
        table_sum,
        modulate_sum,
        modulate_bias_sum,
        attend_sum.astype(F32),
        attend_bias_sum,
        output_sum.astype(F32),
        output_bias_sum,
        expand_sum.astype(F32),
        expand_bias_sum,
        shrink_sum.astype(F32),
        shrink_bias_sum,
        inner_sum.astype(F32),
        inner_bias_sum,
        middle_sum.astype(F32),
        middle_bias_sum,
        outer_sum.astype(F32),
        outer_bias_sum,
    )


def solution(mesh):
    in_specs = (
        P(("img", "blk"), None),
        P(("img", "blk")),
        P(),
        P(),
        P(("img", "blk"), None),
        P(("img", "blk"), None),
        P(None, "img"),
        P("img", None),
        P(),
        P("img", None),
        P("img"),
        P("img", None),
        P("img"),
        P("img", None),
        P("img"),
        P("img", None),
        P("img"),
        P("img", None),
        P("img"),
        P("img", None),
        P("img"),
        P("img", None),
        P("img"),
    )
    out_specs = (
        P(("img", "blk"), None),
        P(("img", "blk"), None),
        P(None, "img"),
        P("img", None),
        P(),
        P("img", None),
        P("img"),
        P("img", None),
        P("img"),
        P("img", None),
        P("img"),
        P("img", None),
        P("img"),
        P("img", None),
        P("img"),
        P("img", None),
        P("img"),
        P("img", None),
        P("img"),
    )
    return jax.shard_map(
        per_device, mesh=mesh, in_specs=in_specs, out_specs=out_specs, check_vma=False
    )
```

```python
from functools import partial
import math

import jax
import jax.numpy as jnp
from jax import lax
from jax.experimental import pallas as pl
from jax.experimental.pallas import tpu as pltpu
from jax.sharding import PartitionSpec as P

HEADS = 16
SHORT = 256
RATIO = 4
LANES = 128

EPSILON = 1e-06
HIGH = lax.Precision.HIGHEST
BF = jnp.bfloat16
F32 = jnp.float32


def layer_norm(values):
    mean = jnp.mean(values, axis=-1, keepdims=True)
    centered = values - mean
    variance = jnp.mean(centered * centered, axis=-1, keepdims=True)
    inverse = lax.rsqrt(variance + EPSILON)
    return (centered * inverse, inverse)


def norm_back(grad, normal, inverse):
    mean_grad = jnp.mean(grad, axis=-1, keepdims=True)
    mean_cross = jnp.mean(grad * normal, axis=-1, keepdims=True)
    return inverse * (grad - mean_grad - normal * mean_cross)


def local_back(function, point, grad):
    return jax.vjp(function, point)[1](grad)[0]


def left_product(left, right):
    return jnp.einsum("ti,to->io", left, right, preferred_element_type=F32).astype(BF)


def right_product(grad, weight):
    return jnp.einsum("to,io->ti", grad, weight, preferred_element_type=F32)


def column_sum(values):
    return jnp.sum(values.astype(F32), axis=0)


def dot(left, right):
    return jnp.dot(left, right, preferred_element_type=F32)


def dot_general(left, right, contract):
    return lax.dot_general(left, right, ((contract[:1], contract[1:]), ((), ())), preferred_element_type=F32)


def softmax_keys(keys, queries, scale):
    scores = dot_general(keys, queries, (1, 1)) * scale
    raised = jnp.exp(scores - jnp.max(scores, axis=0, keepdims=True))
    return raised * (1.0 / jnp.sum(raised, axis=0, keepdims=True))


def attend_forward_kernel(heads, scale, start_ref, length_ref, qkv_ref, pick_ref, out_ref):
    parts, _, unit, _ = qkv_ref.shape
    u = pl.program_id(0)
    first = start_ref[u]

    def work(span):
        outs = []
        for h in range(heads):

            def head(which, lo, n):
                at = (which * heads + h) * LANES
                return qkv_ref[:, pl.ds(lo, n), :, at : at + LANES].reshape(parts * n * unit, LANES)

            chance = softmax_keys(head(1, first, span), head(0, u, 1), scale).astype(BF)
            outs.append(dot_general(chance, head(2, first, span), (0, 0)).astype(BF))
        packed = dot(jnp.concatenate(outs, axis=1), pick_ref[...]).astype(BF)
        out_ref[...] = packed.reshape(out_ref.shape)

    pl.when(length_ref[u] == 1)(lambda: work(1))
    pl.when(length_ref[u] != 1)(lambda: work(RATIO))


def attend_backward_kernel(
    heads, scale, start_ref, length_ref, qkv_ref, grad_ref, spread_ref, pick_ref, out_ref, dq, dk, dv
):
    parts, units, unit, _ = qkv_ref.shape
    u = pl.program_id(0)
    first = start_ref[u]

    @pl.when(u == 0)
    def _():
        dk[...] = jnp.zeros_like(dk)
        dv[...] = jnp.zeros_like(dv)

    def work(span):
        grads = dot(grad_ref[...].reshape(parts * unit, -1), spread_ref[...]).astype(BF)
        for h in range(heads):

            def head(which, lo, n):
                at = (which * heads + h) * LANES
                return qkv_ref[:, pl.ds(lo, n), :, at : at + LANES].reshape(parts * n * unit, LANES)

            at = slice(h * LANES, (h + 1) * LANES)
            grad = grads[:, at]
            query, key, value = head(0, u, 1), head(1, first, span), head(2, first, span)
            chance = softmax_keys(key, query, scale)
            chance_grad = dot_general(value, grad, (1, 1))
            offset = jnp.sum(chance * chance_grad, axis=0, keepdims=True)
            score_grad = (chance * (chance_grad - offset)).astype(BF)
            into = (parts, span, unit, LANES)
            dv[:, pl.ds(first, span), :, at] += dot(chance.astype(BF), grad).reshape(into)
            dk[:, pl.ds(first, span), :, at] += (dot(score_grad, query) * scale).reshape(into)
            dq[:, pl.ds(u, 1), :, at] = (
                (dot_general(score_grad, key, (0, 0)) * scale).astype(BF).reshape(parts, 1, unit, LANES)
            )

    pl.when(length_ref[u] == 1)(lambda: work(1))
    pl.when(length_ref[u] != 1)(lambda: work(RATIO))

    @pl.when(u == units - 1)
    def _():
        def pack(i, carry):
            rows = [ref[:, pl.ds(i, 1)].astype(BF).reshape(parts * unit, -1) for ref in (dq, dk, dv)]
            packed = dot(jnp.concatenate(rows, axis=1), pick_ref[...]).astype(BF)
            out_ref[:, pl.ds(i, 1)] = packed.reshape(parts, 1, unit, -1)
            return carry

        lax.fori_loop(0, units, pack, 0)


def whole_lanes(width):
    return -(-width // LANES) * LANES


def picker(heads, head_dim, dtype, width=None):
    row = jnp.arange(heads * LANES)[:, None]
    col = jnp.arange(heads * head_dim if width is None else width)[None, :]
    return ((row // LANES == col // head_dim) & (row % LANES == col % head_dim)).astype(dtype)


def attend_forward(start, length, qkv, heads, head_dim):
    parts, units, unit, lanes = qkv.shape
    width = heads * head_dim
    whole = lambda *shape: pl.BlockSpec(shape, lambda u, *_: (0,) * len(shape))
    return pl.pallas_call(
        partial(attend_forward_kernel, heads, 1.0 / math.sqrt(head_dim)),
        grid_spec=pltpu.PrefetchScalarGridSpec(
            num_scalar_prefetch=2,
            grid=(units,),
            in_specs=[whole(parts, units, unit, lanes), whole(heads * LANES, width)],
            out_specs=pl.BlockSpec((parts, 1, unit, width), lambda u, *_: (0, u, 0, 0)),
        ),
        out_shape=jax.ShapeDtypeStruct((parts, units, unit, width), BF),
        compiler_params=pltpu.CompilerParams(vmem_limit_bytes=48 * 2**20),
        cost_estimate=pl.CostEstimate(flops=10 * 2**30, bytes_accessed=16 * 2**20, transcendentals=2**23),
        name="attend_forward",
    )(start, length, qkv, picker(heads, head_dim, BF))


def attend_backward(start, length, qkv, grad, heads, head_dim):
    parts, units, unit, lanes = qkv.shape
    width = heads * head_dim
    whole = lambda *shape: pl.BlockSpec(shape, lambda u, *_: (0,) * len(shape))
    pick = picker(heads, head_dim, BF)
    return pl.pallas_call(
        partial(attend_backward_kernel, heads, 1.0 / math.sqrt(head_dim)),
        grid_spec=pltpu.PrefetchScalarGridSpec(
            num_scalar_prefetch=2,
            grid=(units,),
            in_specs=[
                whole(parts, units, unit, lanes),
                pl.BlockSpec((parts, 1, unit, width), lambda u, *_: (0, u, 0, 0)),
                whole(width, heads * LANES),
                whole(3 * heads * LANES, whole_lanes(3 * width)),
            ],
            out_specs=whole(parts, units, unit, whole_lanes(3 * width)),
            scratch_shapes=[
                pltpu.VMEM((parts, units, unit, heads * LANES), BF),
                pltpu.VMEM((parts, units, unit, heads * LANES), F32),
                pltpu.VMEM((parts, units, unit, heads * LANES), F32),
            ],
        ),
        out_shape=jax.ShapeDtypeStruct((parts, units, unit, whole_lanes(3 * width)), BF),
        compiler_params=pltpu.CompilerParams(vmem_limit_bytes=56 * 2**20),
        cost_estimate=pl.CostEstimate(flops=40 * 2**30, bytes_accessed=16 * 2**20, transcendentals=2**23),
        name="attend_backward",
    )(start, length, qkv, grad, pick.T, picker(3 * heads, head_dim, BF, whole_lanes(3 * width)))


MESH = pl.DeviceIdType.MESH


def add_into(ref, at, other):
    ref[at] = (ref[at].astype(F32) + other.astype(F32)).astype(BF)


def cut_rows(rows, k):
    up = (rows // 2 + 15) // 16 * 16
    return up if k % 2 == 0 else rows - up


def reduce_kernel(chunks, tensors, *refs):
    grads, outs, scratch = refs[:tensors], refs[tensors : 2 * tensors], list(refs[2 * tensors :])
    own, local_sem, send_sem, recv_sem = scratch[:4]
    bufs = scratch[4:]
    per = 8
    place, z = lax.axis_index("img"), lax.axis_index("blk")
    y, x, c = lax.div(place, 4), lax.rem(lax.div(place, 2), 2), lax.rem(place, 2)
    pair, beside, across = place + 1 - 2 * c, place + 2 - 4 * x, place + 4 - 8 * y
    near, far = z + 1 - 2 * lax.rem(z, 2), 3 - z
    inside = (z == 1) | (z == 2)
    outside = (z == 0) | (z == 3)

    barrier = pltpu.get_barrier_semaphore()
    for other in (pair, beside, across):
        pl.semaphore_signal(barrier, inc=1, device_id={"img": other}, device_id_type=MESH)
    for step in (1, 2, 3):
        pl.semaphore_signal(barrier, inc=1, device_id={"blk": lax.rem(z + step, 4)}, device_id_type=MESH)
    pl.semaphore_wait(barrier, 6)

    def send(k, which, source, target, where):
        return pltpu.make_async_remote_copy(
            src_ref=source,
            dst_ref=target,
            send_sem=send_sem.at[k, which],
            recv_sem=recv_sem.at[k, which],
            device_id=where,
            device_id_type=MESH,
        )

    def parts_of(k):
        t, row, rows, col, cols, gather = chunks[k]
        return grads[t], outs[t], row, rows, col, cols, gather

    def cut(k):
        return cut_rows(chunks[k][2], k)

    copies = {}

    def begin(k, which, source, target, where):
        copies[k, which] = send(k, which, source, target, where)
        copies[k, which].start()

    def load(k):
        grad, _, row, rows, col, cols, _ = parts_of(k)
        return pltpu.make_async_copy(
            grad.at[:, :, c, pl.ds(row, rows), pl.ds(col, cols)],
            own.at[k % 2, :, :, pl.ds(0, rows), pl.ds(0, cols)],
            local_sem.at[k % 2],
        )

    count = len(chunks)
    for k in range(count):
        grad, _, row, rows, col, cols, _ = parts_of(k)
        begin(k, 0, grad.at[:, :, 1 - c, pl.ds(row, rows), pl.ds(col, cols)], bufs[per * k], {"img": pair})
    for k in range(min(2, count)):
        load(k).start()

    def stage_one(k):
        _, _, _, rows, _, cols, _ = parts_of(k)
        acc, rx, ry = bufs[per * k : per * k + 3]
        load(k).wait()
        copies[k, 0].wait_recv()
        for i in range(2):
            for j in range(2):
                add_into(acc, (i, j), own[k % 2, i, j, :rows, :cols])
        if k + 2 < count:
            load(k + 2).start()
        first = cut(k)
        begin(k, 1, acc.at[:, 1 - x, pl.ds(0, first)], rx, {"img": beside})
        begin(k, 2, acc.at[1 - y, :, pl.ds(first, rows - first)], ry, {"img": across})

    def stage_two(k):
        rows = chunks[k][2]
        acc, rx, ry, rx2, ry2 = bufs[per * k : per * k + 5]
        first = cut(k)
        copies[k, 1].wait_recv()
        copies[k, 2].wait_recv()
        copies[k, 1].wait_send()
        copies[k, 2].wait_send()
        for i in range(2):
            add_into(acc, (i, x, slice(0, first)), rx[i])
            add_into(acc, (y, i, slice(first, rows)), ry[i])
        begin(k, 3, acc.at[y, 1 - x, pl.ds(first, rows - first)], rx2, {"img": beside})
        begin(k, 4, acc.at[1 - y, x, pl.ds(0, first)], ry2, {"img": across})

    def stage_three(k):
        _, out, row, rows, col, cols, gather = parts_of(k)
        acc, _, _, rx2, ry2, from_near, from_far, total = bufs[per * k : per * (k + 1)]
        first = cut(k)
        copies[k, 3].wait_recv()
        copies[k, 4].wait_recv()
        low = (acc[y, x, 0:first].astype(F32) + ry2[...].astype(F32)).astype(BF)
        high = (acc[y, x, first:rows].astype(F32) + rx2[...].astype(F32)).astype(BF)
        if gather:
            total[z, 0:first] = low
            total[z, first:rows] = high
            for step in (1, 2, 3):
                begin(k, 4 + step, total.at[z], total.at[z], {"blk": lax.rem(z + step, 4)})
            return
        from_far[0, 0:first] = low
        from_far[0, first:rows] = high
        copies[k, 5] = send(k, 5, from_far.at[0], from_near, {"blk": near})
        pl.when(outside)(copies[k, 5].start)

    def stage_four(k):
        if chunks[k][5]:
            return
        from_near, from_far, total = bufs[per * k + 5 : per * k + 8]
        copies[k, 6] = send(k, 6, from_far.at[0], from_far.at[1], {"blk": far})

        @pl.when(inside)
        def _():
            copies[k, 5].wait_recv()
            add_into(from_far, 0, from_near[...])
            copies[k, 6].start()

    def stage_five(k):
        if chunks[k][5]:
            return
        from_near, from_far, total = bufs[per * k + 5 : per * k + 8]
        copies[k, 7] = send(k, 7, total, total, {"blk": near})

        @pl.when(inside)
        def _():
            copies[k, 6].wait_recv()
            total[...] = (from_far[0].astype(F32) + from_far[1].astype(F32)).astype(BF)
            copies[k, 7].start()

    def stage_six(k):
        _, out, row, rows, col, cols, gather = parts_of(k)
        total = bufs[per * k + 7]
        if gather:
            for step in (1, 2, 3):
                copies[k, 4 + step].wait()
            out[:, row : row + rows, col : col + cols] = total[...]
            return
        pl.when(outside)(copies[k, 7].wait_recv)
        out[row : row + rows, col : col + cols] = total[...]

    stages = ((stage_one, 0), (stage_two, 2), (stage_three, 4), (stage_four, 5), (stage_five, 6), (stage_six, 7))
    for step in range(count + 7):
        for stage, behind in stages:
            if 0 <= step - behind < count:
                stage(step - behind)
    for k in range(count):
        copies[k, 0].wait_send()
        copies[k, 3].wait_send()
        copies[k, 4].wait_send()
        if not chunks[k][5]:
            pl.when(outside)(copies[k, 5].wait_send)
            pl.when(inside)(copies[k, 6].wait_send)
            pl.when(inside)(copies[k, 7].wait_send)


def reduce_call(grads, gathered, depth, width, collective_id):
    chunks, shapes = [], []
    for t, grad in enumerate(grads):
        rows, cols = grad.shape[0] // 8, grad.shape[1]
        for row in range(0, rows, depth):
            for col in range(0, cols, width):
                chunks.append((t, row, min(depth, rows - row), col, min(width, cols - col), gathered[t]))
        shapes.append(jax.ShapeDtypeStruct((4, rows, cols) if gathered[t] else (rows, cols), BF))
    scratch = [
        pltpu.VMEM((2, 2, 2, depth, width), BF),
        pltpu.SemaphoreType.DMA((2,)),
        pltpu.SemaphoreType.DMA((len(chunks), 8)),
        pltpu.SemaphoreType.DMA((len(chunks), 8)),
    ]
    for k, (_, _, rows, _, cols, gather) in enumerate(chunks):
        first = cut_rows(rows, k)
        for shape in (
            (2, 2, rows, cols),
            (2, first, cols),
            (2, rows - first, cols),
            (rows - first, cols),
            (first, cols),
            (16, cols) if gather else (rows, cols),
            (1, 16, cols) if gather else (2, rows, cols),
            (4, rows, cols) if gather else (rows, cols),
        ):
            scratch.append(pltpu.VMEM(shape, BF))
    return pl.pallas_call(
        partial(reduce_kernel, chunks, len(grads)),
        out_shape=shapes,
        in_specs=[pl.BlockSpec(memory_space=pl.ANY)] * len(grads),
        out_specs=[pl.BlockSpec(memory_space=pltpu.VMEM)] * len(grads),
        scratch_shapes=scratch,
        compiler_params=pltpu.CompilerParams(
            collective_id=collective_id, has_side_effects=True, vmem_limit_bytes=56 * 2**20
        ),
        cost_estimate=pl.CostEstimate(flops=0, bytes_accessed=500 * 2**20, transcendentals=0),
        name=f"reduce_{collective_id}",
    )(*(g.reshape(2, 2, 2, g.shape[0] // 8, g.shape[1]) for g in grads))


def gather_kernel(chunks, tensors, early, hot_ref, x_ref, share_ref, bias_ref, start_ref, *refs):
    shards, refs = refs[:tensors], refs[tensors:]
    fulls, refs = refs[:tensors], refs[tensors:]
    rows_ref, modulation_ref, bias_out = refs[:3]
    share_got, own_sem, first_send, first_recv, rest_send, rest_recv, bias_send, bias_recv = refs[3:11]
    send_sem, recv_sem, line_send, line_recv, spread_send, spread_recv = refs[11:]
    place, z = lax.axis_index("img"), lax.axis_index("blk")
    y, x, c = lax.div(place, 4), lax.rem(lax.div(place, 2), 2), lax.rem(place, 2)
    step_x, step_y = 2 - 4 * x, 4 - 8 * y
    pair, beside, across = place + 1 - 2 * c, place + step_x, place + step_y
    diagonal = place + step_x + step_y
    devices = share_got.shape[0]
    units, slots = hot_ref.shape
    unit = x_ref.shape[0] // units
    wide = x_ref.shape[1]

    barrier = pltpu.get_barrier_semaphore()
    for step in range(1, devices):
        pl.semaphore_signal(barrier, inc=1, device_id={"img": lax.rem(place + step, devices)}, device_id_type=MESH)
    for step in (1, 2, 3):
        pl.semaphore_signal(barrier, inc=1, device_id={"blk": lax.rem(z + step, 4)}, device_id_type=MESH)
    pl.semaphore_wait(barrier, devices + 2)

    def remote(source, target, send, recv, where):
        return pltpu.make_async_remote_copy(
            src_ref=source,
            dst_ref=target,
            send_sem=send,
            recv_sem=recv,
            device_id=where,
            device_id_type=MESH,
        )

    part = (share_ref.shape[2] - early) // 4
    part_at = pl.multiple_of(early + z * part, LANES)
    first, rest, biases = [], [], []
    for step in range(1, devices):
        to = lax.rem(place + step, devices)
        for copies, lo, size, send, recv in (
            (first, 0, early, first_send, first_recv),
            (rest, part_at, part, rest_send, rest_recv),
        ):
            copies.append(
                remote(
                    share_ref.at[to, :, pl.ds(lo, size)],
                    share_got.at[place, :, pl.ds(lo, size)],
                    send.at[step],
                    recv.at[step],
                    {"img": to},
                )
            )
        biases.append(remote(bias_ref, bias_out.at[place], bias_send.at[step], bias_recv.at[step], {"img": to}))
    for copy in first:
        copy.start()

    copies = {}

    def begin(k, which, block, rows, where):
        t, row, count = chunks[k]
        at = (block, pl.ds(row + rows[0], rows[1]))
        copies[k, which] = remote(
            fulls[t].at[at], fulls[t].at[at], send_sem.at[k, which], recv_sem.at[k, which], where
        )
        copies[k, which].start()

    def begin_own(k, which, where):
        t, row, count = chunks[k]
        source = shards[t].at[pl.ds(row, count)]
        copies[k, which] = remote(
            source, fulls[t].at[place, pl.ds(row, count)], send_sem.at[k, which], recv_sem.at[k, which], where
        )
        copies[k, which].start()

    own = [pltpu.make_async_copy(shards[t], fulls[t].at[place], own_sem.at[t]) for t in range(tensors)]
    def ahead(k):
        if k < len(chunks):
            begin_own(k, 0, {"img": beside})
            begin_own(k, 1, {"img": across})
            begin_own(k, 2, {"img": pair})

    ahead(0)
    for copy in rest + biases:
        copy.start()
    for k in range(1, 3):
        ahead(k)
    for copy in own:
        copy.start()

    share_got[place] = share_ref[place]
    bias_out[place] = bias_ref[...]
    for copy in first:
        copy.wait()

    def modulation_of(lo, size):
        at = pl.ds(lo, size)
        total = share_got[0, :, at]
        for i in range(1, devices):
            total = total + share_got[i, :, at]
        modulation_ref[:, at] = start_ref[:, at] + total

    modulation_of(0, early)
    for u in range(units):
        chosen = hot_ref[u : u + 1, 0:1] * modulation_ref[0:1, 0:early]
        for s in range(1, slots):
            chosen = chosen + hot_ref[u : u + 1, s : s + 1] * modulation_ref[s : s + 1, 0:early]
        at = pl.ds(u * unit, unit)
        values = x_ref[at, :].astype(F32)
        centered = values - jnp.mean(values, axis=1, keepdims=True)
        inverse = lax.rsqrt(jnp.mean(centered * centered, axis=1, keepdims=True) + EPSILON)
        rows_ref[z, at, :] = (centered * inverse * (1.0 + chosen[:, wide:]) + chosen[:, :wide]).astype(BF)

    up = [
        remote(block, block, line_send.at[0, s], line_recv.at[0, s], {"blk": lax.rem(z + 1, 4)})
        for s, block in ((s, rows_ref.at[lax.rem(z - s + 4, 4)]) for s in range(3))
    ]
    down = [
        remote(block, block, line_send.at[1, s], line_recv.at[1, s], {"blk": lax.rem(z + 3, 4)})
        for s, block in ((s, rows_ref.at[lax.rem(z + s, 4)]) for s in range(3))
    ]

    def line_step(s):
        if s > 0:
            pl.when(z >= s)(up[s - 1].wait_recv)
            pl.when(z + s < 4)(down[s - 1].wait_recv)
        if s < 3:
            pl.when((z >= s) & (z < 3))(up[s].start)
            pl.when((z + s < 4) & (z > 0))(down[s].start)

    def cut(k):
        return cut_rows(chunks[k][2], k)

    def relay(k):
        count, half = chunks[k][2], cut(k)
        copies[k, 0].wait_recv()
        begin(k, 3, beside, (0, half), {"img": across})
        begin(k, 5, beside, (0, count), {"img": pair})
        copies[k, 1].wait_recv()
        begin(k, 4, across, (half, count - half), {"img": beside})
        begin(k, 6, across, (0, count), {"img": pair})

    def last(k):
        count, half = chunks[k][2], cut(k)
        copies[k, 3].wait_recv()
        begin(k, 7, diagonal, (0, half), {"img": pair})
        copies[k, 4].wait_recv()
        begin(k, 8, diagonal, (half, count - half), {"img": pair})

    line_step(0)
    for copy in rest:
        copy.wait()
    modulation_of(part_at, part)
    own_part = modulation_ref.at[:, pl.ds(part_at, part)]
    spread = [
        remote(own_part, own_part, spread_send.at[step], spread_recv.at[step], {"blk": lax.rem(z + step, 4)})
        for step in (1, 2, 3)
    ]
    for copy in spread:
        copy.start()
    n = len(chunks)
    for k in range(n + 2):
        if k < n:
            relay(k)
            ahead(k + 3)
        if k >= 2:
            last(k - 2)
        for s in (1, 2):
            if k == 2 * s - 1:
                line_step(s)
    for copy in biases:
        copy.wait()
    line_step(3)
    for copy in spread:
        copy.wait()
    for copy in own:
        copy.wait()
    for k in range(n):
        for which in (0, 1, 3, 4):
            copies[k, which].wait_send()
        copies[k, 2].wait()
        for which in (5, 6, 7, 8):
            copies[k, which].wait()
    for s in range(3):
        pl.when((z >= s) & (z < 3))(up[s].wait_send)
        pl.when((z + s < 4) & (z > 0))(down[s].wait_send)


def gather_call(shards, unit_hot, rows, shares, bias_row, modulate_bias, collective_id):
    devices = shares.shape[0]
    slots, wide = shares.shape[1:]
    chunks = []
    for t, shard in enumerate(shards):
        depth = shard.shape[0]
        for row in range(0, depth, 144):
            chunks.append((t, row, min(144, depth - row)))
    n = len(chunks)
    vmem, anywhere = pl.BlockSpec(memory_space=pltpu.VMEM), pl.BlockSpec(memory_space=pl.ANY)
    dma = pltpu.SemaphoreType.DMA
    first_modulation = jnp.broadcast_to(modulate_bias.astype(F32)[None, :], (slots, wide))
    return pl.pallas_call(
        partial(gather_kernel, chunks, len(shards), 2 * rows.shape[1]),
        out_shape=[jax.ShapeDtypeStruct((devices, *s.shape), BF) for s in shards]
        + [
            jax.ShapeDtypeStruct((4, *rows.shape), BF),
            jax.ShapeDtypeStruct((slots, wide), F32),
            jax.ShapeDtypeStruct((devices, *bias_row.shape), F32),
        ],
        in_specs=[vmem] * 5 + [anywhere] * len(shards),
        out_specs=[anywhere] * len(shards) + [vmem] * 3,
        scratch_shapes=[
            pltpu.VMEM((devices, slots, wide), F32),
            dma((len(shards),)),
            dma((devices,)),
            dma((devices,)),
            dma((devices,)),
            dma((devices,)),
            dma((devices,)),
            dma((devices,)),
            dma((n, 9)),
            dma((n, 9)),
            dma((2, 3)),
            dma((2, 3)),
            dma((4,)),
            dma((4,)),
        ],
        compiler_params=pltpu.CompilerParams(
            collective_id=collective_id, has_side_effects=True, vmem_limit_bytes=48 * 2**20
        ),
        cost_estimate=pl.CostEstimate(flops=0, bytes_accessed=450 * 2**20, transcendentals=0),
        name=f"gather_{collective_id}",
    )(unit_hot, rows, shares, bias_row, first_modulation, *shards)


def total_kernel(mine_ref, out_ref, lines, line_send, line_recv, send_sem, recv_sem):
    place, z = lax.axis_index("img"), lax.axis_index("blk")
    parts, devices = lines.shape[0], out_ref.shape[0]
    barrier = pltpu.get_barrier_semaphore()
    for step in range(1, parts):
        pl.semaphore_signal(barrier, inc=1, device_id={"blk": lax.rem(z + step, parts)}, device_id_type=MESH)
    for step in range(1, devices):
        pl.semaphore_signal(barrier, inc=1, device_id={"img": lax.rem(place + step, devices)}, device_id_type=MESH)
    pl.semaphore_wait(barrier, parts + devices - 2)

    lines[z] = mine_ref[...]
    copies = [
        pltpu.make_async_remote_copy(
            src_ref=lines.at[z],
            dst_ref=lines.at[z],
            send_sem=line_send.at[step],
            recv_sem=line_recv.at[step],
            device_id={"blk": lax.rem(z + step, parts)},
            device_id_type=MESH,
        )
        for step in range(1, parts)
    ]
    for copy in copies:
        copy.start()
    for copy in copies:
        copy.wait()
    total = lines[0]
    for step in range(1, parts):
        total = total + lines[step]
    out_ref[place] = total
    copies = [
        pltpu.make_async_remote_copy(
            src_ref=out_ref.at[place],
            dst_ref=out_ref.at[place],
            send_sem=send_sem.at[step],
            recv_sem=recv_sem.at[step],
            device_id={"img": lax.rem(place + step, devices)},
            device_id_type=MESH,
        )
        for step in range(1, devices)
    ]
    for copy in copies:
        copy.start()
    for copy in copies:
        copy.wait()


def total_call(mine, devices, parts, collective_id):
    if (devices, parts) != (8, 4):
        return lax.all_gather(lax.psum(mine, "blk"), "img", axis=0, tiled=False)
    return pl.pallas_call(
        total_kernel,
        out_shape=jax.ShapeDtypeStruct((devices, *mine.shape), mine.dtype),
        in_specs=[pl.BlockSpec(memory_space=pltpu.VMEM)],
        out_specs=pl.BlockSpec(memory_space=pltpu.VMEM),
        scratch_shapes=[
            pltpu.VMEM((parts, *mine.shape), mine.dtype),
            pltpu.SemaphoreType.DMA((parts,)),
            pltpu.SemaphoreType.DMA((parts,)),
            pltpu.SemaphoreType.DMA((devices,)),
            pltpu.SemaphoreType.DMA((devices,)),
        ],
        compiler_params=pltpu.CompilerParams(
            collective_id=collective_id, has_side_effects=True, vmem_limit_bytes=32 * 2**20
        ),
        name=f"total_{collective_id}",
    )(mine)


def per_device(
    inputs,
    token_image,
    image_time,
    image_class,
    targets,
    cotangent,
    class_table,
    modulate_weight,
    modulate_bias,
    attend_weight,
    attend_bias,
    output_weight,
    output_bias,
    expand_weight,
    expand_bias,
    shrink_weight,
    shrink_bias,
    inner_weight,
    inner_bias,
    middle_weight,
    middle_bias,
    outer_weight,
    outer_bias,
):
    count, width = inputs.shape
    head_dim = width // HEADS
    columns = class_table.shape[1]
    devices, parts = lax.axis_size("img"), lax.axis_size("blk")
    place_img, place_blk = lax.axis_index("img"), lax.axis_index("blk")
    slots = image_class.shape[0] // devices
    unit = SHORT // parts
    units = count // unit
    heads = HEADS // parts
    mine = heads * head_dim
    half = width // 2

    class_hot = (image_class[:, None] == jnp.arange(class_table.shape[0])[None, :]).astype(BF)
    column = place_img * columns + jnp.arange(columns)
    frequency = jnp.exp(-math.log(10000.0) * (column % half).astype(F32) / half)
    angle = image_time.astype(F32)[:, None] * frequency[None, :]
    condition = dot(class_hot, class_table) + jnp.where(column[None, :] < half, jnp.cos(angle), jnp.sin(angle))
    silu_condition = jax.nn.silu(condition).astype(BF)
    shares = dot(silu_condition, modulate_weight)
    biases = (attend_bias, output_bias, expand_bias, shrink_bias, inner_bias, middle_bias, outer_bias)
    bias_row = jnp.concatenate(biases).astype(F32)
    bias_row = jnp.pad(bias_row, (0, whole_lanes(bias_row.shape[0]) - bias_row.shape[0]))[None, :]
    shares = shares.reshape(devices, slots, -1)

    labels = token_image[::unit]
    same = labels[:, None] == labels[None, :]
    start = jnp.argmax(same, axis=1).astype(jnp.int32)
    length = jnp.sum(same, axis=1).astype(jnp.int32)
    unit_hot = (labels[:, None] == jnp.arange(slots)[None, :]).astype(F32)
    def by_unit(values):
        return values.reshape(units, unit, width)

    def by_row(values):
        return values.reshape(count, width)

    attend_mine = lax.dynamic_slice_in_dim(
        attend_weight.reshape(-1, 3, parts, mine), place_blk, 1, axis=2
    ).reshape(-1, 3 * mine)
    attend_mine = jnp.pad(attend_mine, ((0, 0), (0, whole_lanes(3 * mine) - 3 * mine)))

    def gather(shard):
        return lax.all_gather(shard, "img", axis=0, tiled=True)

    source = by_unit(inputs.astype(F32))
    normal_one, inverse_one = layer_norm(source)
    first_weights = (attend_mine, output_weight, expand_weight, outer_weight, shrink_weight)
    if (devices, parts) == (8, 4):
        *fulls, rows_group, modulation, got_bias = gather_call(
            first_weights, unit_hot, inputs, shares, bias_row, modulate_bias, 3
        )
        fulls = [full.reshape(-1, full.shape[2]) for full in fulls]
        modulated_group = rows_group.reshape(parts * count, width)
    else:
        fulls = [gather(shard) for shard in first_weights]
        modulation = modulate_bias.astype(F32)[None, :] + lax.psum_scatter(
            shares.reshape(devices * slots, -1), "img", scatter_dimension=0, tiled=True
        )
        got_bias = lax.all_gather(bias_row, "img", axis=0, tiled=False)
        chosen = jnp.dot(unit_hot, modulation, precision=HIGH)[:, None, : 2 * width]
        modulated_one = normal_one * (1.0 + chosen[:, :, width:]) + chosen[:, :, :width]
        modulated_group = lax.all_gather(by_row(modulated_one.astype(BF)), "blk", axis=0, tiled=True)
    attend_full, output_full, expand_full, outer_full, shrink_full = fulls
    inner_shard, middle_shard, modulated_group = lax.optimization_barrier(
        (inner_weight, middle_weight, modulated_group)
    )
    inner_full, middle_full = gather(inner_shard), gather(middle_shard)
    full_biases = []
    at = 0
    for bias in biases:
        full_biases.append(got_bias[:, 0, at : at + bias.shape[0]].reshape(-1))
        at += bias.shape[0]
    (
        attend_bias_full,
        output_bias_full,
        expand_bias_full,
        shrink_bias_full,
        inner_bias_full,
        middle_bias_full,
        outer_bias_full,
    ) = full_biases
    unit_modulation = jnp.dot(unit_hot, modulation, precision=HIGH)
    shift_one, scale_one, gate_one, shift_two, scale_two, gate_two = (
        block[:, None, :] for block in jnp.split(unit_modulation, 6, axis=1)
    )

    def pad_heads(values):
        lead = values.shape[:-1]
        values = values.reshape(*lead, 3 * heads, head_dim)
        values = jnp.pad(values, ((0, 0),) * len(lead) + ((0, 0), (0, LANES - head_dim)))
        return values.reshape(*lead, 3 * heads * LANES)

    bias_mine = lax.dynamic_slice_in_dim(attend_bias_full.reshape(2, parts, mine), place_blk, 1, axis=1)
    bias_mine = jnp.concatenate([bias_mine[0, 0], jnp.zeros((mine,), F32), bias_mine[1, 0]])
    projected = dot(modulated_group, pad_heads(attend_full[:, : 3 * mine])) + pad_heads(bias_mine)[None, :]
    qkv = projected.astype(BF).reshape(parts, units, unit, 3 * heads * LANES)
    attended_heads = attend_forward(start, length, qkv, heads, head_dim)
    attended = lax.all_to_all(
        attended_heads.reshape(parts, count, mine), "blk", split_axis=0, concat_axis=0, tiled=True
    )
    output_heads = output_full.reshape(parts, mine, width)
    branch_one = by_unit(
        jnp.einsum("pti,pio->to", attended, output_heads, preferred_element_type=F32) + output_bias_full
    )
    middle = source + gate_one * branch_one
    normal_two, inverse_two = layer_norm(middle)
    modulated_two = by_row((normal_two * (1.0 + scale_two) + shift_two).astype(BF))
    expanded = dot(modulated_two, expand_full) + expand_bias_full
    gelu_tanh = partial(jax.nn.gelu, approximate=True)
    activated = gelu_tanh(expanded).astype(BF)
    branch_two = by_unit(dot(activated, shrink_full) + shrink_bias_full)
    whole = middle + gate_two * branch_two
    whole_low = by_row(whole.astype(BF))
    pre_one = dot(whole_low, inner_full) + inner_bias_full
    first = jax.nn.silu(pre_one).astype(BF)
    pre_two = dot(first, middle_full) + middle_bias_full
    second = jax.nn.silu(pre_two).astype(BF)
    aligned = dot(second, outer_full) + outer_bias_full
    target = targets.astype(F32)
    cross = jnp.sum(aligned * target, axis=1)
    aligned_inverse = lax.rsqrt(jnp.sum(aligned * aligned, axis=1) + EPSILON)
    target_inverse = lax.rsqrt(jnp.sum(target * target, axis=1) + EPSILON)
    cosine = cross * aligned_inverse * target_inverse
    grad_aligned = (
        -0.5
        * (
            target * (aligned_inverse * target_inverse)[:, None]
            - (cosine * aligned_inverse * aligned_inverse)[:, None] * aligned
        )
    ).astype(BF)

    def scatter(values):
        return lax.psum_scatter(values, "img", scatter_dimension=0, tiled=True)

    outer_part = scatter(left_product(second, grad_aligned))
    grad_outer_bias = column_sum(grad_aligned)
    grad_pre_two = local_back(jax.nn.silu, pre_two, right_product(grad_aligned, outer_full)).astype(BF)
    middle_part = scatter(left_product(first, grad_pre_two))
    grad_middle_bias = column_sum(grad_pre_two)
    grad_pre_one = local_back(jax.nn.silu, pre_one, right_product(grad_pre_two, middle_full)).astype(BF)
    grad_inner = left_product(whole_low, grad_pre_one)
    grad_inner_bias = column_sum(grad_pre_one)
    grad_whole = by_unit(cotangent.astype(F32)) + by_unit(right_product(grad_pre_one, inner_full))
    grad_gate_two = grad_whole * branch_two
    grad_branch_two = by_row((grad_whole * gate_two).astype(BF))
    grad_shrink = left_product(activated, grad_branch_two)
    grad_shrink_bias = column_sum(grad_branch_two)
    grad_expanded = local_back(gelu_tanh, expanded, right_product(grad_branch_two, shrink_full)).astype(BF)
    grad_expand = left_product(modulated_two, grad_expanded)
    grad_expand_bias = column_sum(grad_expanded)
    grad_mod_two = by_unit(right_product(grad_expanded, expand_full))
    grad_scale_two = grad_mod_two * normal_two
    grad_middle = grad_whole + norm_back(grad_mod_two * (1.0 + scale_two), normal_two, inverse_two)
    grad_gate_one = grad_middle * branch_one
    grad_branch_one = by_row((grad_middle * gate_one).astype(BF))
    grad_output = jnp.einsum("pti,to->pio", attended, grad_branch_one, preferred_element_type=F32)
    grad_output = grad_output.astype(BF).reshape(width, width)
    grad_output_bias = column_sum(grad_branch_one)
    def slot_sum(*values):
        rows = jnp.concatenate([jnp.sum(v, axis=1) for v in values], axis=1)
        return jnp.dot(unit_hot.T, rows, precision=HIGH)

    early_slots = lax.psum(slot_sum(grad_gate_one, grad_mod_two, grad_scale_two, grad_gate_two), "blk")
    grad_attended = jnp.einsum("to,pio->pti", grad_branch_one, output_heads, preferred_element_type=F32)
    grad_heads = lax.all_to_all(grad_attended.astype(BF), "blk", split_axis=0, concat_axis=0, tiled=True)
    grad_heads, outer_part, early_slots = lax.optimization_barrier((grad_heads, outer_part, early_slots))
    early_grad = lax.all_gather(early_slots, "img", axis=0, tiled=True)
    grad_qkv = attend_backward(
        start, length, qkv, grad_heads.reshape(parts, units, unit, mine), heads, head_dim
    ).reshape(parts * count, -1)
    grad_qkv, middle_part, early_grad = lax.optimization_barrier((grad_qkv, middle_part, early_grad))
    outer_sum, middle_sum = lax.psum((outer_part, middle_part), "blk")
    grad_attend = left_product(modulated_group, grad_qkv)
    partial_mod_one = right_product(grad_qkv, attend_full).astype(BF)
    late_grads = (grad_inner, grad_shrink, grad_attend, grad_output, grad_expand)
    if (devices, parts) == (8, 4):
        inner_sum, shrink_sum, attend_parts, output_sum, expand_sum = reduce_call(
            late_grads, (False, False, True, False, False), width // devices, 640, 1
        )
    else:
        inner_sum, shrink_sum, attend_part, output_sum, expand_sum = (scatter(g) for g in late_grads)
        sums = lax.psum((inner_sum, shrink_sum, output_sum, expand_sum), "blk")
        inner_sum, shrink_sum, output_sum, expand_sum = sums
        attend_parts = lax.all_gather(attend_part, "blk", axis=0, tiled=False)
    attend_parts = attend_parts[:, :, : 3 * mine].reshape(parts, -1, 3, mine)
    attend_sum = jnp.transpose(attend_parts, (1, 2, 0, 3)).reshape(-1, 3 * width)
    grad_mod_one = by_unit(
        lax.psum_scatter(partial_mod_one, "blk", scatter_dimension=0, tiled=True).astype(F32)
    )
    grad_scale_one = grad_mod_one * normal_one
    grad_source = grad_middle + norm_back(grad_mod_one * (1.0 + scale_one), normal_one, inverse_one)

    qkv_bias = column_sum(grad_qkv[:, : 3 * mine]).reshape(3, 1, mine)
    spread = (jnp.arange(parts) == place_blk).astype(F32)[None, :, None]
    attend_bias_rows = jnp.concatenate([qkv_bias[:1], qkv_bias[2:]]) * spread
    bias_grads = (
        attend_bias_rows,
        grad_output_bias,
        grad_expand_bias,
        grad_shrink_bias,
        grad_inner_bias,
        grad_middle_bias,
        grad_outer_bias,
    )
    bias_rows = jnp.concatenate([b.reshape(devices, -1) for b in bias_grads], axis=1)
    late_slots = slot_sum(grad_mod_one, grad_scale_one)
    late_rows = jnp.concatenate(
        [late_slots, jnp.pad(bias_rows, ((0, 0), (0, late_slots.shape[1] - bias_rows.shape[1])))], axis=0
    )
    late = total_call(late_rows, devices, parts, 2)
    late_grad = late[:, :slots].reshape(devices * slots, 2 * width)
    bias_sum = jnp.sum(lax.dynamic_index_in_dim(late, slots + place_img, axis=1, keepdims=False), axis=0)
    bias_sums = []
    at = 0
    for bias in biases:
        bias_sums.append(bias_sum[at : at + bias.shape[0]])
        at += bias.shape[0]
    (
        attend_bias_sum,
        output_bias_sum,
        expand_bias_sum,
        shrink_bias_sum,
        inner_bias_sum,
        middle_bias_sum,
        outer_bias_sum,
    ) = bias_sums
    modulation_grad = jnp.concatenate([late_grad, early_grad], axis=1)
    modulate_sum = jnp.dot(silu_condition.astype(F32).T, modulation_grad, precision=HIGH)
    modulate_bias_sum = jnp.sum(modulation_grad, axis=0)
    silu_grad = jnp.dot(modulation_grad, modulate_weight.astype(F32).T, precision=HIGH)
    condition_grad = local_back(jax.nn.silu, condition, silu_grad)
    table_sum = jnp.dot(class_hot.astype(F32).T, condition_grad, precision=HIGH)
    return (
        whole_low,
        by_row(grad_source.astype(BF)),
        table_sum,
        modulate_sum,
        modulate_bias_sum,
        attend_sum.astype(F32),
        attend_bias_sum,
        output_sum.astype(F32),
        output_bias_sum,
        expand_sum.astype(F32),
        expand_bias_sum,
        shrink_sum.astype(F32),
        shrink_bias_sum,
        inner_sum.astype(F32),
        inner_bias_sum,
        middle_sum.astype(F32),
        middle_bias_sum,
        outer_sum.astype(F32),
        outer_bias_sum,
    )


def solution(mesh):
    in_specs = (
        P(("img", "blk"), None),
        P(("img", "blk")),
        P(),
        P(),
        P(("img", "blk"), None),
        P(("img", "blk"), None),
        P(None, "img"),
        P("img", None),
        P(),
        P("img", None),
        P("img"),
        P("img", None),
        P("img"),
        P("img", None),
        P("img"),
        P("img", None),
        P("img"),
        P("img", None),
        P("img"),
        P("img", None),
        P("img"),
        P("img", None),
        P("img"),
    )
    out_specs = (
        P(("img", "blk"), None),
        P(("img", "blk"), None),
        P(None, "img"),
        P("img", None),
        P(),
        P("img", None),
        P("img"),
        P("img", None),
        P("img"),
        P("img", None),
        P("img"),
        P("img", None),
        P("img"),
        P("img", None),
        P("img"),
        P("img", None),
        P("img"),
        P("img", None),
        P("img"),
    )
    return jax.shard_map(
        per_device, mesh=mesh, in_specs=in_specs, out_specs=out_specs, check_vma=False
    )
```

```python
from functools import partial
import math

import jax
import jax.numpy as jnp
from jax import lax
from jax.experimental import pallas as pl
from jax.experimental.pallas import tpu as pltpu
from jax.sharding import PartitionSpec as P

HEADS = 16
SHORT = 256
RATIO = 4
LANES = 128

EPSILON = 1e-06
HIGH = lax.Precision.HIGHEST
BF = jnp.bfloat16
F32 = jnp.float32


def layer_norm(values):
    mean = jnp.mean(values, axis=-1, keepdims=True)
    centered = values - mean
    variance = jnp.mean(centered * centered, axis=-1, keepdims=True)
    inverse = lax.rsqrt(variance + EPSILON)
    return (centered * inverse, inverse)


def norm_back(grad, normal, inverse):
    mean_grad = jnp.mean(grad, axis=-1, keepdims=True)
    mean_cross = jnp.mean(grad * normal, axis=-1, keepdims=True)
    return inverse * (grad - mean_grad - normal * mean_cross)


def local_back(function, point, grad):
    return jax.vjp(function, point)[1](grad)[0]


def left_product(left, right):
    return jnp.einsum("ti,to->io", left, right, preferred_element_type=F32).astype(BF)


def right_product(grad, weight):
    return jnp.einsum("to,io->ti", grad, weight, preferred_element_type=F32)


def column_sum(values):
    return jnp.sum(values.astype(F32), axis=0)


def dot(left, right):
    return jnp.dot(left, right, preferred_element_type=F32)


def dot_general(left, right, contract):
    return lax.dot_general(left, right, ((contract[:1], contract[1:]), ((), ())), preferred_element_type=F32)


def softmax_base(scale):
    return scale * math.log2(math.e)


def attend_forward_kernel(heads, scale, start_ref, length_ref, qkv_ref, pick_ref, out_ref, norm_ref):
    parts, _, unit, _ = qkv_ref.shape
    base = softmax_base(scale)
    u = pl.program_id(0)
    first = start_ref[u]

    def head(which, h, at):
        lane = (which * heads + h) * LANES
        return qkv_ref[:, pl.ds(at, 1), :, lane : lane + LANES].reshape(parts * unit, LANES)

    def work(span):
        outs = []
        lane = lax.broadcasted_iota(jnp.int32, (parts * unit, LANES), 1)
        norms = jnp.zeros((parts * unit, LANES), F32)
        for h in range(heads):
            query = head(0, h, u)
            scores = [dot_general(query, head(1, h, first + j), (1, 1)) for j in range(span)]
            top = scores[0]
            for block in scores[1:]:
                top = jnp.maximum(top, block)
            top = jnp.max(top, axis=1, keepdims=True) * base
            attended = 0.0
            for j in range(span):
                raised = jnp.exp2(scores[j] * base - top).astype(BF)
                attended = attended + dot(raised, head(2, h, first + j))
            total = attended[:, LANES - 1 :]
            norms = jnp.where(lane == h, top + jnp.log2(total), norms)
            outs.append((attended * (1.0 / total)).astype(BF))
        norm_ref[0] = jnp.transpose(norms)[:8]
        packed = dot(jnp.concatenate(outs, axis=1), pick_ref[...]).astype(BF)
        out_ref[...] = packed.reshape(out_ref.shape)

    pl.when(length_ref[u] == 1)(lambda: work(1))
    pl.when(length_ref[u] != 1)(lambda: work(RATIO))


def attend_backward_kernel(
    heads,
    scale,
    start_ref,
    length_ref,
    qkv_ref,
    norm_ref,
    attended_ref,
    grad_ref,
    spread_ref,
    mark_ref,
    pick_ref,
    out_ref,
    dq,
    dk,
    dv,
    keys_across,
):
    parts, units, unit, _ = qkv_ref.shape
    base = softmax_base(scale)
    u = pl.program_id(0)
    first = start_ref[u]

    def head(which, h, at):
        lane = (which * heads + h) * LANES
        return qkv_ref[:, pl.ds(at, 1), :, lane : lane + LANES].reshape(parts * unit, LANES)

    @pl.when(u == 0)
    def _():
        dk[...] = jnp.zeros_like(dk)
        dv[...] = jnp.zeros_like(dv)

        def turn(i, carry):
            for h in range(heads):
                keys_across[i, h] = jnp.transpose(head(1, h, i))
            return carry

        lax.fori_loop(0, units, turn, 0)

    def work(span):
        packed = grad_ref[...].reshape(parts * unit, -1)
        grads = dot(packed, spread_ref[...]).astype(BF)
        product = packed.astype(F32) * attended_ref[...].reshape(parts * unit, -1).astype(F32)
        high = product.astype(BF)
        low = (product - high.astype(F32)).astype(BF)
        offsets = dot_general(mark_ref[...], high, (1, 1)) + dot_general(mark_ref[...], low, (1, 1))
        into = (parts, 1, unit, LANES)
        for h in range(heads):
            at = slice(h * LANES, (h + 1) * LANES)
            grad, query = grads[:, at], head(0, h, u)
            norm, offset = norm_ref[0, h : h + 1, :], offsets[h : h + 1]
            query_grad = 0.0
            for j in range(span):
                key, value = head(1, h, first + j), head(2, h, first + j)
                chance = jnp.exp2(dot_general(key, query, (1, 1)) * base - norm)
                chance_grad = dot_general(value, grad, (1, 1))
                score_grad = (chance * (chance_grad - offset)).astype(BF)
                block = pl.ds(first + j, 1)
                dv[:, block, :, at] += dot(chance.astype(BF), grad).reshape(into)
                dk[:, block, :, at] += dot(score_grad, query).reshape(into)
                query_grad = query_grad + dot(keys_across[first + j, h], score_grad)
            dq[:, pl.ds(u, 1), :, at] = jnp.transpose(query_grad * scale).astype(BF).reshape(into)

    pl.when(length_ref[u] == 1)(lambda: work(1))
    pl.when(length_ref[u] != 1)(lambda: work(RATIO))

    @pl.when(u == units - 1)
    def _():
        def pack(i, carry):
            at = pl.ds(i, 1)
            rows = [dq[:, at], (dk[:, at] * scale).astype(BF), dv[:, at].astype(BF)]
            rows = [row.reshape(parts * unit, -1) for row in rows]
            packed = dot(jnp.concatenate(rows, axis=1), pick_ref[...]).astype(BF)
            out_ref[:, at] = packed.reshape(parts, 1, unit, -1)
            return carry

        lax.fori_loop(0, units, pack, 0)


def whole_lanes(width):
    return -(-width // LANES) * LANES


def picker(heads, head_dim, dtype, width=None):
    row = jnp.arange(heads * LANES)[:, None]
    col = jnp.arange(heads * head_dim if width is None else width)[None, :]
    return ((row // LANES == col // head_dim) & (row % LANES == col % head_dim)).astype(dtype)


def attend_forward(start, length, qkv, heads, head_dim):
    parts, units, unit, lanes = qkv.shape
    width = heads * head_dim
    whole = lambda *shape: pl.BlockSpec(shape, lambda u, *_: (0,) * len(shape))
    return pl.pallas_call(
        partial(attend_forward_kernel, heads, 1.0 / math.sqrt(head_dim)),
        grid_spec=pltpu.PrefetchScalarGridSpec(
            num_scalar_prefetch=2,
            grid=(units,),
            in_specs=[whole(parts, units, unit, lanes), whole(heads * LANES, width)],
            out_specs=[
                pl.BlockSpec((parts, 1, unit, width), lambda u, *_: (0, u, 0, 0)),
                pl.BlockSpec((1, 8, parts * unit), lambda u, *_: (u, 0, 0)),
            ],
        ),
        out_shape=[
            jax.ShapeDtypeStruct((parts, units, unit, width), BF),
            jax.ShapeDtypeStruct((units, 8, parts * unit), F32),
        ],
        compiler_params=pltpu.CompilerParams(vmem_limit_bytes=48 * 2**20),
        cost_estimate=pl.CostEstimate(flops=10 * 2**30, bytes_accessed=16 * 2**20, transcendentals=2**23),
        name="attend_forward",
    )(start, length, qkv, picker(heads, head_dim, BF))


def attend_backward(start, length, qkv, norms, attended, grad, heads, head_dim):
    parts, units, unit, lanes = qkv.shape
    width = heads * head_dim
    whole = lambda *shape: pl.BlockSpec(shape, lambda u, *_: (0,) * len(shape))
    one_unit = pl.BlockSpec((parts, 1, unit, width), lambda u, *_: (0, u, 0, 0))
    pick = picker(heads, head_dim, BF)
    mark = (jnp.arange(8)[:, None] == jnp.arange(width)[None, :] // head_dim).astype(BF)
    return pl.pallas_call(
        partial(attend_backward_kernel, heads, 1.0 / math.sqrt(head_dim)),
        grid_spec=pltpu.PrefetchScalarGridSpec(
            num_scalar_prefetch=2,
            grid=(units,),
            in_specs=[
                whole(parts, units, unit, lanes),
                pl.BlockSpec((1, 8, parts * unit), lambda u, *_: (u, 0, 0)),
                one_unit,
                one_unit,
                whole(width, heads * LANES),
                whole(8, width),
                whole(3 * heads * LANES, whole_lanes(3 * width)),
            ],
            out_specs=whole(parts, units, unit, whole_lanes(3 * width)),
            scratch_shapes=[
                pltpu.VMEM((parts, units, unit, heads * LANES), BF),
                pltpu.VMEM((parts, units, unit, heads * LANES), F32),
                pltpu.VMEM((parts, units, unit, heads * LANES), F32),
                pltpu.VMEM((units, heads, LANES, parts * unit), BF),
            ],
        ),
        out_shape=jax.ShapeDtypeStruct((parts, units, unit, whole_lanes(3 * width)), BF),
        compiler_params=pltpu.CompilerParams(vmem_limit_bytes=56 * 2**20),
        cost_estimate=pl.CostEstimate(flops=40 * 2**30, bytes_accessed=16 * 2**20, transcendentals=2**23),
        name="attend_backward",
    )(start, length, qkv, norms, attended, grad, pick.T, mark, picker(3 * heads, head_dim, BF, whole_lanes(3 * width)))


MESH = pl.DeviceIdType.MESH


def add_into(ref, at, other):
    ref[at] = (ref[at].astype(F32) + other.astype(F32)).astype(BF)


def cut_rows(rows, k):
    up = (rows // 2 + 15) // 16 * 16
    return up if k % 2 == 0 else rows - up


def reduce_kernel(chunks, tensors, ring, *refs):
    grads, slots, refs = refs[:tensors], refs[tensors], refs[tensors + 1 :]
    outs, slots_out, scratch = refs[:tensors], refs[tensors], list(refs[tensors + 1 :])
    own, local_sem, send_sem, recv_sem, credit, gathered_parts, slots_line, slots_send, slots_recv = scratch[:9]
    rings = scratch[9:]
    place, z = lax.axis_index("img"), lax.axis_index("blk")
    y, x, c = lax.div(place, 4), lax.rem(lax.div(place, 2), 2), lax.rem(place, 2)
    pair, beside, across = place + 1 - 2 * c, place + 2 - 4 * x, place + 4 - 8 * y
    near, far = z + 1 - 2 * lax.rem(z, 2), 3 - z
    inside = (z == 1) | (z == 2)
    outside = (z == 0) | (z == 3)

    barrier = pltpu.get_barrier_semaphore()
    for step in (1, 2, 3):
        pl.semaphore_signal(barrier, inc=1, device_id={"blk": lax.rem(z + step, 4)}, device_id_type=MESH)
    others = [lax.rem(place + step, 8) for step in range(1, 8)]
    for other in others:
        pl.semaphore_signal(barrier, inc=1, device_id={"img": other}, device_id_type=MESH)
    pl.semaphore_wait(barrier, 10)

    def send(k, which, source, target, where):
        return pltpu.make_async_remote_copy(
            src_ref=source,
            dst_ref=target,
            send_sem=send_sem.at[k, which],
            recv_sem=recv_sem.at[k, which],
            device_id=where,
            device_id_type=MESH,
        )

    def parts_of(k):
        t, row, rows, col, cols, gather = chunks[k]
        return grads[t], outs[t], row, rows, col, cols, gather

    def cut(k):
        return cut_rows(chunks[k][2], k)

    def slot(k):
        _, _, rows, _, cols, _ = chunks[k]
        first = cut(k)
        i = k % ring
        wide = pl.ds(0, cols)
        acc, rx, ry, rx2, ry2, from_near, from_far, total = rings
        return (
            acc.at[i, :, :, pl.ds(0, rows), wide],
            rx.at[i, :, pl.ds(0, first), wide],
            ry.at[i, :, pl.ds(0, rows - first), wide],
            rx2.at[i, pl.ds(0, rows - first), wide],
            ry2.at[i, pl.ds(0, first), wide],
            from_near.at[i, pl.ds(0, rows), wide],
            from_far.at[i, :, pl.ds(0, rows), wide],
            total.at[i, pl.ds(0, rows), wide],
        )

    copies = {}

    def begin(k, which, source, target, where):
        copies[k, which] = send(k, which, source, target, where)
        copies[k, which].start()

    def load(k):
        grad, _, row, rows, col, cols, _ = parts_of(k)
        return pltpu.make_async_copy(
            grad.at[:, :, c, pl.ds(row, rows), pl.ds(col, cols)],
            own.at[k % 2, :, :, pl.ds(0, rows), pl.ds(0, cols)],
            local_sem.at[k % 2],
        )

    count = len(chunks)

    def stage_zero(k):
        grad, _, row, rows, col, cols, _ = parts_of(k)
        if k >= ring:
            pl.semaphore_wait(credit.at[k % ring], 5)
        begin(k, 0, grad.at[:, :, 1 - c, pl.ds(row, rows), pl.ds(col, cols)], slot(k)[0], {"img": pair})

    for k in range(min(ring, count)):
        stage_zero(k)
    for k in range(min(2, count)):
        load(k).start()

    wide_chunks = [k for k in range(count) if chunks[k][5]]

    def wide_total(k):
        _, _, rows, _, cols, _ = chunks[k]
        return gathered_parts.at[wide_chunks.index(k), :, pl.ds(0, rows), pl.ds(0, cols)]

    def stage_one(k):
        _, _, _, rows, _, cols, _ = parts_of(k)
        acc, rx, ry = slot(k)[:3]
        load(k).wait()
        copies[k, 0].wait_recv()
        for i in range(2):
            for j in range(2):
                add_into(acc, (i, j), own[k % 2, i, j, :rows, :cols])
        if k + 2 < count:
            load(k + 2).start()
        first = cut(k)
        begin(k, 1, acc.at[:, 1 - x, pl.ds(0, first)], rx, {"img": beside})
        begin(k, 2, acc.at[1 - y, :, pl.ds(first, rows - first)], ry, {"img": across})

    def stage_two(k):
        rows = chunks[k][2]
        acc, rx, ry, rx2, ry2 = slot(k)[:5]
        first = cut(k)
        copies[k, 1].wait_recv()
        copies[k, 2].wait_recv()
        copies[k, 1].wait_send()
        copies[k, 2].wait_send()
        for i in range(2):
            add_into(acc, (i, x, slice(0, first)), rx[i])
            add_into(acc, (y, i, slice(first, rows)), ry[i])
        begin(k, 3, acc.at[y, 1 - x, pl.ds(first, rows - first)], rx2, {"img": beside})
        begin(k, 4, acc.at[1 - y, x, pl.ds(0, first)], ry2, {"img": across})

    def stage_three(k):
        _, out, row, rows, col, cols, gather = parts_of(k)
        acc, _, _, rx2, ry2, from_near, from_far, total = slot(k)
        if gather:
            total = wide_total(k)
        first = cut(k)
        copies[k, 3].wait_recv()
        copies[k, 4].wait_recv()
        low = (acc[y, x, 0:first].astype(F32) + ry2[...].astype(F32)).astype(BF)
        high = (acc[y, x, first:rows].astype(F32) + rx2[...].astype(F32)).astype(BF)
        if gather:
            total[z, 0:first] = low
            total[z, first:rows] = high
            for step in (1, 2, 3):
                begin(k, 4 + step, total.at[z], total.at[z], {"blk": lax.rem(z + step, 4)})
            return
        from_far[0, 0:first] = low
        from_far[0, first:rows] = high
        copies[k, 5] = send(k, 5, from_far.at[0], from_near, {"blk": near})
        pl.when(outside)(copies[k, 5].start)

    def stage_four(k):
        if chunks[k][5]:
            return
        from_near, from_far, total = slot(k)[5:]
        copies[k, 6] = send(k, 6, from_far.at[0], from_far.at[1], {"blk": far})

        @pl.when(inside)
        def _():
            copies[k, 5].wait_recv()
            add_into(from_far, 0, from_near[...])
            copies[k, 6].start()

    def stage_five(k):
        if chunks[k][5]:
            return
        from_near, from_far, total = slot(k)[5:]
        copies[k, 7] = send(k, 7, total, total, {"blk": near})

        @pl.when(inside)
        def _():
            copies[k, 6].wait_recv()
            total[...] = (from_far[0].astype(F32) + from_far[1].astype(F32)).astype(BF)
            copies[k, 7].start()

    def stage_six(k):
        _, out, row, rows, col, cols, gather = parts_of(k)
        total = wide_total(k) if gather else slot(k)[7]
        if gather:
            for step in (1, 2, 3):
                copies[k, 4 + step].wait()
            out[:, row : row + rows, col : col + cols] = total[...]
        else:
            pl.when(outside)(copies[k, 7].wait_recv)
            out[row : row + rows, col : col + cols] = total[...]
            pl.when(outside)(copies[k, 5].wait_send)
            pl.when(inside)(copies[k, 6].wait_send)
            pl.when(inside)(copies[k, 7].wait_send)
        for which in (0, 3, 4):
            copies[k, which].wait_send()
        if k + ring < count:
            for other in (pair, beside, across):
                pl.semaphore_signal(credit.at[k % ring], inc=1, device_id={"img": other}, device_id_type=MESH)
            for other in (near, far):
                pl.semaphore_signal(credit.at[k % ring], inc=1, device_id={"blk": other}, device_id_type=MESH)

    def slots_copy(which, source, target, where):
        return pltpu.make_async_remote_copy(
            src_ref=source,
            dst_ref=target,
            send_sem=slots_send.at[which],
            recv_sem=slots_recv.at[which],
            device_id=where,
            device_id_type=MESH,
        )

    slots_near = slots_copy(0, slots, slots_line.at[0], {"blk": near})
    slots_far = slots_copy(8, slots_line.at[1], slots_line.at[2], {"blk": far})
    slots_back = slots_copy(9, slots_out.at[place], slots_out.at[place], {"blk": near})
    slots_round = [
        slots_copy(1 + i, slots_out.at[place], slots_out.at[place], {"img": other}) for i, other in enumerate(others)
    ]

    def slots_one():
        pl.when(outside)(slots_near.start)

    def slots_two():
        @pl.when(inside)
        def _():
            slots_near.wait_recv()
            slots_line[1] = slots_line[0] + slots[...]
            slots_far.start()

    def slots_three():
        @pl.when(inside)
        def _():
            slots_far.wait_recv()
            slots_out[place] = slots_line[1] + slots_line[2]
            slots_back.start()

    def slots_four():
        pl.when(outside)(slots_back.wait_recv)
        for copy in slots_round:
            copy.start()

    def slots_five():
        for copy in slots_round:
            copy.wait()
        pl.when(outside)(slots_near.wait_send)
        pl.when(inside)(slots_far.wait_send)
        pl.when(inside)(slots_back.wait_send)

    slots_stages = {0: slots_one, 2: slots_two, 4: slots_three, 6: slots_four, 9: slots_five}
    stages = ((stage_one, 0), (stage_two, 2), (stage_three, 4), (stage_four, 5), (stage_five, 6), (stage_six, 7))
    for step in range(max(count + 7, 10)):
        for stage, behind in stages:
            if 0 <= step - behind < count:
                stage(step - behind)
        if step - 8 >= 0 and step - 8 + ring < count:
            stage_zero(step - 8 + ring)
        if step in slots_stages:
            slots_stages[step]()


def reduce_call(grads, gathered, slots, width, collective_id):
    chunks, shapes = [], []
    for t, grad in enumerate(grads):
        rows, cols = grad.shape[0] // 8, grad.shape[1]
        depth = 144 if rows % 144 == 0 else 128
        for row in range(0, rows, depth):
            for col in range(0, cols, width):
                chunks.append((t, row, min(depth, rows - row), col, min(width, cols - col), gathered[t]))
        shapes.append(jax.ShapeDtypeStruct((4, rows, cols) if gathered[t] else (rows, cols), BF))
    shapes.append(jax.ShapeDtypeStruct((8, *slots.shape), F32))
    n, ring = len(chunks), 12
    deep = max(rows for _, _, rows, _, _, _ in chunks)
    half = (deep // 2 + 15) // 16 * 16
    dma = pltpu.SemaphoreType.DMA
    scratch = [
        pltpu.VMEM((2, 2, 2, deep, width), BF),
        dma((2,)),
        dma((n, 8)),
        dma((n, 8)),
        pltpu.SemaphoreType.REGULAR((ring,)),
        pltpu.VMEM((max(1, sum(g for *_, g in chunks)), 4, deep, width), BF),
        pltpu.VMEM((3, *slots.shape), F32),
        dma((10,)),
        dma((10,)),
    ]
    for shape in (
        (2, 2, deep, width),
        (2, half, width),
        (2, half, width),
        (half, width),
        (half, width),
        (deep, width),
        (2, deep, width),
        (deep, width),
    ):
        scratch.append(pltpu.VMEM((ring, *shape), BF))
    vmem, anywhere = pl.BlockSpec(memory_space=pltpu.VMEM), pl.BlockSpec(memory_space=pl.ANY)
    return pl.pallas_call(
        partial(reduce_kernel, chunks, len(grads), ring),
        out_shape=shapes,
        in_specs=[anywhere] * len(grads) + [vmem],
        out_specs=[vmem] * (len(grads) + 1),
        scratch_shapes=scratch,
        compiler_params=pltpu.CompilerParams(
            collective_id=collective_id, has_side_effects=True, vmem_limit_bytes=56 * 2**20
        ),
        cost_estimate=pl.CostEstimate(flops=0, bytes_accessed=500 * 2**20, transcendentals=0),
        name=f"reduce_{collective_id}",
    )(*(g.reshape(2, 2, 2, g.shape[0] // 8, g.shape[1]) for g in grads), slots)


def gather_kernel(chunks, tensors, early, hot_ref, x_ref, share_ref, bias_ref, start_ref, *refs):
    shards, refs = refs[:tensors], refs[tensors:]
    fulls, refs = refs[:tensors], refs[tensors:]
    rows_ref, modulation_ref, bias_out = refs[:3]
    share_got, own_sem, first_send, first_recv, rest_send, rest_recv, bias_send, bias_recv = refs[3:11]
    send_sem, recv_sem, line_send, line_recv, spread_send, spread_recv = refs[11:]
    place, z = lax.axis_index("img"), lax.axis_index("blk")
    y, x, c = lax.div(place, 4), lax.rem(lax.div(place, 2), 2), lax.rem(place, 2)
    step_x, step_y = 2 - 4 * x, 4 - 8 * y
    pair, beside, across = place + 1 - 2 * c, place + step_x, place + step_y
    diagonal = place + step_x + step_y
    devices = share_got.shape[0]
    units, slots = hot_ref.shape
    unit = x_ref.shape[0] // units
    wide = x_ref.shape[1]

    barrier = pltpu.get_barrier_semaphore()
    for step in range(1, devices):
        pl.semaphore_signal(barrier, inc=1, device_id={"img": lax.rem(place + step, devices)}, device_id_type=MESH)
    for step in (1, 2, 3):
        pl.semaphore_signal(barrier, inc=1, device_id={"blk": lax.rem(z + step, 4)}, device_id_type=MESH)
    pl.semaphore_wait(barrier, devices + 2)

    def remote(source, target, send, recv, where):
        return pltpu.make_async_remote_copy(
            src_ref=source,
            dst_ref=target,
            send_sem=send,
            recv_sem=recv,
            device_id=where,
            device_id_type=MESH,
        )

    part = (share_ref.shape[2] - early) // 4
    part_at = pl.multiple_of(early + z * part, LANES)
    first, rest, biases = [], [], []
    for step in range(1, devices):
        to = lax.rem(place + step, devices)
        for copies, lo, size, send, recv in (
            (first, 0, early, first_send, first_recv),
            (rest, part_at, part, rest_send, rest_recv),
        ):
            copies.append(
                remote(
                    share_ref.at[to, :, pl.ds(lo, size)],
                    share_got.at[place, :, pl.ds(lo, size)],
                    send.at[step],
                    recv.at[step],
                    {"img": to},
                )
            )
        biases.append(remote(bias_ref, bias_out.at[place], bias_send.at[step], bias_recv.at[step], {"img": to}))
    for copy in first:
        copy.start()

    copies = {}

    def begin(k, which, block, rows, where):
        t, row, count = chunks[k]
        at = (block, pl.ds(row + rows[0], rows[1]))
        copies[k, which] = remote(
            fulls[t].at[at], fulls[t].at[at], send_sem.at[k, which], recv_sem.at[k, which], where
        )
        copies[k, which].start()

    def begin_own(k, which, where):
        t, row, count = chunks[k]
        source = shards[t].at[pl.ds(row, count)]
        copies[k, which] = remote(
            source, fulls[t].at[place, pl.ds(row, count)], send_sem.at[k, which], recv_sem.at[k, which], where
        )
        copies[k, which].start()

    own = [pltpu.make_async_copy(shards[t], fulls[t].at[place], own_sem.at[t]) for t in range(tensors)]
    def ahead(k):
        if k < len(chunks):
            begin_own(k, 0, {"img": beside})
            begin_own(k, 1, {"img": across})
            begin_own(k, 2, {"img": pair})

    ahead(0)
    for copy in rest + biases:
        copy.start()
    for k in range(1, 3):
        ahead(k)
    for copy in own:
        copy.start()

    share_got[place] = share_ref[place]
    bias_out[place] = bias_ref[...]
    for copy in first:
        copy.wait()

    def modulation_of(lo, size):
        at = pl.ds(lo, size)
        total = share_got[0, :, at]
        for i in range(1, devices):
            total = total + share_got[i, :, at]
        modulation_ref[:, at] = start_ref[:, at] + total

    modulation_of(0, early)
    for u in range(units):
        chosen = hot_ref[u : u + 1, 0:1] * modulation_ref[0:1, 0:early]
        for s in range(1, slots):
            chosen = chosen + hot_ref[u : u + 1, s : s + 1] * modulation_ref[s : s + 1, 0:early]
        at = pl.ds(u * unit, unit)
        values = x_ref[at, :].astype(F32)
        centered = values - jnp.mean(values, axis=1, keepdims=True)
        inverse = lax.rsqrt(jnp.mean(centered * centered, axis=1, keepdims=True) + EPSILON)
        rows_ref[z, at, :] = (centered * inverse * (1.0 + chosen[:, wide:]) + chosen[:, :wide]).astype(BF)

    up = [
        remote(block, block, line_send.at[0, s], line_recv.at[0, s], {"blk": lax.rem(z + 1, 4)})
        for s, block in ((s, rows_ref.at[lax.rem(z - s + 4, 4)]) for s in range(3))
    ]
    down = [
        remote(block, block, line_send.at[1, s], line_recv.at[1, s], {"blk": lax.rem(z + 3, 4)})
        for s, block in ((s, rows_ref.at[lax.rem(z + s, 4)]) for s in range(3))
    ]

    def line_step(s):
        if s > 0:
            pl.when(z >= s)(up[s - 1].wait_recv)
            pl.when(z + s < 4)(down[s - 1].wait_recv)
        if s < 3:
            pl.when((z >= s) & (z < 3))(up[s].start)
            pl.when((z + s < 4) & (z > 0))(down[s].start)

    def cut(k):
        return cut_rows(chunks[k][2], k)

    def relay(k):
        count, half = chunks[k][2], cut(k)
        copies[k, 0].wait_recv()
        begin(k, 3, beside, (0, half), {"img": across})
        begin(k, 5, beside, (0, count), {"img": pair})
        copies[k, 1].wait_recv()
        begin(k, 4, across, (half, count - half), {"img": beside})
        begin(k, 6, across, (0, count), {"img": pair})

    def last(k):
        count, half = chunks[k][2], cut(k)
        copies[k, 3].wait_recv()
        begin(k, 7, diagonal, (0, half), {"img": pair})
        copies[k, 4].wait_recv()
        begin(k, 8, diagonal, (half, count - half), {"img": pair})

    line_step(0)
    for copy in rest:
        copy.wait()
    modulation_of(part_at, part)
    own_part = modulation_ref.at[:, pl.ds(part_at, part)]
    spread = [
        remote(own_part, own_part, spread_send.at[step], spread_recv.at[step], {"blk": lax.rem(z + step, 4)})
        for step in (1, 2, 3)
    ]
    for copy in spread:
        copy.start()
    n = len(chunks)
    for k in range(n + 2):
        if k < n:
            relay(k)
            ahead(k + 3)
        if k >= 2:
            last(k - 2)
        for s in (1, 2):
            if k == 2 * s - 1:
                line_step(s)
    for copy in biases:
        copy.wait()
    line_step(3)
    for copy in spread:
        copy.wait()
    for copy in own:
        copy.wait()
    for k in range(n):
        for which in (0, 1, 3, 4):
            copies[k, which].wait_send()
        copies[k, 2].wait()
        for which in (5, 6, 7, 8):
            copies[k, which].wait()
    for s in range(3):
        pl.when((z >= s) & (z < 3))(up[s].wait_send)
        pl.when((z + s < 4) & (z > 0))(down[s].wait_send)


def gather_call(shards, unit_hot, rows, shares, bias_row, modulate_bias, collective_id):
    devices = shares.shape[0]
    slots, wide = shares.shape[1:]
    chunks = []
    for t, shard in enumerate(shards):
        depth = shard.shape[0]
        for row in range(0, depth, 144):
            chunks.append((t, row, min(144, depth - row)))
    n = len(chunks)
    vmem, anywhere = pl.BlockSpec(memory_space=pltpu.VMEM), pl.BlockSpec(memory_space=pl.ANY)
    dma = pltpu.SemaphoreType.DMA
    first_modulation = jnp.broadcast_to(modulate_bias.astype(F32)[None, :], (slots, wide))
    return pl.pallas_call(
        partial(gather_kernel, chunks, len(shards), 2 * rows.shape[1]),
        out_shape=[jax.ShapeDtypeStruct((devices, *s.shape), BF) for s in shards]
        + [
            jax.ShapeDtypeStruct((4, *rows.shape), BF),
            jax.ShapeDtypeStruct((slots, wide), F32),
            jax.ShapeDtypeStruct((devices, *bias_row.shape), F32),
        ],
        in_specs=[vmem] * 5 + [anywhere] * len(shards),
        out_specs=[anywhere] * len(shards) + [vmem] * 3,
        scratch_shapes=[
            pltpu.VMEM((devices, slots, wide), F32),
            dma((len(shards),)),
            dma((devices,)),
            dma((devices,)),
            dma((devices,)),
            dma((devices,)),
            dma((devices,)),
            dma((devices,)),
            dma((n, 9)),
            dma((n, 9)),
            dma((2, 3)),
            dma((2, 3)),
            dma((4,)),
            dma((4,)),
        ],
        compiler_params=pltpu.CompilerParams(
            collective_id=collective_id, has_side_effects=True, vmem_limit_bytes=48 * 2**20
        ),
        cost_estimate=pl.CostEstimate(flops=0, bytes_accessed=450 * 2**20, transcendentals=0),
        name=f"gather_{collective_id}",
    )(unit_hot, rows, shares, bias_row, first_modulation, *shards)


def total_kernel(mine_ref, out_ref, lines, line_send, line_recv, send_sem, recv_sem):
    place, z = lax.axis_index("img"), lax.axis_index("blk")
    parts, devices = lines.shape[0], out_ref.shape[0]
    barrier = pltpu.get_barrier_semaphore()
    for step in range(1, parts):
        pl.semaphore_signal(barrier, inc=1, device_id={"blk": lax.rem(z + step, parts)}, device_id_type=MESH)
    for step in range(1, devices):
        pl.semaphore_signal(barrier, inc=1, device_id={"img": lax.rem(place + step, devices)}, device_id_type=MESH)
    pl.semaphore_wait(barrier, parts + devices - 2)

    lines[z] = mine_ref[...]
    copies = [
        pltpu.make_async_remote_copy(
            src_ref=lines.at[z],
            dst_ref=lines.at[z],
            send_sem=line_send.at[step],
            recv_sem=line_recv.at[step],
            device_id={"blk": lax.rem(z + step, parts)},
            device_id_type=MESH,
        )
        for step in range(1, parts)
    ]
    for copy in copies:
        copy.start()
    for copy in copies:
        copy.wait()
    total = lines[0]
    for step in range(1, parts):
        total = total + lines[step]
    out_ref[place] = total
    copies = [
        pltpu.make_async_remote_copy(
            src_ref=out_ref.at[place],
            dst_ref=out_ref.at[place],
            send_sem=send_sem.at[step],
            recv_sem=recv_sem.at[step],
            device_id={"img": lax.rem(place + step, devices)},
            device_id_type=MESH,
        )
        for step in range(1, devices)
    ]
    for copy in copies:
        copy.start()
    for copy in copies:
        copy.wait()


def total_call(mine, devices, parts, collective_id):
    if (devices, parts) != (8, 4):
        return lax.all_gather(lax.psum(mine, "blk"), "img", axis=0, tiled=False)
    return pl.pallas_call(
        total_kernel,
        out_shape=jax.ShapeDtypeStruct((devices, *mine.shape), mine.dtype),
        in_specs=[pl.BlockSpec(memory_space=pltpu.VMEM)],
        out_specs=pl.BlockSpec(memory_space=pltpu.VMEM),
        scratch_shapes=[
            pltpu.VMEM((parts, *mine.shape), mine.dtype),
            pltpu.SemaphoreType.DMA((parts,)),
            pltpu.SemaphoreType.DMA((parts,)),
            pltpu.SemaphoreType.DMA((devices,)),
            pltpu.SemaphoreType.DMA((devices,)),
        ],
        compiler_params=pltpu.CompilerParams(
            collective_id=collective_id, has_side_effects=True, vmem_limit_bytes=32 * 2**20
        ),
        name=f"total_{collective_id}",
    )(mine)


def per_device(
    inputs,
    token_image,
    image_time,
    image_class,
    targets,
    cotangent,
    class_table,
    modulate_weight,
    modulate_bias,
    attend_weight,
    attend_bias,
    output_weight,
    output_bias,
    expand_weight,
    expand_bias,
    shrink_weight,
    shrink_bias,
    inner_weight,
    inner_bias,
    middle_weight,
    middle_bias,
    outer_weight,
    outer_bias,
):
    count, width = inputs.shape
    head_dim = width // HEADS
    columns = class_table.shape[1]
    devices, parts = lax.axis_size("img"), lax.axis_size("blk")
    place_img, place_blk = lax.axis_index("img"), lax.axis_index("blk")
    slots = image_class.shape[0] // devices
    unit = SHORT // parts
    units = count // unit
    heads = HEADS // parts
    mine = heads * head_dim
    half = width // 2

    class_hot = (image_class[:, None] == jnp.arange(class_table.shape[0])[None, :]).astype(BF)
    column = place_img * columns + jnp.arange(columns)
    frequency = jnp.exp(-math.log(10000.0) * (column % half).astype(F32) / half)
    angle = image_time.astype(F32)[:, None] * frequency[None, :]
    condition = dot(class_hot, class_table) + jnp.where(column[None, :] < half, jnp.cos(angle), jnp.sin(angle))
    silu_condition = jax.nn.silu(condition).astype(BF)
    shares = dot(silu_condition, modulate_weight)
    biases = (attend_bias, output_bias, expand_bias, shrink_bias, inner_bias, middle_bias, outer_bias)
    bias_row = jnp.concatenate(biases).astype(F32)
    bias_row = jnp.pad(bias_row, (0, whole_lanes(bias_row.shape[0]) - bias_row.shape[0]))[None, :]
    shares = shares.reshape(devices, slots, -1)

    labels = token_image[::unit]
    same = labels[:, None] == labels[None, :]
    start = jnp.argmax(same, axis=1).astype(jnp.int32)
    length = jnp.sum(same, axis=1).astype(jnp.int32)
    unit_hot = (labels[:, None] == jnp.arange(slots)[None, :]).astype(F32)
    def by_unit(values):
        return values.reshape(units, unit, width)

    def by_row(values):
        return values.reshape(count, width)

    attend_mine = lax.dynamic_slice_in_dim(
        attend_weight.reshape(-1, 3, parts, mine), place_blk, 1, axis=2
    ).reshape(-1, 3 * mine)
    attend_mine = jnp.pad(attend_mine, ((0, 0), (0, whole_lanes(3 * mine) - 3 * mine)))

    def gather(shard):
        return lax.all_gather(shard, "img", axis=0, tiled=True)

    source = by_unit(inputs.astype(F32))
    normal_one, inverse_one = layer_norm(source)
    first_weights = (attend_mine, output_weight, expand_weight, outer_weight, shrink_weight)
    if (devices, parts) == (8, 4):
        *fulls, rows_group, modulation, got_bias = gather_call(
            first_weights, unit_hot, inputs, shares, bias_row, modulate_bias, 3
        )
        fulls = [full.reshape(-1, full.shape[2]) for full in fulls]
        modulated_group = rows_group.reshape(parts * count, width)
    else:
        fulls = [gather(shard) for shard in first_weights]
        modulation = modulate_bias.astype(F32)[None, :] + lax.psum_scatter(
            shares.reshape(devices * slots, -1), "img", scatter_dimension=0, tiled=True
        )
        got_bias = lax.all_gather(bias_row, "img", axis=0, tiled=False)
        chosen = jnp.dot(unit_hot, modulation, precision=HIGH)[:, None, : 2 * width]
        modulated_one = normal_one * (1.0 + chosen[:, :, width:]) + chosen[:, :, :width]
        modulated_group = lax.all_gather(by_row(modulated_one.astype(BF)), "blk", axis=0, tiled=True)
    attend_full, output_full, expand_full, outer_full, shrink_full = fulls
    inner_shard, middle_shard, modulated_group = lax.optimization_barrier(
        (inner_weight, middle_weight, modulated_group)
    )
    inner_full, middle_full = gather(inner_shard), gather(middle_shard)
    full_biases = []
    at = 0
    for bias in biases:
        full_biases.append(got_bias[:, 0, at : at + bias.shape[0]].reshape(-1))
        at += bias.shape[0]
    (
        attend_bias_full,
        output_bias_full,
        expand_bias_full,
        shrink_bias_full,
        inner_bias_full,
        middle_bias_full,
        outer_bias_full,
    ) = full_biases
    unit_modulation = jnp.dot(unit_hot, modulation, precision=HIGH)
    shift_one, scale_one, gate_one, shift_two, scale_two, gate_two = (
        block[:, None, :] for block in jnp.split(unit_modulation, 6, axis=1)
    )

    def pad_heads(values):
        lead = values.shape[:-1]
        values = values.reshape(*lead, 3 * heads, head_dim)
        values = jnp.pad(values, ((0, 0),) * len(lead) + ((0, 0), (0, LANES - head_dim)))
        return values.reshape(*lead, 3 * heads * LANES)

    bias_mine = lax.dynamic_slice_in_dim(attend_bias_full.reshape(2, parts, mine), place_blk, 1, axis=1)
    bias_mine = jnp.concatenate([bias_mine[0, 0], jnp.zeros((mine,), F32), bias_mine[1, 0]])
    is_value = jnp.arange(3 * heads * LANES) >= 2 * heads * LANES
    is_last = jnp.arange(3 * heads * LANES) % LANES == LANES - 1
    padded_bias = jnp.where(is_value & is_last, 1.0, pad_heads(bias_mine))
    projected = dot(modulated_group, pad_heads(attend_full[:, : 3 * mine])) + padded_bias[None, :]
    qkv = projected.astype(BF).reshape(parts, units, unit, 3 * heads * LANES)
    attended_heads, norms = attend_forward(start, length, qkv, heads, head_dim)
    attended = lax.all_to_all(
        attended_heads.reshape(parts, count, mine), "blk", split_axis=0, concat_axis=0, tiled=True
    )
    output_heads = output_full.reshape(parts, mine, width)
    branch_one = by_unit(
        jnp.einsum("pti,pio->to", attended, output_heads, preferred_element_type=F32) + output_bias_full
    )
    middle = source + gate_one * branch_one
    normal_two, inverse_two = layer_norm(middle)
    modulated_two = by_row((normal_two * (1.0 + scale_two) + shift_two).astype(BF))
    expanded = dot(modulated_two, expand_full) + expand_bias_full
    gelu_tanh = partial(jax.nn.gelu, approximate=True)
    activated = gelu_tanh(expanded).astype(BF)
    branch_two = by_unit(dot(activated, shrink_full) + shrink_bias_full)
    whole = middle + gate_two * branch_two
    whole_low = by_row(whole.astype(BF))
    pre_one = dot(whole_low, inner_full) + inner_bias_full
    first = jax.nn.silu(pre_one).astype(BF)
    pre_two = dot(first, middle_full) + middle_bias_full
    second = jax.nn.silu(pre_two).astype(BF)
    aligned = dot(second, outer_full) + outer_bias_full
    target = targets.astype(F32)
    cross = jnp.sum(aligned * target, axis=1)
    aligned_inverse = lax.rsqrt(jnp.sum(aligned * aligned, axis=1) + EPSILON)
    target_inverse = lax.rsqrt(jnp.sum(target * target, axis=1) + EPSILON)
    cosine = cross * aligned_inverse * target_inverse
    grad_aligned = (
        -0.5
        * (
            target * (aligned_inverse * target_inverse)[:, None]
            - (cosine * aligned_inverse * aligned_inverse)[:, None] * aligned
        )
    ).astype(BF)

    def scatter(values):
        return lax.psum_scatter(values, "img", scatter_dimension=0, tiled=True)

    grad_outer = left_product(second, grad_aligned)
    grad_outer_bias = column_sum(grad_aligned)
    grad_pre_two = local_back(jax.nn.silu, pre_two, right_product(grad_aligned, outer_full)).astype(BF)
    grad_middle_weight = left_product(first, grad_pre_two)
    grad_middle_bias = column_sum(grad_pre_two)
    grad_pre_one = local_back(jax.nn.silu, pre_one, right_product(grad_pre_two, middle_full)).astype(BF)
    grad_inner = left_product(whole_low, grad_pre_one)
    grad_inner_bias = column_sum(grad_pre_one)
    grad_whole = by_unit(cotangent.astype(F32)) + by_unit(right_product(grad_pre_one, inner_full))
    grad_gate_two = grad_whole * branch_two
    grad_branch_two = by_row((grad_whole * gate_two).astype(BF))
    grad_shrink = left_product(activated, grad_branch_two)
    grad_shrink_bias = column_sum(grad_branch_two)
    grad_expanded = local_back(gelu_tanh, expanded, right_product(grad_branch_two, shrink_full)).astype(BF)
    grad_expand = left_product(modulated_two, grad_expanded)
    grad_expand_bias = column_sum(grad_expanded)
    grad_mod_two = by_unit(right_product(grad_expanded, expand_full))
    grad_scale_two = grad_mod_two * normal_two
    grad_middle = grad_whole + norm_back(grad_mod_two * (1.0 + scale_two), normal_two, inverse_two)
    grad_gate_one = grad_middle * branch_one
    grad_branch_one = by_row((grad_middle * gate_one).astype(BF))
    grad_output = jnp.einsum("pti,to->pio", attended, grad_branch_one, preferred_element_type=F32)
    grad_output = grad_output.astype(BF).reshape(width, width)
    grad_output_bias = column_sum(grad_branch_one)
    def slot_sum(*values):
        rows = jnp.concatenate([jnp.sum(v, axis=1) for v in values], axis=1)
        return jnp.dot(unit_hot.T, rows, precision=HIGH)

    early_slots = slot_sum(grad_gate_one, grad_mod_two, grad_scale_two, grad_gate_two)
    grad_attended = jnp.einsum("to,pio->pti", grad_branch_one, output_heads, preferred_element_type=F32)
    grad_heads = lax.all_to_all(grad_attended.astype(BF), "blk", split_axis=0, concat_axis=0, tiled=True)
    grad_heads = grad_heads.reshape(parts, units, unit, mine)
    grad_qkv = attend_backward(start, length, qkv, norms, attended_heads, grad_heads, heads, head_dim).reshape(parts * count, -1)
    grad_attend = left_product(modulated_group, grad_qkv)
    partial_mod_one = right_product(grad_qkv, attend_full).astype(BF)
    grads = (
        grad_outer,
        grad_middle_weight,
        grad_inner,
        grad_attend,
        grad_output,
        grad_shrink,
        grad_expand,
    )
    gathered = (False, False, False, True, False, False, False)
    if (devices, parts) == (8, 4):
        *sums, early_grad = reduce_call(grads, gathered, early_slots, 640, 1)
    else:
        sums = [scatter(grad) for grad in grads]
        attend_part = lax.all_gather(sums[3], "blk", axis=0, tiled=False)
        sums = list(lax.psum(tuple(sums[:3] + sums[4:]), "blk"))
        sums.insert(3, attend_part)
        early_grad = lax.all_gather(lax.psum(early_slots, "blk"), "img", axis=0, tiled=False)
    outer_sum, middle_sum, inner_sum, attend_parts, output_sum, shrink_sum, expand_sum = sums
    early_grad = early_grad.reshape(devices * slots, -1)
    attend_parts = attend_parts[:, :, : 3 * mine].reshape(parts, -1, 3, mine)
    attend_sum = jnp.transpose(attend_parts, (1, 2, 0, 3)).reshape(-1, 3 * width)
    grad_mod_one = lax.psum_scatter(partial_mod_one, "blk", scatter_dimension=0, tiled=True)
    grad_mod_one, early_grad = lax.optimization_barrier((grad_mod_one, early_grad))
    grad_mod_one = by_unit(grad_mod_one.astype(F32))
    grad_scale_one = grad_mod_one * normal_one
    grad_source = grad_middle + norm_back(grad_mod_one * (1.0 + scale_one), normal_one, inverse_one)

    qkv_bias = column_sum(grad_qkv[:, : 3 * mine]).reshape(3, 1, mine)
    spread = (jnp.arange(parts) == place_blk).astype(F32)[None, :, None]
    attend_bias_rows = jnp.concatenate([qkv_bias[:1], qkv_bias[2:]]) * spread
    bias_grads = (
        attend_bias_rows,
        grad_output_bias,
        grad_expand_bias,
        grad_shrink_bias,
        grad_inner_bias,
        grad_middle_bias,
        grad_outer_bias,
    )
    bias_rows = jnp.concatenate([b.reshape(devices, -1) for b in bias_grads], axis=1)
    late_slots = slot_sum(grad_mod_one, grad_scale_one)
    late_rows = jnp.concatenate(
        [late_slots, jnp.pad(bias_rows, ((0, 0), (0, late_slots.shape[1] - bias_rows.shape[1])))], axis=0
    )
    late = total_call(late_rows, devices, parts, 2)
    late_grad = late[:, :slots].reshape(devices * slots, 2 * width)
    bias_sum = jnp.sum(lax.dynamic_index_in_dim(late, slots + place_img, axis=1, keepdims=False), axis=0)
    bias_sums = []
    at = 0
    for bias in biases:
        bias_sums.append(bias_sum[at : at + bias.shape[0]])
        at += bias.shape[0]
    (
        attend_bias_sum,
        output_bias_sum,
        expand_bias_sum,
        shrink_bias_sum,
        inner_bias_sum,
        middle_bias_sum,
        outer_bias_sum,
    ) = bias_sums
    modulation_grad = jnp.concatenate([late_grad, early_grad], axis=1)
    modulate_sum = jnp.dot(silu_condition.astype(F32).T, modulation_grad, precision=HIGH)
    modulate_bias_sum = jnp.sum(modulation_grad, axis=0)
    silu_grad = jnp.dot(modulation_grad, modulate_weight.astype(F32).T, precision=HIGH)
    condition_grad = local_back(jax.nn.silu, condition, silu_grad)
    table_sum = jnp.dot(class_hot.astype(F32).T, condition_grad, precision=HIGH)
    return (
        whole_low,
        by_row(grad_source.astype(BF)),
        table_sum,
        modulate_sum,
        modulate_bias_sum,
        attend_sum.astype(F32),
        attend_bias_sum,
        output_sum.astype(F32),
        output_bias_sum,
        expand_sum.astype(F32),
        expand_bias_sum,
        shrink_sum.astype(F32),
        shrink_bias_sum,
        inner_sum.astype(F32),
        inner_bias_sum,
        middle_sum.astype(F32),
        middle_bias_sum,
        outer_sum.astype(F32),
        outer_bias_sum,
    )


def solution(mesh):
    in_specs = (
        P(("img", "blk"), None),
        P(("img", "blk")),
        P(),
        P(),
        P(("img", "blk"), None),
        P(("img", "blk"), None),
        P(None, "img"),
        P("img", None),
        P(),
        P("img", None),
        P("img"),
        P("img", None),
        P("img"),
        P("img", None),
        P("img"),
        P("img", None),
        P("img"),
        P("img", None),
        P("img"),
        P("img", None),
        P("img"),
        P("img", None),
        P("img"),
    )
    out_specs = (
        P(("img", "blk"), None),
        P(("img", "blk"), None),
        P(None, "img"),
        P("img", None),
        P(),
        P("img", None),
        P("img"),
        P("img", None),
        P("img"),
        P("img", None),
        P("img"),
        P("img", None),
        P("img"),
        P("img", None),
        P("img"),
        P("img", None),
        P("img"),
        P("img", None),
        P("img"),
    )
    return jax.shard_map(
        per_device, mesh=mesh, in_specs=in_specs, out_specs=out_specs, check_vma=False
    )
```

```python
from functools import partial
import math

import jax
import jax.numpy as jnp
from jax import lax
from jax.experimental import pallas as pl
from jax.experimental.pallas import tpu as pltpu
from jax.sharding import PartitionSpec as P

HEADS = 16
SHORT = 256
RATIO = 4
LANES = 128

EPSILON = 1e-06
HIGH = lax.Precision.HIGHEST
BF = jnp.bfloat16
F32 = jnp.float32


def layer_norm(values):
    mean = jnp.mean(values, axis=-1, keepdims=True)
    centered = values - mean
    variance = jnp.mean(centered * centered, axis=-1, keepdims=True)
    inverse = lax.rsqrt(variance + EPSILON)
    return (centered * inverse, inverse)


def norm_back(grad, normal, inverse):
    mean_grad = jnp.mean(grad, axis=-1, keepdims=True)
    mean_cross = jnp.mean(grad * normal, axis=-1, keepdims=True)
    return inverse * (grad - mean_grad - normal * mean_cross)


def local_back(function, point, grad):
    return jax.vjp(function, point)[1](grad)[0]


def left_product(left, right):
    return jnp.einsum("ti,to->io", left, right, preferred_element_type=F32).astype(BF)


def right_product(grad, weight):
    return jnp.einsum("to,io->ti", grad, weight, preferred_element_type=F32)


def column_sum(values):
    return jnp.sum(values.astype(F32), axis=0)


def dot(left, right):
    return jnp.dot(left, right, preferred_element_type=F32)


def dot_general(left, right, contract):
    return lax.dot_general(left, right, ((contract[:1], contract[1:]), ((), ())), preferred_element_type=F32)


def softmax_base(scale):
    return scale * math.log2(math.e)


def attend_forward_kernel(heads, scale, start_ref, length_ref, qkv_ref, pick_ref, out_ref, norm_ref):
    parts, _, unit, _ = qkv_ref.shape
    base = softmax_base(scale)
    u = pl.program_id(0)
    first = start_ref[u]

    def head(which, h, at):
        lane = (which * heads + h) * LANES
        return qkv_ref[:, pl.ds(at, 1), :, lane : lane + LANES].reshape(parts * unit, LANES)

    def work(span):
        outs = []
        lane = lax.broadcasted_iota(jnp.int32, (parts * unit, LANES), 1)
        norms = jnp.zeros((parts * unit, LANES), F32)
        for h in range(heads):
            query = head(0, h, u)
            scores = [dot_general(query, head(1, h, first + j), (1, 1)) for j in range(span)]
            top = scores[0]
            for block in scores[1:]:
                top = jnp.maximum(top, block)
            top = jnp.max(top, axis=1, keepdims=True) * base
            attended = 0.0
            for j in range(span):
                raised = jnp.exp2(scores[j] * base - top).astype(BF)
                attended = attended + dot(raised, head(2, h, first + j))
            total = attended[:, LANES - 1 :]
            norms = jnp.where(lane == h, top + jnp.log2(total), norms)
            outs.append((attended * (1.0 / total)).astype(BF))
        norm_ref[0] = jnp.transpose(norms)[:8]
        packed = dot(jnp.concatenate(outs, axis=1), pick_ref[...]).astype(BF)
        out_ref[...] = packed.reshape(out_ref.shape)

    pl.when(length_ref[u] == 1)(lambda: work(1))
    pl.when(length_ref[u] != 1)(lambda: work(RATIO))


def attend_backward_kernel(
    heads,
    scale,
    start_ref,
    length_ref,
    qkv_ref,
    norm_ref,
    attended_ref,
    grad_ref,
    spread_ref,
    mark_ref,
    pick_ref,
    out_ref,
    dq,
    dk,
    dv,
    keys_across,
):
    parts, units, unit, _ = qkv_ref.shape
    base = softmax_base(scale)
    u = pl.program_id(0)
    first = start_ref[u]

    def head(which, h, at):
        lane = (which * heads + h) * LANES
        return qkv_ref[:, pl.ds(at, 1), :, lane : lane + LANES].reshape(parts * unit, LANES)

    @pl.when(u == 0)
    def _():
        dk[...] = jnp.zeros_like(dk)
        dv[...] = jnp.zeros_like(dv)

        def turn(i, carry):
            for h in range(heads):
                keys_across[i, h] = jnp.transpose(head(1, h, i))
            return carry

        lax.fori_loop(0, units, turn, 0)

    def work(span):
        packed = grad_ref[...].reshape(parts * unit, -1)
        grads = dot(packed, spread_ref[...]).astype(BF)
        product = packed.astype(F32) * attended_ref[...].reshape(parts * unit, -1).astype(F32)
        high = product.astype(BF)
        low = (product - high.astype(F32)).astype(BF)
        offsets = dot_general(mark_ref[...], high, (1, 1)) + dot_general(mark_ref[...], low, (1, 1))
        into = (parts, 1, unit, LANES)
        for h in range(heads):
            at = slice(h * LANES, (h + 1) * LANES)
            grad, query = grads[:, at], head(0, h, u)
            norm, offset = norm_ref[0, h : h + 1, :], offsets[h : h + 1]
            query_grad = 0.0
            for j in range(span):
                key, value = head(1, h, first + j), head(2, h, first + j)
                chance = jnp.exp2(dot_general(key, query, (1, 1)) * base - norm)
                chance_grad = dot_general(value, grad, (1, 1))
                score_grad = (chance * (chance_grad - offset)).astype(BF)
                block = pl.ds(first + j, 1)
                dv[:, block, :, at] += dot(chance.astype(BF), grad).reshape(into)
                dk[:, block, :, at] += dot(score_grad, query).reshape(into)
                query_grad = query_grad + dot(keys_across[first + j, h], score_grad)
            dq[:, pl.ds(u, 1), :, at] = jnp.transpose(query_grad * scale).astype(BF).reshape(into)

    pl.when(length_ref[u] == 1)(lambda: work(1))
    pl.when(length_ref[u] != 1)(lambda: work(RATIO))

    @pl.when(u == units - 1)
    def _():
        def pack(i, carry):
            at = pl.ds(i, 1)
            rows = [dq[:, at], (dk[:, at] * scale).astype(BF), dv[:, at].astype(BF)]
            rows = [row.reshape(parts * unit, -1) for row in rows]
            packed = dot(jnp.concatenate(rows, axis=1), pick_ref[...]).astype(BF)
            out_ref[:, at] = packed.reshape(parts, 1, unit, -1)
            return carry

        lax.fori_loop(0, units, pack, 0)


def whole_lanes(width):
    return -(-width // LANES) * LANES


def picker(heads, head_dim, dtype, width=None):
    row = jnp.arange(heads * LANES)[:, None]
    col = jnp.arange(heads * head_dim if width is None else width)[None, :]
    return ((row // LANES == col // head_dim) & (row % LANES == col % head_dim)).astype(dtype)


def attend_forward(start, length, qkv, heads, head_dim):
    parts, units, unit, lanes = qkv.shape
    width = heads * head_dim
    whole = lambda *shape: pl.BlockSpec(shape, lambda u, *_: (0,) * len(shape))
    return pl.pallas_call(
        partial(attend_forward_kernel, heads, 1.0 / math.sqrt(head_dim)),
        grid_spec=pltpu.PrefetchScalarGridSpec(
            num_scalar_prefetch=2,
            grid=(units,),
            in_specs=[whole(parts, units, unit, lanes), whole(heads * LANES, width)],
            out_specs=[
                pl.BlockSpec((parts, 1, unit, width), lambda u, *_: (0, u, 0, 0)),
                pl.BlockSpec((1, 8, parts * unit), lambda u, *_: (u, 0, 0)),
            ],
        ),
        out_shape=[
            jax.ShapeDtypeStruct((parts, units, unit, width), BF),
            jax.ShapeDtypeStruct((units, 8, parts * unit), F32),
        ],
        compiler_params=pltpu.CompilerParams(vmem_limit_bytes=48 * 2**20),
        cost_estimate=pl.CostEstimate(flops=10 * 2**30, bytes_accessed=16 * 2**20, transcendentals=2**23),
        name="attend_forward",
    )(start, length, qkv, picker(heads, head_dim, BF))


def attend_backward(start, length, qkv, norms, attended, grad, heads, head_dim):
    parts, units, unit, lanes = qkv.shape
    width = heads * head_dim
    whole = lambda *shape: pl.BlockSpec(shape, lambda u, *_: (0,) * len(shape))
    one_unit = pl.BlockSpec((parts, 1, unit, width), lambda u, *_: (0, u, 0, 0))
    pick = picker(heads, head_dim, BF)
    mark = (jnp.arange(8)[:, None] == jnp.arange(width)[None, :] // head_dim).astype(BF)
    return pl.pallas_call(
        partial(attend_backward_kernel, heads, 1.0 / math.sqrt(head_dim)),
        grid_spec=pltpu.PrefetchScalarGridSpec(
            num_scalar_prefetch=2,
            grid=(units,),
            in_specs=[
                whole(parts, units, unit, lanes),
                pl.BlockSpec((1, 8, parts * unit), lambda u, *_: (u, 0, 0)),
                one_unit,
                one_unit,
                whole(width, heads * LANES),
                whole(8, width),
                whole(3 * heads * LANES, whole_lanes(3 * width)),
            ],
            out_specs=whole(parts, units, unit, whole_lanes(3 * width)),
            scratch_shapes=[
                pltpu.VMEM((parts, units, unit, heads * LANES), BF),
                pltpu.VMEM((parts, units, unit, heads * LANES), F32),
                pltpu.VMEM((parts, units, unit, heads * LANES), F32),
                pltpu.VMEM((units, heads, LANES, parts * unit), BF),
            ],
        ),
        out_shape=jax.ShapeDtypeStruct((parts, units, unit, whole_lanes(3 * width)), BF),
        compiler_params=pltpu.CompilerParams(vmem_limit_bytes=56 * 2**20),
        cost_estimate=pl.CostEstimate(flops=2**20, bytes_accessed=2**20, transcendentals=0),
        name="attend_backward",
    )(start, length, qkv, norms, attended, grad, pick.T, mark, picker(3 * heads, head_dim, BF, whole_lanes(3 * width)))


MESH = pl.DeviceIdType.MESH


def add_into(ref, at, other):
    ref[at] = (ref[at].astype(F32) + other.astype(F32)).astype(BF)


def cut_rows(rows, k):
    up = (rows // 2 + 15) // 16 * 16
    return up if k % 2 == 0 else rows - up


def reduce_kernel(chunks, tensors, ready, ring, *refs):
    grads, slots, refs = refs[:tensors], refs[tensors], refs[tensors + 1 :]
    outs, slots_out, scratch = refs[:tensors], refs[tensors], list(refs[tensors + 1 :])
    own, local_sem, send_sem, recv_sem, credit, gathered_parts, slots_line, slots_send, slots_recv = scratch[:9]
    rings = scratch[9:]
    place, z = lax.axis_index("img"), lax.axis_index("blk")
    y, x, c = lax.div(place, 4), lax.rem(lax.div(place, 2), 2), lax.rem(place, 2)
    pair, beside, across = place + 1 - 2 * c, place + 2 - 4 * x, place + 4 - 8 * y
    near, far = z + 1 - 2 * lax.rem(z, 2), 3 - z
    inside = (z == 1) | (z == 2)
    outside = (z == 0) | (z == 3)

    barrier = pltpu.get_barrier_semaphore()
    for step in (1, 2, 3):
        pl.semaphore_signal(barrier, inc=1, device_id={"blk": lax.rem(z + step, 4)}, device_id_type=MESH)
    others = [lax.rem(place + step, 8) for step in range(1, 8)]
    for other in others:
        pl.semaphore_signal(barrier, inc=1, device_id={"img": other}, device_id_type=MESH)
    pl.semaphore_wait(barrier, 10)

    def send(k, which, source, target, where):
        return pltpu.make_async_remote_copy(
            src_ref=source,
            dst_ref=target,
            send_sem=send_sem.at[k, which],
            recv_sem=recv_sem.at[k, which],
            device_id=where,
            device_id_type=MESH,
        )

    def parts_of(k):
        t, row, rows, col, cols, gather = chunks[k]
        return grads[t], outs[t], row, rows, col, cols, gather

    def cut(k):
        return cut_rows(chunks[k][2], k)

    def is_ready(k):
        return chunks[k][0] in ready

    def slot(k):
        _, _, rows, _, cols, _ = chunks[k]
        first = cut(k)
        i = k % ring
        wide = pl.ds(0, cols)
        acc, rx, ry, rx2, ry2, from_near, from_far, total = rings
        return (
            acc.at[i, :, :, pl.ds(0, rows), wide],
            rx.at[i, :, pl.ds(0, first), wide],
            ry.at[i, :, pl.ds(0, rows - first), wide],
            rx2.at[i, pl.ds(0, rows - first), wide],
            ry2.at[i, pl.ds(0, first), wide],
            from_near.at[i, pl.ds(0, rows), wide],
            from_far.at[i, :, pl.ds(0, rows), wide],
            total.at[i, pl.ds(0, rows), wide],
        )

    copies = {}

    def begin(k, which, source, target, where):
        copies[k, which] = send(k, which, source, target, where)
        copies[k, which].start()

    def load(k):
        grad, _, row, rows, col, cols, _ = parts_of(k)
        return pltpu.make_async_copy(
            grad.at[:, :, c, pl.ds(row, rows), pl.ds(col, cols)],
            own.at[summed.index(k) % 2, :, :, pl.ds(0, rows), pl.ds(0, cols)],
            local_sem.at[summed.index(k) % 2],
        )

    count = len(chunks)

    def stage_zero(k):
        grad, _, row, rows, col, cols, _ = parts_of(k)
        if k >= ring:
            pl.semaphore_wait(credit.at[k % ring], 5)
        if is_ready(k):
            return
        begin(k, 0, grad.at[:, :, 1 - c, pl.ds(row, rows), pl.ds(col, cols)], slot(k)[0], {"img": pair})

    for k in range(min(ring, count)):
        stage_zero(k)
    summed = [k for k in range(count) if not is_ready(k)]
    for k in summed[:2]:
        load(k).start()

    wide_chunks = [k for k in range(count) if chunks[k][5]]

    def wide_total(k):
        _, _, rows, _, cols, _ = chunks[k]
        return gathered_parts.at[wide_chunks.index(k), :, pl.ds(0, rows), pl.ds(0, cols)]

    def stage_one(k):
        _, _, _, rows, _, cols, _ = parts_of(k)
        if is_ready(k):
            return
        acc, rx, ry = slot(k)[:3]
        load(k).wait()
        copies[k, 0].wait_recv()
        for i in range(2):
            for j in range(2):
                add_into(acc, (i, j), own[summed.index(k) % 2, i, j, :rows, :cols])
        for later in summed[summed.index(k) + 2 : summed.index(k) + 3]:
            load(later).start()
        first = cut(k)
        begin(k, 1, acc.at[:, 1 - x, pl.ds(0, first)], rx, {"img": beside})
        begin(k, 2, acc.at[1 - y, :, pl.ds(first, rows - first)], ry, {"img": across})

    def stage_two(k):
        if is_ready(k):
            return
        rows = chunks[k][2]
        acc, rx, ry, rx2, ry2 = slot(k)[:5]
        first = cut(k)
        copies[k, 1].wait_recv()
        copies[k, 2].wait_recv()
        copies[k, 1].wait_send()
        copies[k, 2].wait_send()
        for i in range(2):
            add_into(acc, (i, x, slice(0, first)), rx[i])
            add_into(acc, (y, i, slice(first, rows)), ry[i])
        begin(k, 3, acc.at[y, 1 - x, pl.ds(first, rows - first)], rx2, {"img": beside})
        begin(k, 4, acc.at[1 - y, x, pl.ds(0, first)], ry2, {"img": across})

    def stage_three(k):
        _, out, row, rows, col, cols, gather = parts_of(k)
        acc, _, _, rx2, ry2, from_near, from_far, total = slot(k)
        if gather:
            total = wide_total(k)
        if is_ready(k):
            from_far[0] = grads[chunks[k][0]][row : row + rows, col : col + cols]
            copies[k, 5] = send(k, 5, from_far.at[0], from_near, {"blk": near})
            pl.when(outside)(copies[k, 5].start)
            return
        first = cut(k)
        copies[k, 3].wait_recv()
        copies[k, 4].wait_recv()
        low = (acc[y, x, 0:first].astype(F32) + ry2[...].astype(F32)).astype(BF)
        high = (acc[y, x, first:rows].astype(F32) + rx2[...].astype(F32)).astype(BF)
        if gather:
            total[z, 0:first] = low
            total[z, first:rows] = high
            for step in (1, 2, 3):
                begin(k, 4 + step, total.at[z], total.at[z], {"blk": lax.rem(z + step, 4)})
            return
        from_far[0, 0:first] = low
        from_far[0, first:rows] = high
        copies[k, 5] = send(k, 5, from_far.at[0], from_near, {"blk": near})
        pl.when(outside)(copies[k, 5].start)

    def stage_four(k):
        if chunks[k][5]:
            return
        from_near, from_far, total = slot(k)[5:]
        copies[k, 6] = send(k, 6, from_far.at[0], from_far.at[1], {"blk": far})

        @pl.when(inside)
        def _():
            copies[k, 5].wait_recv()
            add_into(from_far, 0, from_near[...])
            copies[k, 6].start()

    def stage_five(k):
        if chunks[k][5]:
            return
        from_near, from_far, total = slot(k)[5:]
        copies[k, 7] = send(k, 7, total, total, {"blk": near})

        @pl.when(inside)
        def _():
            copies[k, 6].wait_recv()
            total[...] = (from_far[0].astype(F32) + from_far[1].astype(F32)).astype(BF)
            copies[k, 7].start()

    def stage_six(k):
        _, out, row, rows, col, cols, gather = parts_of(k)
        total = wide_total(k) if gather else slot(k)[7]
        if gather:
            for step in (1, 2, 3):
                copies[k, 4 + step].wait()
            out[:, row : row + rows, col : col + cols] = total[...]
        else:
            pl.when(outside)(copies[k, 7].wait_recv)
            out[row : row + rows, col : col + cols] = total[...]
            pl.when(outside)(copies[k, 5].wait_send)
            pl.when(inside)(copies[k, 6].wait_send)
            pl.when(inside)(copies[k, 7].wait_send)
        for which in () if is_ready(k) else (0, 3, 4):
            copies[k, which].wait_send()
        if k + ring < count:
            for other in (pair, beside, across):
                pl.semaphore_signal(credit.at[k % ring], inc=1, device_id={"img": other}, device_id_type=MESH)
            for other in (near, far):
                pl.semaphore_signal(credit.at[k % ring], inc=1, device_id={"blk": other}, device_id_type=MESH)

    def slots_copy(which, source, target, where):
        return pltpu.make_async_remote_copy(
            src_ref=source,
            dst_ref=target,
            send_sem=slots_send.at[which],
            recv_sem=slots_recv.at[which],
            device_id=where,
            device_id_type=MESH,
        )

    slots_near = slots_copy(0, slots, slots_line.at[0], {"blk": near})
    slots_far = slots_copy(8, slots_line.at[1], slots_line.at[2], {"blk": far})
    slots_back = slots_copy(9, slots_out.at[place], slots_out.at[place], {"blk": near})
    slots_round = [
        slots_copy(1 + i, slots_out.at[place], slots_out.at[place], {"img": other}) for i, other in enumerate(others)
    ]

    def slots_one():
        pl.when(outside)(slots_near.start)

    def slots_two():
        @pl.when(inside)
        def _():
            slots_near.wait_recv()
            slots_line[1] = slots_line[0] + slots[...]
            slots_far.start()

    def slots_three():
        @pl.when(inside)
        def _():
            slots_far.wait_recv()
            slots_out[place] = slots_line[1] + slots_line[2]
            slots_back.start()

    def slots_four():
        pl.when(outside)(slots_back.wait_recv)
        for copy in slots_round:
            copy.start()

    def slots_five():
        for copy in slots_round:
            copy.wait()
        pl.when(outside)(slots_near.wait_send)
        pl.when(inside)(slots_far.wait_send)
        pl.when(inside)(slots_back.wait_send)

    slots_stages = {0: slots_one, 2: slots_two, 4: slots_three, 6: slots_four, 9: slots_five}
    stages = ((stage_one, 0), (stage_two, 2), (stage_three, 4), (stage_four, 5), (stage_five, 6), (stage_six, 7))
    for step in range(max(count + 7, 10)):
        for stage, behind in stages:
            if 0 <= step - behind < count:
                stage(step - behind)
        if step - 8 >= 0 and step - 8 + ring < count:
            stage_zero(step - 8 + ring)
        if step in slots_stages:
            slots_stages[step]()


def reduce_call(grads, ready, gathered, slots, width, collective_id):
    chunks, shapes = [], []
    for t, grad in enumerate(grads):
        rows, cols = grad.shape[0] // (1 if t in ready else 8), grad.shape[1]
        depth = 144 if rows % 144 == 0 or t in ready else 128
        for row in range(0, rows, depth):
            for col in range(0, cols, width):
                chunks.append((t, row, min(depth, rows - row), col, min(width, cols - col), t == gathered))
        shapes.append(jax.ShapeDtypeStruct((4, rows, cols) if t == gathered else (rows, cols), BF))
    shapes.append(jax.ShapeDtypeStruct((8, *slots.shape), F32))
    n, ring = len(chunks), 12
    deep = max(rows for _, _, rows, _, _, _ in chunks)
    half = (deep // 2 + 15) // 16 * 16
    dma = pltpu.SemaphoreType.DMA
    scratch = [
        pltpu.VMEM((2, 2, 2, deep, width), BF),
        dma((2,)),
        dma((n, 8)),
        dma((n, 8)),
        pltpu.SemaphoreType.REGULAR((ring,)),
        pltpu.VMEM((max(1, sum(g for *_, g in chunks)), 4, deep, width), BF),
        pltpu.VMEM((3, *slots.shape), F32),
        dma((10,)),
        dma((10,)),
    ]
    for shape in (
        (2, 2, deep, width),
        (2, half, width),
        (2, half, width),
        (half, width),
        (half, width),
        (deep, width),
        (2, deep, width),
        (deep, width),
    ):
        scratch.append(pltpu.VMEM((ring, *shape), BF))
    vmem, anywhere = pl.BlockSpec(memory_space=pltpu.VMEM), pl.BlockSpec(memory_space=pl.ANY)
    return pl.pallas_call(
        partial(reduce_kernel, chunks, len(grads), ready, ring),
        out_shape=shapes,
        in_specs=[vmem if t in ready else anywhere for t in range(len(grads))] + [vmem],
        out_specs=[vmem] * (len(grads) + 1),
        scratch_shapes=scratch,
        compiler_params=pltpu.CompilerParams(
            collective_id=collective_id, has_side_effects=True, vmem_limit_bytes=56 * 2**20
        ),
        cost_estimate=pl.CostEstimate(flops=0, bytes_accessed=500 * 2**20, transcendentals=0),
        name=f"reduce_{collective_id}",
    )(
        *(g if t in ready else g.reshape(2, 2, 2, g.shape[0] // 8, g.shape[1]) for t, g in enumerate(grads)),
        slots,
    )


def gather_kernel(chunks, tensors, early, hot_ref, x_ref, share_ref, bias_ref, start_ref, *refs):
    shards, refs = refs[:tensors], refs[tensors:]
    fulls, refs = refs[:tensors], refs[tensors:]
    rows_ref, modulation_ref, bias_out = refs[:3]
    share_got, own_sem, first_send, first_recv, rest_send, rest_recv, bias_send, bias_recv = refs[3:11]
    send_sem, recv_sem, line_send, line_recv, spread_send, spread_recv = refs[11:]
    place, z = lax.axis_index("img"), lax.axis_index("blk")
    y, x, c = lax.div(place, 4), lax.rem(lax.div(place, 2), 2), lax.rem(place, 2)
    step_x, step_y = 2 - 4 * x, 4 - 8 * y
    pair, beside, across = place + 1 - 2 * c, place + step_x, place + step_y
    diagonal = place + step_x + step_y
    devices = share_got.shape[0]
    units, slots = hot_ref.shape
    unit = x_ref.shape[0] // units
    wide = x_ref.shape[1]

    barrier = pltpu.get_barrier_semaphore()
    for step in range(1, devices):
        pl.semaphore_signal(barrier, inc=1, device_id={"img": lax.rem(place + step, devices)}, device_id_type=MESH)
    for step in (1, 2, 3):
        pl.semaphore_signal(barrier, inc=1, device_id={"blk": lax.rem(z + step, 4)}, device_id_type=MESH)
    pl.semaphore_wait(barrier, devices + 2)

    def remote(source, target, send, recv, where):
        return pltpu.make_async_remote_copy(
            src_ref=source,
            dst_ref=target,
            send_sem=send,
            recv_sem=recv,
            device_id=where,
            device_id_type=MESH,
        )

    part = (share_ref.shape[2] - early) // 4
    part_at = pl.multiple_of(early + z * part, LANES)
    first, rest, biases = [], [], []
    for step in range(1, devices):
        to = lax.rem(place + step, devices)
        for copies, lo, size, send, recv in (
            (first, 0, early, first_send, first_recv),
            (rest, part_at, part, rest_send, rest_recv),
        ):
            copies.append(
                remote(
                    share_ref.at[to, :, pl.ds(lo, size)],
                    share_got.at[place, :, pl.ds(lo, size)],
                    send.at[step],
                    recv.at[step],
                    {"img": to},
                )
            )
        biases.append(remote(bias_ref, bias_out.at[place], bias_send.at[step], bias_recv.at[step], {"img": to}))
    for copy in first:
        copy.start()

    copies = {}

    def begin(k, which, block, rows, where):
        t, row, count = chunks[k]
        at = (block, pl.ds(row + rows[0], rows[1]))
        copies[k, which] = remote(
            fulls[t].at[at], fulls[t].at[at], send_sem.at[k, which], recv_sem.at[k, which], where
        )
        copies[k, which].start()

    def begin_own(k, which, where):
        t, row, count = chunks[k]
        source = shards[t].at[pl.ds(row, count)]
        copies[k, which] = remote(
            source, fulls[t].at[place, pl.ds(row, count)], send_sem.at[k, which], recv_sem.at[k, which], where
        )
        copies[k, which].start()

    own = [pltpu.make_async_copy(shards[t], fulls[t].at[place], own_sem.at[t]) for t in range(tensors)]
    def ahead(k):
        if k < len(chunks):
            begin_own(k, 0, {"img": beside})
            begin_own(k, 1, {"img": across})
            begin_own(k, 2, {"img": pair})

    ahead(0)
    for copy in rest + biases:
        copy.start()
    for k in range(1, 3):
        ahead(k)
    for copy in own:
        copy.start()

    share_got[place] = share_ref[place]
    bias_out[place] = bias_ref[...]
    for copy in first:
        copy.wait()

    def modulation_of(lo, size):
        at = pl.ds(lo, size)
        total = share_got[0, :, at]
        for i in range(1, devices):
            total = total + share_got[i, :, at]
        modulation_ref[:, at] = start_ref[:, at] + total

    modulation_of(0, early)
    for u in range(units):
        chosen = hot_ref[u : u + 1, 0:1] * modulation_ref[0:1, 0:early]
        for s in range(1, slots):
            chosen = chosen + hot_ref[u : u + 1, s : s + 1] * modulation_ref[s : s + 1, 0:early]
        at = pl.ds(u * unit, unit)
        values = x_ref[at, :].astype(F32)
        centered = values - jnp.mean(values, axis=1, keepdims=True)
        inverse = lax.rsqrt(jnp.mean(centered * centered, axis=1, keepdims=True) + EPSILON)
        rows_ref[z, at, :] = (centered * inverse * (1.0 + chosen[:, wide:]) + chosen[:, :wide]).astype(BF)

    up = [
        remote(block, block, line_send.at[0, s], line_recv.at[0, s], {"blk": lax.rem(z + 1, 4)})
        for s, block in ((s, rows_ref.at[lax.rem(z - s + 4, 4)]) for s in range(3))
    ]
    down = [
        remote(block, block, line_send.at[1, s], line_recv.at[1, s], {"blk": lax.rem(z + 3, 4)})
        for s, block in ((s, rows_ref.at[lax.rem(z + s, 4)]) for s in range(3))
    ]

    def line_step(s):
        if s > 0:
            pl.when(z >= s)(up[s - 1].wait_recv)
            pl.when(z + s < 4)(down[s - 1].wait_recv)
        if s < 3:
            pl.when((z >= s) & (z < 3))(up[s].start)
            pl.when((z + s < 4) & (z > 0))(down[s].start)

    def cut(k):
        return cut_rows(chunks[k][2], k)

    def relay(k):
        count, half = chunks[k][2], cut(k)
        copies[k, 0].wait_recv()
        begin(k, 3, beside, (0, half), {"img": across})
        begin(k, 5, beside, (0, count), {"img": pair})
        copies[k, 1].wait_recv()
        begin(k, 4, across, (half, count - half), {"img": beside})
        begin(k, 6, across, (0, count), {"img": pair})

    def last(k):
        count, half = chunks[k][2], cut(k)
        copies[k, 3].wait_recv()
        begin(k, 7, diagonal, (0, half), {"img": pair})
        copies[k, 4].wait_recv()
        begin(k, 8, diagonal, (half, count - half), {"img": pair})

    line_step(0)
    for copy in rest:
        copy.wait()
    modulation_of(part_at, part)
    own_part = modulation_ref.at[:, pl.ds(part_at, part)]
    spread = [
        remote(own_part, own_part, spread_send.at[step], spread_recv.at[step], {"blk": lax.rem(z + step, 4)})
        for step in (1, 2, 3)
    ]
    for copy in spread:
        copy.start()
    n = len(chunks)
    for k in range(n + 2):
        if k < n:
            relay(k)
            ahead(k + 3)
        if k >= 2:
            last(k - 2)
        for s in (1, 2):
            if k == 2 * s - 1:
                line_step(s)
    for copy in biases:
        copy.wait()
    line_step(3)
    for copy in spread:
        copy.wait()
    for copy in own:
        copy.wait()
    for k in range(n):
        for which in (0, 1, 3, 4):
            copies[k, which].wait_send()
        copies[k, 2].wait()
        for which in (5, 6, 7, 8):
            copies[k, which].wait()
    for s in range(3):
        pl.when((z >= s) & (z < 3))(up[s].wait_send)
        pl.when((z + s < 4) & (z > 0))(down[s].wait_send)


def gather_call(shards, unit_hot, rows, shares, bias_row, modulate_bias, collective_id):
    devices = shares.shape[0]
    slots, wide = shares.shape[1:]
    chunks = []
    for t, shard in enumerate(shards):
        depth = shard.shape[0]
        for row in range(0, depth, 144):
            chunks.append((t, row, min(144, depth - row)))
    n = len(chunks)
    vmem, anywhere = pl.BlockSpec(memory_space=pltpu.VMEM), pl.BlockSpec(memory_space=pl.ANY)
    dma = pltpu.SemaphoreType.DMA
    first_modulation = jnp.broadcast_to(modulate_bias.astype(F32)[None, :], (slots, wide))
    return pl.pallas_call(
        partial(gather_kernel, chunks, len(shards), 2 * rows.shape[1]),
        out_shape=[jax.ShapeDtypeStruct((devices, *s.shape), BF) for s in shards]
        + [
            jax.ShapeDtypeStruct((4, *rows.shape), BF),
            jax.ShapeDtypeStruct((slots, wide), F32),
            jax.ShapeDtypeStruct((devices, *bias_row.shape), F32),
        ],
        in_specs=[vmem] * 5 + [anywhere] * len(shards),
        out_specs=[anywhere] * len(shards) + [vmem] * 3,
        scratch_shapes=[
            pltpu.VMEM((devices, slots, wide), F32),
            dma((len(shards),)),
            dma((devices,)),
            dma((devices,)),
            dma((devices,)),
            dma((devices,)),
            dma((devices,)),
            dma((devices,)),
            dma((n, 9)),
            dma((n, 9)),
            dma((2, 3)),
            dma((2, 3)),
            dma((4,)),
            dma((4,)),
        ],
        compiler_params=pltpu.CompilerParams(
            collective_id=collective_id, has_side_effects=True, vmem_limit_bytes=48 * 2**20
        ),
        cost_estimate=pl.CostEstimate(flops=0, bytes_accessed=450 * 2**20, transcendentals=0),
        name=f"gather_{collective_id}",
    )(unit_hot, rows, shares, bias_row, first_modulation, *shards)


def assemble_kernel(mine, parts_ref, out_ref):
    pieces = [
        parts_ref[part, :, which * mine : (which + 1) * mine].astype(F32)
        for which in range(3)
        for part in range(parts_ref.shape[0])
    ]
    out_ref[...] = jnp.concatenate(pieces, axis=1)


def assemble(parts, mine):
    return pl.pallas_call(
        partial(assemble_kernel, mine),
        out_shape=jax.ShapeDtypeStruct((parts.shape[1], 3 * mine * parts.shape[0]), F32),
        compiler_params=pltpu.CompilerParams(vmem_limit_bytes=32 * 2**20),
        name="assemble",
    )(parts)


def total_kernel(mine_ref, out_ref, lines, line_send, line_recv, send_sem, recv_sem):
    place, z = lax.axis_index("img"), lax.axis_index("blk")
    parts, devices = lines.shape[0], out_ref.shape[0]
    barrier = pltpu.get_barrier_semaphore()
    for step in range(1, parts):
        pl.semaphore_signal(barrier, inc=1, device_id={"blk": lax.rem(z + step, parts)}, device_id_type=MESH)
    for step in range(1, devices):
        pl.semaphore_signal(barrier, inc=1, device_id={"img": lax.rem(place + step, devices)}, device_id_type=MESH)
    pl.semaphore_wait(barrier, parts + devices - 2)

    lines[z] = mine_ref[...]
    copies = [
        pltpu.make_async_remote_copy(
            src_ref=lines.at[z],
            dst_ref=lines.at[z],
            send_sem=line_send.at[step],
            recv_sem=line_recv.at[step],
            device_id={"blk": lax.rem(z + step, parts)},
            device_id_type=MESH,
        )
        for step in range(1, parts)
    ]
    for copy in copies:
        copy.start()
    for copy in copies:
        copy.wait()
    total = lines[0]
    for step in range(1, parts):
        total = total + lines[step]
    out_ref[place] = total
    copies = [
        pltpu.make_async_remote_copy(
            src_ref=out_ref.at[place],
            dst_ref=out_ref.at[place],
            send_sem=send_sem.at[step],
            recv_sem=recv_sem.at[step],
            device_id={"img": lax.rem(place + step, devices)},
            device_id_type=MESH,
        )
        for step in range(1, devices)
    ]
    for copy in copies:
        copy.start()
    for copy in copies:
        copy.wait()


def total_call(mine, devices, parts, collective_id):
    if (devices, parts) != (8, 4):
        return lax.all_gather(lax.psum(mine, "blk"), "img", axis=0, tiled=False)
    return pl.pallas_call(
        total_kernel,
        out_shape=jax.ShapeDtypeStruct((devices, *mine.shape), mine.dtype),
        in_specs=[pl.BlockSpec(memory_space=pltpu.VMEM)],
        out_specs=pl.BlockSpec(memory_space=pltpu.VMEM),
        scratch_shapes=[
            pltpu.VMEM((parts, *mine.shape), mine.dtype),
            pltpu.SemaphoreType.DMA((parts,)),
            pltpu.SemaphoreType.DMA((parts,)),
            pltpu.SemaphoreType.DMA((devices,)),
            pltpu.SemaphoreType.DMA((devices,)),
        ],
        compiler_params=pltpu.CompilerParams(
            collective_id=collective_id, has_side_effects=True, vmem_limit_bytes=32 * 2**20
        ),
        name=f"total_{collective_id}",
    )(mine)


def per_device(
    inputs,
    token_image,
    image_time,
    image_class,
    targets,
    cotangent,
    class_table,
    modulate_weight,
    modulate_bias,
    attend_weight,
    attend_bias,
    output_weight,
    output_bias,
    expand_weight,
    expand_bias,
    shrink_weight,
    shrink_bias,
    inner_weight,
    inner_bias,
    middle_weight,
    middle_bias,
    outer_weight,
    outer_bias,
):
    count, width = inputs.shape
    head_dim = width // HEADS
    columns = class_table.shape[1]
    devices, parts = lax.axis_size("img"), lax.axis_size("blk")
    place_img, place_blk = lax.axis_index("img"), lax.axis_index("blk")
    slots = image_class.shape[0] // devices
    unit = SHORT // parts
    units = count // unit
    heads = HEADS // parts
    mine = heads * head_dim
    half = width // 2

    class_hot = (image_class[:, None] == jnp.arange(class_table.shape[0])[None, :]).astype(BF)
    column = place_img * columns + jnp.arange(columns)
    frequency = jnp.exp(-math.log(10000.0) * (column % half).astype(F32) / half)
    angle = image_time.astype(F32)[:, None] * frequency[None, :]
    condition = dot(class_hot, class_table) + jnp.where(column[None, :] < half, jnp.cos(angle), jnp.sin(angle))
    silu_condition = jax.nn.silu(condition).astype(BF)
    shares = dot(silu_condition, modulate_weight)
    biases = (attend_bias, output_bias, expand_bias, shrink_bias, inner_bias, middle_bias, outer_bias)
    longest = whole_lanes(max(bias.shape[0] for bias in biases))
    bias_row = jnp.stack([jnp.pad(bias.astype(F32), (0, longest - bias.shape[0])) for bias in biases])
    bias_row = jnp.pad(bias_row, ((0, 8 - len(biases)), (0, 0)))
    shares = shares.reshape(devices, slots, -1)

    labels = token_image[::unit]
    same = labels[:, None] == labels[None, :]
    start = jnp.argmax(same, axis=1).astype(jnp.int32)
    length = jnp.sum(same, axis=1).astype(jnp.int32)
    unit_hot = (labels[:, None] == jnp.arange(slots)[None, :]).astype(F32)
    def by_unit(values):
        return values.reshape(units, unit, width)

    def by_row(values):
        return values.reshape(count, width)

    attend_mine = lax.dynamic_slice_in_dim(
        attend_weight.reshape(-1, 3, parts, mine), place_blk, 1, axis=2
    ).reshape(-1, 3 * mine)
    attend_mine = jnp.pad(attend_mine, ((0, 0), (0, whole_lanes(3 * mine) - 3 * mine)))

    def gather(shard):
        return lax.all_gather(shard, "img", axis=0, tiled=True)

    source = by_unit(inputs.astype(F32))
    normal_one, inverse_one = layer_norm(source)
    first_weights = (attend_mine, output_weight, expand_weight, outer_weight, shrink_weight)
    if (devices, parts) == (8, 4):
        *fulls, rows_group, modulation, got_bias = gather_call(
            first_weights, unit_hot, inputs, shares, bias_row, modulate_bias, 3
        )
        fulls = [full.reshape(-1, full.shape[2]) for full in fulls]
        modulated_group = rows_group.reshape(parts * count, width)
    else:
        fulls = [gather(shard) for shard in first_weights]
        modulation = modulate_bias.astype(F32)[None, :] + lax.psum_scatter(
            shares.reshape(devices * slots, -1), "img", scatter_dimension=0, tiled=True
        )
        got_bias = lax.all_gather(bias_row, "img", axis=0, tiled=False)
        chosen = jnp.dot(unit_hot, modulation, precision=HIGH)[:, None, : 2 * width]
        modulated_one = normal_one * (1.0 + chosen[:, :, width:]) + chosen[:, :, :width]
        modulated_group = lax.all_gather(by_row(modulated_one.astype(BF)), "blk", axis=0, tiled=True)
    attend_full, output_full, expand_full, outer_full, shrink_full = fulls
    inner_shard, middle_shard, modulated_group = lax.optimization_barrier(
        (inner_weight, middle_weight, modulated_group)
    )
    inner_full, middle_full = gather(inner_shard), gather(middle_shard)
    full_biases = [got_bias[:, i, : bias.shape[0]].reshape(-1) for i, bias in enumerate(biases)]
    (
        attend_bias_full,
        output_bias_full,
        expand_bias_full,
        shrink_bias_full,
        inner_bias_full,
        middle_bias_full,
        outer_bias_full,
    ) = full_biases
    unit_modulation = jnp.dot(unit_hot, modulation, precision=HIGH)
    shift_one, scale_one, gate_one, shift_two, scale_two, gate_two = (
        block[:, None, :] for block in jnp.split(unit_modulation, 6, axis=1)
    )

    def pad_heads(values):
        lead = values.shape[:-1]
        values = values.reshape(*lead, 3 * heads, head_dim)
        values = jnp.pad(values, ((0, 0),) * len(lead) + ((0, 0), (0, LANES - head_dim)))
        return values.reshape(*lead, 3 * heads * LANES)

    bias_mine = lax.dynamic_slice_in_dim(attend_bias_full.reshape(2, parts, mine), place_blk, 1, axis=1)
    bias_mine = jnp.concatenate([bias_mine[0, 0], jnp.zeros((mine,), F32), bias_mine[1, 0]])
    is_value = jnp.arange(3 * heads * LANES) >= 2 * heads * LANES
    is_last = jnp.arange(3 * heads * LANES) % LANES == LANES - 1
    padded_bias = jnp.where(is_value & is_last, 1.0, pad_heads(bias_mine))
    projected = dot(modulated_group, pad_heads(attend_full[:, : 3 * mine])) + padded_bias[None, :]
    qkv = projected.astype(BF).reshape(parts, units, unit, 3 * heads * LANES)
    attended_heads, norms = attend_forward(start, length, qkv, heads, head_dim)
    attended = lax.all_to_all(
        attended_heads.reshape(parts, count, mine), "blk", split_axis=0, concat_axis=0, tiled=True
    )
    output_heads = output_full.reshape(parts, mine, width)
    branch_one = by_unit(
        jnp.einsum("pti,pio->to", attended, output_heads, preferred_element_type=F32) + output_bias_full
    )
    middle = source + gate_one * branch_one
    normal_two, inverse_two = layer_norm(middle)
    modulated_two = by_row((normal_two * (1.0 + scale_two) + shift_two).astype(BF))
    expanded = dot(modulated_two, expand_full) + expand_bias_full
    gelu_tanh = partial(jax.nn.gelu, approximate=True)
    activated = gelu_tanh(expanded).astype(BF)
    branch_two = by_unit(dot(activated, shrink_full) + shrink_bias_full)
    whole = middle + gate_two * branch_two
    whole_low = by_row(whole.astype(BF))
    pre_one = dot(whole_low, inner_full) + inner_bias_full
    first = jax.nn.silu(pre_one).astype(BF)
    pre_two = dot(first, middle_full) + middle_bias_full
    second = jax.nn.silu(pre_two).astype(BF)
    aligned = dot(second, outer_full) + outer_bias_full
    target = targets.astype(F32)
    cross = jnp.sum(aligned * target, axis=1)
    aligned_inverse = lax.rsqrt(jnp.sum(aligned * aligned, axis=1) + EPSILON)
    target_inverse = lax.rsqrt(jnp.sum(target * target, axis=1) + EPSILON)
    cosine = cross * aligned_inverse * target_inverse
    grad_aligned = (
        -0.5
        * (
            target * (aligned_inverse * target_inverse)[:, None]
            - (cosine * aligned_inverse * aligned_inverse)[:, None] * aligned
        )
    ).astype(BF)

    def scatter(values):
        return lax.psum_scatter(values, "img", scatter_dimension=0, tiled=True)

    grad_outer = left_product(second, grad_aligned)
    grad_outer_bias = column_sum(grad_aligned)
    grad_pre_two = local_back(jax.nn.silu, pre_two, right_product(grad_aligned, outer_full)).astype(BF)
    grad_middle_weight = left_product(first, grad_pre_two)
    grad_middle_bias = column_sum(grad_pre_two)
    grad_pre_one = local_back(jax.nn.silu, pre_one, right_product(grad_pre_two, middle_full)).astype(BF)
    grad_inner = left_product(whole_low, grad_pre_one)
    grad_inner_bias = column_sum(grad_pre_one)
    early_weights = jnp.concatenate(
        [g.reshape(devices, -1, g.shape[1]) for g in (grad_inner, grad_middle_weight)], axis=1
    )
    early_part = scatter(early_weights.reshape(-1, early_weights.shape[2]))
    grad_whole = by_unit(cotangent.astype(F32)) + by_unit(right_product(grad_pre_one, inner_full))
    grad_gate_two = grad_whole * branch_two
    grad_branch_two = by_row((grad_whole * gate_two).astype(BF))
    grad_shrink = left_product(activated, grad_branch_two)
    grad_shrink_bias = column_sum(grad_branch_two)
    grad_expanded = local_back(gelu_tanh, expanded, right_product(grad_branch_two, shrink_full)).astype(BF)
    grad_expand = left_product(modulated_two, grad_expanded)
    grad_expand_bias = column_sum(grad_expanded)
    grad_mod_two = by_unit(right_product(grad_expanded, expand_full))
    grad_scale_two = grad_mod_two * normal_two
    grad_middle = grad_whole + norm_back(grad_mod_two * (1.0 + scale_two), normal_two, inverse_two)
    grad_gate_one = grad_middle * branch_one
    grad_branch_one = by_row((grad_middle * gate_one).astype(BF))
    grad_output = jnp.einsum("pti,to->pio", attended, grad_branch_one, preferred_element_type=F32)
    grad_output = grad_output.astype(BF).reshape(width, width)
    grad_output_bias = column_sum(grad_branch_one)
    def slot_sum(*values):
        rows = jnp.concatenate([jnp.sum(v, axis=1) for v in values], axis=1)
        return jnp.dot(unit_hot.T, rows, precision=HIGH)

    early_slots = slot_sum(grad_gate_one, grad_mod_two, grad_scale_two, grad_gate_two)
    grad_attended = jnp.einsum("to,pio->pti", grad_branch_one, output_heads, preferred_element_type=F32)
    grad_heads = lax.all_to_all(grad_attended.astype(BF), "blk", split_axis=0, concat_axis=0, tiled=True)
    grad_heads, grad_shrink, grad_expand = lax.optimization_barrier((grad_heads, grad_shrink, grad_expand))
    grad_heads = grad_heads.reshape(parts, units, unit, mine)
    grad_qkv = attend_backward(start, length, qkv, norms, attended_heads, grad_heads, heads, head_dim).reshape(parts * count, -1)
    grad_tied, early_sum = lax.optimization_barrier((grad_qkv, lax.psum(early_part, "blk")))
    grad_attend = left_product(modulated_group, grad_tied)
    partial_mod_one = right_product(grad_qkv, attend_full).astype(BF)
    grads = (grad_outer, grad_attend, grad_output, grad_shrink, grad_expand)
    if (devices, parts) == (8, 4):
        *sums, early_grad = reduce_call(grads, (), 1, early_slots, 640, 1)
    else:
        sums = [scatter(grad) for grad in grads]
        attend_part = lax.all_gather(sums[1], "blk", axis=0, tiled=False)
        sums = list(lax.psum(tuple(sums[:1] + sums[2:]), "blk"))
        sums.insert(1, attend_part)
        early_grad = lax.all_gather(lax.psum(early_slots, "blk"), "img", axis=0, tiled=False)
    outer_sum, attend_parts, output_sum, shrink_sum, expand_sum = sums
    inner_sum, middle_sum = early_sum[: inner_weight.shape[0]], early_sum[inner_weight.shape[0] :]
    early_grad = early_grad.reshape(devices * slots, -1)
    attend_sum = assemble(attend_parts, mine)
    grad_mod_one = lax.psum_scatter(partial_mod_one, "blk", scatter_dimension=0, tiled=True)
    grad_mod_one, early_grad = lax.optimization_barrier((grad_mod_one, early_grad))
    grad_mod_one = by_unit(grad_mod_one.astype(F32))
    grad_scale_one = grad_mod_one * normal_one
    grad_source = grad_middle + norm_back(grad_mod_one * (1.0 + scale_one), normal_one, inverse_one)

    qkv_bias = column_sum(grad_qkv[:, : 3 * mine]).reshape(3, 1, mine)
    spread = (jnp.arange(parts) == place_blk).astype(F32)[None, :, None]
    attend_bias_rows = jnp.concatenate([qkv_bias[:1], qkv_bias[2:]]) * spread
    bias_grads = (
        attend_bias_rows,
        grad_output_bias,
        grad_expand_bias,
        grad_shrink_bias,
        grad_inner_bias,
        grad_middle_bias,
        grad_outer_bias,
    )
    bias_rows = jnp.concatenate([b.reshape(devices, -1) for b in bias_grads], axis=1)
    late_slots = slot_sum(grad_mod_one, grad_scale_one)
    late_rows = jnp.concatenate(
        [late_slots, jnp.pad(bias_rows, ((0, 0), (0, late_slots.shape[1] - bias_rows.shape[1])))], axis=0
    )
    late = total_call(late_rows, devices, parts, 2)
    late_grad = late[:, :slots].reshape(devices * slots, 2 * width)
    bias_sum = jnp.sum(lax.dynamic_index_in_dim(late, slots + place_img, axis=1, keepdims=False), axis=0)
    bias_sums = []
    at = 0
    for bias in biases:
        bias_sums.append(bias_sum[at : at + bias.shape[0]])
        at += bias.shape[0]
    (
        attend_bias_sum,
        output_bias_sum,
        expand_bias_sum,
        shrink_bias_sum,
        inner_bias_sum,
        middle_bias_sum,
        outer_bias_sum,
    ) = bias_sums
    modulation_grad = jnp.concatenate([late_grad, early_grad], axis=1)
    modulate_sum = jnp.dot(silu_condition.astype(F32).T, modulation_grad, precision=HIGH)
    modulate_bias_sum = jnp.sum(modulation_grad, axis=0)
    silu_grad = jnp.dot(modulation_grad, modulate_weight.astype(F32).T, precision=HIGH)
    condition_grad = local_back(jax.nn.silu, condition, silu_grad)
    table_sum = jnp.dot(class_hot.astype(F32).T, condition_grad, precision=HIGH)
    return (
        whole_low,
        by_row(grad_source.astype(BF)),
        table_sum,
        modulate_sum,
        modulate_bias_sum,
        attend_sum.astype(F32),
        attend_bias_sum,
        output_sum.astype(F32),
        output_bias_sum,
        expand_sum.astype(F32),
        expand_bias_sum,
        shrink_sum.astype(F32),
        shrink_bias_sum,
        inner_sum.astype(F32),
        inner_bias_sum,
        middle_sum.astype(F32),
        middle_bias_sum,
        outer_sum.astype(F32),
        outer_bias_sum,
    )


def solution(mesh):
    in_specs = (
        P(("img", "blk"), None),
        P(("img", "blk")),
        P(),
        P(),
        P(("img", "blk"), None),
        P(("img", "blk"), None),
        P(None, "img"),
        P("img", None),
        P(),
        P("img", None),
        P("img"),
        P("img", None),
        P("img"),
        P("img", None),
        P("img"),
        P("img", None),
        P("img"),
        P("img", None),
        P("img"),
        P("img", None),
        P("img"),
        P("img", None),
        P("img"),
    )
    out_specs = (
        P(("img", "blk"), None),
        P(("img", "blk"), None),
        P(None, "img"),
        P("img", None),
        P(),
        P("img", None),
        P("img"),
        P("img", None),
        P("img"),
        P("img", None),
        P("img"),
        P("img", None),
        P("img"),
        P("img", None),
        P("img"),
        P("img", None),
        P("img"),
        P("img", None),
        P("img"),
    )
    return jax.shard_map(
        per_device, mesh=mesh, in_specs=in_specs, out_specs=out_specs, check_vma=False
    )
```

```python
from functools import partial
import math

import jax
import jax.numpy as jnp
from jax import lax
from jax.experimental import pallas as pl
from jax.experimental.pallas import tpu as pltpu
from jax.sharding import PartitionSpec as P

HEADS = 16
SHORT = 256
RATIO = 4
LANES = 128

EPSILON = 1e-06
HIGH = lax.Precision.HIGHEST
BF = jnp.bfloat16
F32 = jnp.float32


def layer_norm(values):
    mean = jnp.mean(values, axis=-1, keepdims=True)
    centered = values - mean
    variance = jnp.mean(centered * centered, axis=-1, keepdims=True)
    inverse = lax.rsqrt(variance + EPSILON)
    return (centered * inverse, inverse)


def norm_back(grad, normal, inverse):
    mean_grad = jnp.mean(grad, axis=-1, keepdims=True)
    mean_cross = jnp.mean(grad * normal, axis=-1, keepdims=True)
    return inverse * (grad - mean_grad - normal * mean_cross)


def local_back(function, point, grad):
    return jax.vjp(function, point)[1](grad)[0]


def left_product(left, right):
    return jnp.einsum("ti,to->io", left, right, preferred_element_type=F32).astype(BF)


def right_product(grad, weight):
    return jnp.einsum("to,io->ti", grad, weight, preferred_element_type=F32)


def column_sum(values):
    return jnp.sum(values.astype(F32), axis=0)


def dot(left, right):
    return jnp.dot(left, right, preferred_element_type=F32)


def dot_general(left, right, contract):
    return lax.dot_general(left, right, ((contract[:1], contract[1:]), ((), ())), preferred_element_type=F32)


def softmax_base(scale):
    return scale * math.log2(math.e)


def attend_forward_kernel(heads, scale, start_ref, length_ref, qkv_ref, pick_ref, out_ref, norm_ref):
    parts, _, unit, _ = qkv_ref.shape
    base = softmax_base(scale)
    u = pl.program_id(0)
    first = start_ref[u]

    def head(which, h, at):
        lane = (which * heads + h) * LANES
        return qkv_ref[:, pl.ds(at, 1), :, lane : lane + LANES].reshape(parts * unit, LANES)

    def work(span):
        outs = []
        lane = lax.broadcasted_iota(jnp.int32, (parts * unit, LANES), 1)
        norms = jnp.zeros((parts * unit, LANES), F32)
        for h in range(heads):
            query = head(0, h, u)
            scores = [dot_general(query, head(1, h, first + j), (1, 1)) for j in range(span)]
            top = scores[0]
            for block in scores[1:]:
                top = jnp.maximum(top, block)
            top = jnp.max(top, axis=1, keepdims=True) * base
            attended = 0.0
            for j in range(span):
                raised = jnp.exp2(scores[j] * base - top).astype(BF)
                attended = attended + dot(raised, head(2, h, first + j))
            total = attended[:, LANES - 1 :]
            norms = jnp.where(lane == h, top + jnp.log2(total), norms)
            outs.append((attended * (1.0 / total)).astype(BF))
        norm_ref[0] = jnp.transpose(norms)[:8]
        packed = dot(jnp.concatenate(outs, axis=1), pick_ref[...]).astype(BF)
        out_ref[...] = packed.reshape(out_ref.shape)

    pl.when(length_ref[u] == 1)(lambda: work(1))
    pl.when(length_ref[u] != 1)(lambda: work(RATIO))


def attend_backward_kernel(
    heads,
    scale,
    start_ref,
    length_ref,
    qkv_ref,
    norm_ref,
    attended_ref,
    grad_ref,
    spread_ref,
    mark_ref,
    pick_ref,
    out_ref,
    dq,
    dk,
    dv,
    keys_across,
):
    parts, units, unit, _ = qkv_ref.shape
    base = softmax_base(scale)
    u = pl.program_id(0)
    first = start_ref[u]

    def head(which, h, at):
        lane = (which * heads + h) * LANES
        return qkv_ref[:, pl.ds(at, 1), :, lane : lane + LANES].reshape(parts * unit, LANES)

    @pl.when(u == 0)
    def _():
        dk[...] = jnp.zeros_like(dk)
        dv[...] = jnp.zeros_like(dv)

        def turn(i, carry):
            for h in range(heads):
                keys_across[i, h] = jnp.transpose(head(1, h, i))
            return carry

        lax.fori_loop(0, units, turn, 0)

    def work(span):
        packed = grad_ref[...].reshape(parts * unit, -1)
        grads = dot(packed, spread_ref[...]).astype(BF)
        product = packed.astype(F32) * attended_ref[...].reshape(parts * unit, -1).astype(F32)
        high = product.astype(BF)
        low = (product - high.astype(F32)).astype(BF)
        offsets = dot_general(mark_ref[...], high, (1, 1)) + dot_general(mark_ref[...], low, (1, 1))
        into = (parts, 1, unit, LANES)
        for h in range(heads):
            at = slice(h * LANES, (h + 1) * LANES)
            grad, query = grads[:, at], head(0, h, u)
            norm, offset = norm_ref[0, h : h + 1, :], offsets[h : h + 1]
            query_grad = 0.0
            for j in range(span):
                key, value = head(1, h, first + j), head(2, h, first + j)
                chance = jnp.exp2(dot_general(key, query, (1, 1)) * base - norm)
                chance_grad = dot_general(value, grad, (1, 1))
                score_grad = (chance * (chance_grad - offset)).astype(BF)
                block = pl.ds(first + j, 1)
                dv[:, block, :, at] += dot(chance.astype(BF), grad).reshape(into)
                dk[:, block, :, at] += dot(score_grad, query).reshape(into)
                query_grad = query_grad + dot(keys_across[first + j, h], score_grad)
            dq[:, pl.ds(u, 1), :, at] = jnp.transpose(query_grad * scale).astype(BF).reshape(into)

    pl.when(length_ref[u] == 1)(lambda: work(1))
    pl.when(length_ref[u] != 1)(lambda: work(RATIO))

    @pl.when(u == units - 1)
    def _():
        def pack(i, carry):
            at = pl.ds(i, 1)
            rows = [dq[:, at], (dk[:, at] * scale).astype(BF), dv[:, at].astype(BF)]
            rows = [row.reshape(parts * unit, -1) for row in rows]
            packed = dot(jnp.concatenate(rows, axis=1), pick_ref[...]).astype(BF)
            out_ref[:, at] = packed.reshape(parts, 1, unit, -1)
            return carry

        lax.fori_loop(0, units, pack, 0)


def whole_lanes(width):
    return -(-width // LANES) * LANES


def picker(heads, head_dim, dtype, width=None):
    row = jnp.arange(heads * LANES)[:, None]
    col = jnp.arange(heads * head_dim if width is None else width)[None, :]
    return ((row // LANES == col // head_dim) & (row % LANES == col % head_dim)).astype(dtype)


def attend_forward(start, length, qkv, heads, head_dim):
    parts, units, unit, lanes = qkv.shape
    width = heads * head_dim
    whole = lambda *shape: pl.BlockSpec(shape, lambda u, *_: (0,) * len(shape))
    return pl.pallas_call(
        partial(attend_forward_kernel, heads, 1.0 / math.sqrt(head_dim)),
        grid_spec=pltpu.PrefetchScalarGridSpec(
            num_scalar_prefetch=2,
            grid=(units,),
            in_specs=[whole(parts, units, unit, lanes), whole(heads * LANES, width)],
            out_specs=[
                pl.BlockSpec((parts, 1, unit, width), lambda u, *_: (0, u, 0, 0)),
                pl.BlockSpec((1, 8, parts * unit), lambda u, *_: (u, 0, 0)),
            ],
        ),
        out_shape=[
            jax.ShapeDtypeStruct((parts, units, unit, width), BF),
            jax.ShapeDtypeStruct((units, 8, parts * unit), F32),
        ],
        compiler_params=pltpu.CompilerParams(vmem_limit_bytes=48 * 2**20),
        cost_estimate=pl.CostEstimate(flops=10 * 2**30, bytes_accessed=16 * 2**20, transcendentals=2**23),
        name="attend_forward",
    )(start, length, qkv, picker(heads, head_dim, BF))


def attend_backward(start, length, qkv, norms, attended, grad, heads, head_dim):
    parts, units, unit, lanes = qkv.shape
    width = heads * head_dim
    whole = lambda *shape: pl.BlockSpec(shape, lambda u, *_: (0,) * len(shape))
    one_unit = pl.BlockSpec((parts, 1, unit, width), lambda u, *_: (0, u, 0, 0))
    pick = picker(heads, head_dim, BF)
    mark = (jnp.arange(8)[:, None] == jnp.arange(width)[None, :] // head_dim).astype(BF)
    return pl.pallas_call(
        partial(attend_backward_kernel, heads, 1.0 / math.sqrt(head_dim)),
        grid_spec=pltpu.PrefetchScalarGridSpec(
            num_scalar_prefetch=2,
            grid=(units,),
            in_specs=[
                whole(parts, units, unit, lanes),
                pl.BlockSpec((1, 8, parts * unit), lambda u, *_: (u, 0, 0)),
                one_unit,
                one_unit,
                whole(width, heads * LANES),
                whole(8, width),
                whole(3 * heads * LANES, whole_lanes(3 * width)),
            ],
            out_specs=whole(parts, units, unit, whole_lanes(3 * width)),
            scratch_shapes=[
                pltpu.VMEM((parts, units, unit, heads * LANES), BF),
                pltpu.VMEM((parts, units, unit, heads * LANES), F32),
                pltpu.VMEM((parts, units, unit, heads * LANES), F32),
                pltpu.VMEM((units, heads, LANES, parts * unit), BF),
            ],
        ),
        out_shape=jax.ShapeDtypeStruct((parts, units, unit, whole_lanes(3 * width)), BF),
        compiler_params=pltpu.CompilerParams(vmem_limit_bytes=56 * 2**20),
        cost_estimate=pl.CostEstimate(flops=2**20, bytes_accessed=2**20, transcendentals=0),
        name="attend_backward",
    )(start, length, qkv, norms, attended, grad, pick.T, mark, picker(3 * heads, head_dim, BF, whole_lanes(3 * width)))


MESH = pl.DeviceIdType.MESH


def add_into(ref, at, other):
    ref[at] = (ref[at].astype(F32) + other.astype(F32)).astype(BF)


def cut_rows(rows, k):
    up = (rows // 2 + 15) // 16 * 16
    return up if k % 2 == 0 else rows - up


def reduce_kernel(chunks, tensors, ready, ring, *refs):
    grads, slots, refs = refs[:tensors], refs[tensors], refs[tensors + 1 :]
    outs, slots_out, scratch = refs[:tensors], refs[tensors], list(refs[tensors + 1 :])
    own, local_sem, send_sem, recv_sem, credit, gathered_parts, slots_line, slots_send, slots_recv = scratch[:9]
    rings = scratch[9:]
    place, z = lax.axis_index("img"), lax.axis_index("blk")
    y, x, c = lax.div(place, 4), lax.rem(lax.div(place, 2), 2), lax.rem(place, 2)
    pair, beside, across = place + 1 - 2 * c, place + 2 - 4 * x, place + 4 - 8 * y
    near, far = z + 1 - 2 * lax.rem(z, 2), 3 - z
    inside = (z == 1) | (z == 2)
    outside = (z == 0) | (z == 3)

    barrier = pltpu.get_barrier_semaphore()
    for step in (1, 2, 3):
        pl.semaphore_signal(barrier, inc=1, device_id={"blk": lax.rem(z + step, 4)}, device_id_type=MESH)
    others = [lax.rem(place + step, 8) for step in range(1, 8)]
    for other in others:
        pl.semaphore_signal(barrier, inc=1, device_id={"img": other}, device_id_type=MESH)
    pl.semaphore_wait(barrier, 10)

    def send(k, which, source, target, where):
        return pltpu.make_async_remote_copy(
            src_ref=source,
            dst_ref=target,
            send_sem=send_sem.at[k, which],
            recv_sem=recv_sem.at[k, which],
            device_id=where,
            device_id_type=MESH,
        )

    def parts_of(k):
        t, row, rows, col, cols, gather = chunks[k]
        return grads[t], outs[t], row, rows, col, cols, gather

    def cut(k):
        return cut_rows(chunks[k][2], k)

    def is_ready(k):
        return chunks[k][0] in ready

    def slot(k):
        _, _, rows, _, cols, _ = chunks[k]
        first = cut(k)
        i = k % ring
        wide = pl.ds(0, cols)
        acc, rx, ry, rx2, ry2, from_near, from_far, total = rings
        return (
            acc.at[i, :, :, pl.ds(0, rows), wide],
            rx.at[i, :, pl.ds(0, first), wide],
            ry.at[i, :, pl.ds(0, rows - first), wide],
            rx2.at[i, pl.ds(0, rows - first), wide],
            ry2.at[i, pl.ds(0, first), wide],
            from_near.at[i, pl.ds(0, rows), wide],
            from_far.at[i, :, pl.ds(0, rows), wide],
            total.at[i, pl.ds(0, rows), wide],
        )

    copies = {}

    def begin(k, which, source, target, where):
        copies[k, which] = send(k, which, source, target, where)
        copies[k, which].start()

    def load(k):
        grad, _, row, rows, col, cols, _ = parts_of(k)
        return pltpu.make_async_copy(
            grad.at[:, :, c, pl.ds(row, rows), pl.ds(col, cols)],
            own.at[summed.index(k) % 2, :, :, pl.ds(0, rows), pl.ds(0, cols)],
            local_sem.at[summed.index(k) % 2],
        )

    count = len(chunks)

    def stage_zero(k):
        grad, _, row, rows, col, cols, _ = parts_of(k)
        if k >= ring:
            pl.semaphore_wait(credit.at[k % ring], 5)
        if is_ready(k):
            return
        begin(k, 0, grad.at[:, :, 1 - c, pl.ds(row, rows), pl.ds(col, cols)], slot(k)[0], {"img": pair})

    for k in range(min(ring, count)):
        stage_zero(k)
    summed = [k for k in range(count) if not is_ready(k)]
    for k in summed[:2]:
        load(k).start()

    wide_chunks = [k for k in range(count) if chunks[k][5]]

    def wide_total(k):
        _, _, rows, _, cols, _ = chunks[k]
        return gathered_parts.at[wide_chunks.index(k), :, pl.ds(0, rows), pl.ds(0, cols)]

    def stage_one(k):
        _, _, _, rows, _, cols, _ = parts_of(k)
        if is_ready(k):
            return
        acc, rx, ry = slot(k)[:3]
        load(k).wait()
        copies[k, 0].wait_recv()
        for i in range(2):
            for j in range(2):
                add_into(acc, (i, j), own[summed.index(k) % 2, i, j, :rows, :cols])
        for later in summed[summed.index(k) + 2 : summed.index(k) + 3]:
            load(later).start()
        first = cut(k)
        begin(k, 1, acc.at[:, 1 - x, pl.ds(0, first)], rx, {"img": beside})
        begin(k, 2, acc.at[1 - y, :, pl.ds(first, rows - first)], ry, {"img": across})

    def stage_two(k):
        if is_ready(k):
            return
        rows = chunks[k][2]
        acc, rx, ry, rx2, ry2 = slot(k)[:5]
        first = cut(k)
        copies[k, 1].wait_recv()
        copies[k, 2].wait_recv()
        copies[k, 1].wait_send()
        copies[k, 2].wait_send()
        for i in range(2):
            add_into(acc, (i, x, slice(0, first)), rx[i])
            add_into(acc, (y, i, slice(first, rows)), ry[i])
        begin(k, 3, acc.at[y, 1 - x, pl.ds(first, rows - first)], rx2, {"img": beside})
        begin(k, 4, acc.at[1 - y, x, pl.ds(0, first)], ry2, {"img": across})

    def stage_three(k):
        _, out, row, rows, col, cols, gather = parts_of(k)
        acc, _, _, rx2, ry2, from_near, from_far, total = slot(k)
        if gather:
            total = wide_total(k)
        if is_ready(k):
            from_far[0] = grads[chunks[k][0]][row : row + rows, col : col + cols]
            copies[k, 5] = send(k, 5, from_far.at[0], from_near, {"blk": near})
            pl.when(outside)(copies[k, 5].start)
            return
        first = cut(k)
        copies[k, 3].wait_recv()
        copies[k, 4].wait_recv()
        low = (acc[y, x, 0:first].astype(F32) + ry2[...].astype(F32)).astype(BF)
        high = (acc[y, x, first:rows].astype(F32) + rx2[...].astype(F32)).astype(BF)
        if gather:
            total[z, 0:first] = low
            total[z, first:rows] = high
            for step in (1, 2, 3):
                begin(k, 4 + step, total.at[z], total.at[z], {"blk": lax.rem(z + step, 4)})
            return
        from_far[0, 0:first] = low
        from_far[0, first:rows] = high
        copies[k, 5] = send(k, 5, from_far.at[0], from_near, {"blk": near})
        pl.when(outside)(copies[k, 5].start)

    def stage_four(k):
        if chunks[k][5]:
            return
        from_near, from_far, total = slot(k)[5:]
        copies[k, 6] = send(k, 6, from_far.at[0], from_far.at[1], {"blk": far})

        @pl.when(inside)
        def _():
            copies[k, 5].wait_recv()
            add_into(from_far, 0, from_near[...])
            copies[k, 6].start()

    def stage_five(k):
        if chunks[k][5]:
            return
        from_near, from_far, total = slot(k)[5:]
        copies[k, 7] = send(k, 7, total, total, {"blk": near})

        @pl.when(inside)
        def _():
            copies[k, 6].wait_recv()
            total[...] = (from_far[0].astype(F32) + from_far[1].astype(F32)).astype(BF)
            copies[k, 7].start()

    def stage_six(k):
        _, out, row, rows, col, cols, gather = parts_of(k)
        total = wide_total(k) if gather else slot(k)[7]
        if gather:
            for step in (1, 2, 3):
                copies[k, 4 + step].wait()
            out[:, row : row + rows, col : col + cols] = total[...]
        else:
            pl.when(outside)(copies[k, 7].wait_recv)
            out[row : row + rows, col : col + cols] = total[...]
            pl.when(outside)(copies[k, 5].wait_send)
            pl.when(inside)(copies[k, 6].wait_send)
            pl.when(inside)(copies[k, 7].wait_send)
        for which in () if is_ready(k) else (0, 3, 4):
            copies[k, which].wait_send()
        if k + ring < count:
            for other in (pair, beside, across):
                pl.semaphore_signal(credit.at[k % ring], inc=1, device_id={"img": other}, device_id_type=MESH)
            for other in (near, far):
                pl.semaphore_signal(credit.at[k % ring], inc=1, device_id={"blk": other}, device_id_type=MESH)

    def slots_copy(which, source, target, where):
        return pltpu.make_async_remote_copy(
            src_ref=source,
            dst_ref=target,
            send_sem=slots_send.at[which],
            recv_sem=slots_recv.at[which],
            device_id=where,
            device_id_type=MESH,
        )

    slots_near = slots_copy(0, slots, slots_line.at[0], {"blk": near})
    slots_far = slots_copy(8, slots_line.at[1], slots_line.at[2], {"blk": far})
    slots_back = slots_copy(9, slots_out.at[place], slots_out.at[place], {"blk": near})
    slots_round = [
        slots_copy(1 + i, slots_out.at[place], slots_out.at[place], {"img": other}) for i, other in enumerate(others)
    ]

    def slots_one():
        pl.when(outside)(slots_near.start)

    def slots_two():
        @pl.when(inside)
        def _():
            slots_near.wait_recv()
            slots_line[1] = slots_line[0] + slots[...]
            slots_far.start()

    def slots_three():
        @pl.when(inside)
        def _():
            slots_far.wait_recv()
            slots_out[place] = slots_line[1] + slots_line[2]
            slots_back.start()

    def slots_four():
        pl.when(outside)(slots_back.wait_recv)
        for copy in slots_round:
            copy.start()

    def slots_five():
        for copy in slots_round:
            copy.wait()
        pl.when(outside)(slots_near.wait_send)
        pl.when(inside)(slots_far.wait_send)
        pl.when(inside)(slots_back.wait_send)

    slots_stages = {0: slots_one, 2: slots_two, 4: slots_three, 6: slots_four, 9: slots_five}
    stages = ((stage_one, 0), (stage_two, 2), (stage_three, 4), (stage_four, 5), (stage_five, 6), (stage_six, 7))
    for step in range(max(count + 7, 10)):
        for stage, behind in stages:
            if 0 <= step - behind < count:
                stage(step - behind)
        if step - 8 >= 0 and step - 8 + ring < count:
            stage_zero(step - 8 + ring)
        if step in slots_stages:
            slots_stages[step]()


def reduce_call(grads, ready, gathered, slots, width, collective_id):
    chunks, shapes = [], []
    for t, grad in enumerate(grads):
        rows, cols = grad.shape[0] // (1 if t in ready else 8), grad.shape[1]
        depth = 144 if rows % 144 == 0 or t in ready else 128
        for row in range(0, rows, depth):
            for col in range(0, cols, width):
                chunks.append((t, row, min(depth, rows - row), col, min(width, cols - col), t == gathered))
        shapes.append(jax.ShapeDtypeStruct((4, rows, cols) if t == gathered else (rows, cols), BF))
    shapes.append(jax.ShapeDtypeStruct((8, *slots.shape), F32))
    n, ring = len(chunks), 12
    deep = max(rows for _, _, rows, _, _, _ in chunks)
    half = (deep // 2 + 15) // 16 * 16
    dma = pltpu.SemaphoreType.DMA
    scratch = [
        pltpu.VMEM((2, 2, 2, deep, width), BF),
        dma((2,)),
        dma((n, 8)),
        dma((n, 8)),
        pltpu.SemaphoreType.REGULAR((ring,)),
        pltpu.VMEM((max(1, sum(g for *_, g in chunks)), 4, deep, width), BF),
        pltpu.VMEM((3, *slots.shape), F32),
        dma((10,)),
        dma((10,)),
    ]
    for shape in (
        (2, 2, deep, width),
        (2, half, width),
        (2, half, width),
        (half, width),
        (half, width),
        (deep, width),
        (2, deep, width),
        (deep, width),
    ):
        scratch.append(pltpu.VMEM((ring, *shape), BF))
    vmem, anywhere = pl.BlockSpec(memory_space=pltpu.VMEM), pl.BlockSpec(memory_space=pl.ANY)
    return pl.pallas_call(
        partial(reduce_kernel, chunks, len(grads), ready, ring),
        out_shape=shapes,
        in_specs=[vmem if t in ready else anywhere for t in range(len(grads))] + [vmem],
        out_specs=[vmem] * (len(grads) + 1),
        scratch_shapes=scratch,
        compiler_params=pltpu.CompilerParams(
            collective_id=collective_id, has_side_effects=True, vmem_limit_bytes=56 * 2**20
        ),
        cost_estimate=pl.CostEstimate(flops=0, bytes_accessed=500 * 2**20, transcendentals=0),
        name=f"reduce_{collective_id}",
    )(
        *(g if t in ready else g.reshape(2, 2, 2, g.shape[0] // 8, g.shape[1]) for t, g in enumerate(grads)),
        slots,
    )


def gather_kernel(chunks, tensors, early, hot_ref, x_ref, share_ref, bias_ref, start_ref, *refs):
    shards, refs = refs[:tensors], refs[tensors:]
    fulls, refs = refs[:tensors], refs[tensors:]
    rows_ref, modulation_ref, bias_out = refs[:3]
    share_got, own_sem, first_send, first_recv, rest_send, rest_recv, bias_send, bias_recv = refs[3:11]
    send_sem, recv_sem, line_send, line_recv, spread_send, spread_recv = refs[11:]
    place, z = lax.axis_index("img"), lax.axis_index("blk")
    y, x, c = lax.div(place, 4), lax.rem(lax.div(place, 2), 2), lax.rem(place, 2)
    step_x, step_y = 2 - 4 * x, 4 - 8 * y
    pair, beside, across = place + 1 - 2 * c, place + step_x, place + step_y
    diagonal = place + step_x + step_y
    devices = share_got.shape[0]
    units, slots = hot_ref.shape
    unit = x_ref.shape[0] // units
    wide = x_ref.shape[1]

    barrier = pltpu.get_barrier_semaphore()
    for step in range(1, devices):
        pl.semaphore_signal(barrier, inc=1, device_id={"img": lax.rem(place + step, devices)}, device_id_type=MESH)
    for step in (1, 2, 3):
        pl.semaphore_signal(barrier, inc=1, device_id={"blk": lax.rem(z + step, 4)}, device_id_type=MESH)
    pl.semaphore_wait(barrier, devices + 2)

    def remote(source, target, send, recv, where):
        return pltpu.make_async_remote_copy(
            src_ref=source,
            dst_ref=target,
            send_sem=send,
            recv_sem=recv,
            device_id=where,
            device_id_type=MESH,
        )

    part = (share_ref.shape[2] - early) // 4
    part_at = pl.multiple_of(early + z * part, LANES)
    first, rest, biases = [], [], []
    for step in range(1, devices):
        to = lax.rem(place + step, devices)
        for copies, lo, size, send, recv in (
            (first, 0, early, first_send, first_recv),
            (rest, part_at, part, rest_send, rest_recv),
        ):
            copies.append(
                remote(
                    share_ref.at[to, :, pl.ds(lo, size)],
                    share_got.at[place, :, pl.ds(lo, size)],
                    send.at[step],
                    recv.at[step],
                    {"img": to},
                )
            )
        biases.append(remote(bias_ref, bias_out.at[place], bias_send.at[step], bias_recv.at[step], {"img": to}))
    for copy in first:
        copy.start()

    copies = {}

    def begin(k, which, block, rows, where):
        t, row, count = chunks[k]
        at = (block, pl.ds(row + rows[0], rows[1]))
        copies[k, which] = remote(
            fulls[t].at[at], fulls[t].at[at], send_sem.at[k, which], recv_sem.at[k, which], where
        )
        copies[k, which].start()

    def begin_own(k, which, where):
        t, row, count = chunks[k]
        source = shards[t].at[pl.ds(row, count)]
        copies[k, which] = remote(
            source, fulls[t].at[place, pl.ds(row, count)], send_sem.at[k, which], recv_sem.at[k, which], where
        )
        copies[k, which].start()

    own = [pltpu.make_async_copy(shards[t], fulls[t].at[place], own_sem.at[t]) for t in range(tensors)]
    def ahead(k):
        if k < len(chunks):
            begin_own(k, 0, {"img": beside})
            begin_own(k, 1, {"img": across})
            begin_own(k, 2, {"img": pair})

    ahead(0)
    for copy in rest + biases:
        copy.start()
    for k in range(1, 3):
        ahead(k)
    for copy in own:
        copy.start()

    share_got[place] = share_ref[place]
    bias_out[place] = bias_ref[...]
    for copy in first:
        copy.wait()

    def modulation_of(lo, size):
        at = pl.ds(lo, size)
        total = share_got[0, :, at]
        for i in range(1, devices):
            total = total + share_got[i, :, at]
        modulation_ref[:, at] = start_ref[:, at] + total

    modulation_of(0, early)
    for u in range(units):
        chosen = hot_ref[u : u + 1, 0:1] * modulation_ref[0:1, 0:early]
        for s in range(1, slots):
            chosen = chosen + hot_ref[u : u + 1, s : s + 1] * modulation_ref[s : s + 1, 0:early]
        at = pl.ds(u * unit, unit)
        values = x_ref[at, :].astype(F32)
        centered = values - jnp.mean(values, axis=1, keepdims=True)
        inverse = lax.rsqrt(jnp.mean(centered * centered, axis=1, keepdims=True) + EPSILON)
        rows_ref[z, at, :] = (centered * inverse * (1.0 + chosen[:, wide:]) + chosen[:, :wide]).astype(BF)

    up = [
        remote(block, block, line_send.at[0, s], line_recv.at[0, s], {"blk": lax.rem(z + 1, 4)})
        for s, block in ((s, rows_ref.at[lax.rem(z - s + 4, 4)]) for s in range(3))
    ]
    down = [
        remote(block, block, line_send.at[1, s], line_recv.at[1, s], {"blk": lax.rem(z + 3, 4)})
        for s, block in ((s, rows_ref.at[lax.rem(z + s, 4)]) for s in range(3))
    ]

    def line_step(s):
        if s > 0:
            pl.when(z >= s)(up[s - 1].wait_recv)
            pl.when(z + s < 4)(down[s - 1].wait_recv)
        if s < 3:
            pl.when((z >= s) & (z < 3))(up[s].start)
            pl.when((z + s < 4) & (z > 0))(down[s].start)

    def cut(k):
        return cut_rows(chunks[k][2], k)

    def relay(k):
        count, half = chunks[k][2], cut(k)
        copies[k, 0].wait_recv()
        begin(k, 3, beside, (0, half), {"img": across})
        begin(k, 5, beside, (0, count), {"img": pair})
        copies[k, 1].wait_recv()
        begin(k, 4, across, (half, count - half), {"img": beside})
        begin(k, 6, across, (0, count), {"img": pair})

    def last(k):
        count, half = chunks[k][2], cut(k)
        copies[k, 3].wait_recv()
        begin(k, 7, diagonal, (0, half), {"img": pair})
        copies[k, 4].wait_recv()
        begin(k, 8, diagonal, (half, count - half), {"img": pair})

    line_step(0)
    for copy in rest:
        copy.wait()
    modulation_of(part_at, part)
    own_part = modulation_ref.at[:, pl.ds(part_at, part)]
    spread = [
        remote(own_part, own_part, spread_send.at[step], spread_recv.at[step], {"blk": lax.rem(z + step, 4)})
        for step in (1, 2, 3)
    ]
    for copy in spread:
        copy.start()
    n = len(chunks)
    for k in range(n + 2):
        if k < n:
            relay(k)
            ahead(k + 3)
        if k >= 2:
            last(k - 2)
        for s in (1, 2):
            if k == 2 * s - 1:
                line_step(s)
    for copy in biases:
        copy.wait()
    line_step(3)
    for copy in spread:
        copy.wait()
    for copy in own:
        copy.wait()
    for k in range(n):
        for which in (0, 1, 3, 4):
            copies[k, which].wait_send()
        copies[k, 2].wait()
        for which in (5, 6, 7, 8):
            copies[k, which].wait()
    for s in range(3):
        pl.when((z >= s) & (z < 3))(up[s].wait_send)
        pl.when((z + s < 4) & (z > 0))(down[s].wait_send)


def gather_call(shards, unit_hot, rows, shares, bias_row, modulate_bias, collective_id):
    devices = shares.shape[0]
    slots, wide = shares.shape[1:]
    chunks = []
    for t, shard in enumerate(shards):
        depth = shard.shape[0]
        for row in range(0, depth, 144):
            chunks.append((t, row, min(144, depth - row)))
    n = len(chunks)
    vmem, anywhere = pl.BlockSpec(memory_space=pltpu.VMEM), pl.BlockSpec(memory_space=pl.ANY)
    dma = pltpu.SemaphoreType.DMA
    first_modulation = jnp.broadcast_to(modulate_bias.astype(F32)[None, :], (slots, wide))
    return pl.pallas_call(
        partial(gather_kernel, chunks, len(shards), 2 * rows.shape[1]),
        out_shape=[jax.ShapeDtypeStruct((devices, *s.shape), BF) for s in shards]
        + [
            jax.ShapeDtypeStruct((4, *rows.shape), BF),
            jax.ShapeDtypeStruct((slots, wide), F32),
            jax.ShapeDtypeStruct((devices, *bias_row.shape), F32),
        ],
        in_specs=[vmem] * 5 + [anywhere] * len(shards),
        out_specs=[anywhere] * len(shards) + [vmem] * 3,
        scratch_shapes=[
            pltpu.VMEM((devices, slots, wide), F32),
            dma((len(shards),)),
            dma((devices,)),
            dma((devices,)),
            dma((devices,)),
            dma((devices,)),
            dma((devices,)),
            dma((devices,)),
            dma((n, 9)),
            dma((n, 9)),
            dma((2, 3)),
            dma((2, 3)),
            dma((4,)),
            dma((4,)),
        ],
        compiler_params=pltpu.CompilerParams(
            collective_id=collective_id, has_side_effects=True, vmem_limit_bytes=48 * 2**20
        ),
        cost_estimate=pl.CostEstimate(flops=0, bytes_accessed=450 * 2**20, transcendentals=0),
        name=f"gather_{collective_id}",
    )(unit_hot, rows, shares, bias_row, first_modulation, *shards)


def assemble_kernel(mine, parts_ref, out_ref):
    pieces = [
        parts_ref[part, :, which * mine : (which + 1) * mine].astype(F32)
        for which in range(3)
        for part in range(parts_ref.shape[0])
    ]
    out_ref[...] = jnp.concatenate(pieces, axis=1)


def assemble(parts, mine):
    return pl.pallas_call(
        partial(assemble_kernel, mine),
        out_shape=jax.ShapeDtypeStruct((parts.shape[1], 3 * mine * parts.shape[0]), F32),
        compiler_params=pltpu.CompilerParams(vmem_limit_bytes=32 * 2**20),
        name="assemble",
    )(parts)


def total_kernel(mine_ref, out_ref, lines, line_send, line_recv, send_sem, recv_sem):
    place, z = lax.axis_index("img"), lax.axis_index("blk")
    parts, devices = lines.shape[0], out_ref.shape[0]
    barrier = pltpu.get_barrier_semaphore()
    for step in range(1, parts):
        pl.semaphore_signal(barrier, inc=1, device_id={"blk": lax.rem(z + step, parts)}, device_id_type=MESH)
    for step in range(1, devices):
        pl.semaphore_signal(barrier, inc=1, device_id={"img": lax.rem(place + step, devices)}, device_id_type=MESH)
    pl.semaphore_wait(barrier, parts + devices - 2)

    lines[z] = mine_ref[...]
    copies = [
        pltpu.make_async_remote_copy(
            src_ref=lines.at[z],
            dst_ref=lines.at[z],
            send_sem=line_send.at[step],
            recv_sem=line_recv.at[step],
            device_id={"blk": lax.rem(z + step, parts)},
            device_id_type=MESH,
        )
        for step in range(1, parts)
    ]
    for copy in copies:
        copy.start()
    for copy in copies:
        copy.wait()
    total = lines[0]
    for step in range(1, parts):
        total = total + lines[step]
    out_ref[place] = total
    copies = [
        pltpu.make_async_remote_copy(
            src_ref=out_ref.at[place],
            dst_ref=out_ref.at[place],
            send_sem=send_sem.at[step],
            recv_sem=recv_sem.at[step],
            device_id={"img": lax.rem(place + step, devices)},
            device_id_type=MESH,
        )
        for step in range(1, devices)
    ]
    for copy in copies:
        copy.start()
    for copy in copies:
        copy.wait()


def total_call(mine, devices, parts, collective_id):
    if (devices, parts) != (8, 4):
        return lax.all_gather(lax.psum(mine, "blk"), "img", axis=0, tiled=False)
    return pl.pallas_call(
        total_kernel,
        out_shape=jax.ShapeDtypeStruct((devices, *mine.shape), mine.dtype),
        in_specs=[pl.BlockSpec(memory_space=pltpu.VMEM)],
        out_specs=pl.BlockSpec(memory_space=pltpu.VMEM),
        scratch_shapes=[
            pltpu.VMEM((parts, *mine.shape), mine.dtype),
            pltpu.SemaphoreType.DMA((parts,)),
            pltpu.SemaphoreType.DMA((parts,)),
            pltpu.SemaphoreType.DMA((devices,)),
            pltpu.SemaphoreType.DMA((devices,)),
        ],
        compiler_params=pltpu.CompilerParams(
            collective_id=collective_id, has_side_effects=True, vmem_limit_bytes=32 * 2**20
        ),
        name=f"total_{collective_id}",
    )(mine)


def per_device(
    inputs,
    token_image,
    image_time,
    image_class,
    targets,
    cotangent,
    class_table,
    modulate_weight,
    modulate_bias,
    attend_weight,
    attend_bias,
    output_weight,
    output_bias,
    expand_weight,
    expand_bias,
    shrink_weight,
    shrink_bias,
    inner_weight,
    inner_bias,
    middle_weight,
    middle_bias,
    outer_weight,
    outer_bias,
):
    count, width = inputs.shape
    head_dim = width // HEADS
    columns = class_table.shape[1]
    devices, parts = lax.axis_size("img"), lax.axis_size("blk")
    place_img, place_blk = lax.axis_index("img"), lax.axis_index("blk")
    slots = image_class.shape[0] // devices
    unit = SHORT // parts
    units = count // unit
    heads = HEADS // parts
    mine = heads * head_dim
    half = width // 2

    class_hot = (image_class[:, None] == jnp.arange(class_table.shape[0])[None, :]).astype(BF)
    column = place_img * columns + jnp.arange(columns)
    frequency = jnp.exp(-math.log(10000.0) * (column % half).astype(F32) / half)
    angle = image_time.astype(F32)[:, None] * frequency[None, :]
    condition = dot(class_hot, class_table) + jnp.where(column[None, :] < half, jnp.cos(angle), jnp.sin(angle))
    silu_condition = jax.nn.silu(condition).astype(BF)
    shares = dot(silu_condition, modulate_weight)
    biases = (attend_bias, output_bias, expand_bias, shrink_bias, inner_bias, middle_bias, outer_bias)
    longest = whole_lanes(max(bias.shape[0] for bias in biases))
    bias_row = jnp.stack([jnp.pad(bias.astype(F32), (0, longest - bias.shape[0])) for bias in biases])
    bias_row = jnp.pad(bias_row, ((0, 8 - len(biases)), (0, 0)))
    shares = shares.reshape(devices, slots, -1)

    labels = token_image[::unit]
    same = labels[:, None] == labels[None, :]
    start = jnp.argmax(same, axis=1).astype(jnp.int32)
    length = jnp.sum(same, axis=1).astype(jnp.int32)
    unit_hot = (labels[:, None] == jnp.arange(slots)[None, :]).astype(F32)
    def by_unit(values):
        return values.reshape(units, unit, width)

    def by_row(values):
        return values.reshape(count, width)

    attend_mine = lax.dynamic_slice_in_dim(
        attend_weight.reshape(-1, 3, parts, mine), place_blk, 1, axis=2
    ).reshape(-1, 3 * mine)
    attend_mine = jnp.pad(attend_mine, ((0, 0), (0, whole_lanes(3 * mine) - 3 * mine)))

    def gather(shard):
        return lax.all_gather(shard, "img", axis=0, tiled=True)

    source = by_unit(inputs.astype(F32))
    normal_one, inverse_one = layer_norm(source)
    first_weights = (attend_mine, output_weight, expand_weight, outer_weight, shrink_weight)
    if (devices, parts) == (8, 4):
        *fulls, rows_group, modulation, got_bias = gather_call(
            first_weights, unit_hot, inputs, shares, bias_row, modulate_bias, 3
        )
        fulls = [full.reshape(-1, full.shape[2]) for full in fulls]
        modulated_group = rows_group.reshape(parts * count, width)
    else:
        fulls = [gather(shard) for shard in first_weights]
        modulation = modulate_bias.astype(F32)[None, :] + lax.psum_scatter(
            shares.reshape(devices * slots, -1), "img", scatter_dimension=0, tiled=True
        )
        got_bias = lax.all_gather(bias_row, "img", axis=0, tiled=False)
        chosen = jnp.dot(unit_hot, modulation, precision=HIGH)[:, None, : 2 * width]
        modulated_one = normal_one * (1.0 + chosen[:, :, width:]) + chosen[:, :, :width]
        modulated_group = lax.all_gather(by_row(modulated_one.astype(BF)), "blk", axis=0, tiled=True)
    attend_full, output_full, expand_full, outer_full, shrink_full = fulls
    inner_shard, middle_shard, modulated_group = lax.optimization_barrier(
        (inner_weight, middle_weight, modulated_group)
    )
    inner_full, middle_full = gather(inner_shard), gather(middle_shard)
    full_biases = [got_bias[:, i, : bias.shape[0]].reshape(-1) for i, bias in enumerate(biases)]
    (
        attend_bias_full,
        output_bias_full,
        expand_bias_full,
        shrink_bias_full,
        inner_bias_full,
        middle_bias_full,
        outer_bias_full,
    ) = full_biases
    unit_modulation = jnp.dot(unit_hot, modulation, precision=HIGH)
    shift_one, scale_one, gate_one, shift_two, scale_two, gate_two = (
        block[:, None, :] for block in jnp.split(unit_modulation, 6, axis=1)
    )

    def pad_heads(values):
        lead = values.shape[:-1]
        values = values.reshape(*lead, 3 * heads, head_dim)
        values = jnp.pad(values, ((0, 0),) * len(lead) + ((0, 0), (0, LANES - head_dim)))
        return values.reshape(*lead, 3 * heads * LANES)

    bias_mine = lax.dynamic_slice_in_dim(attend_bias_full.reshape(2, parts, mine), place_blk, 1, axis=1)
    bias_mine = jnp.concatenate([bias_mine[0, 0], jnp.zeros((mine,), F32), bias_mine[1, 0]])
    is_value = jnp.arange(3 * heads * LANES) >= 2 * heads * LANES
    is_last = jnp.arange(3 * heads * LANES) % LANES == LANES - 1
    padded_bias = jnp.where(is_value & is_last, 1.0, pad_heads(bias_mine))
    projected = dot(modulated_group, pad_heads(attend_full[:, : 3 * mine])) + padded_bias[None, :]
    qkv = projected.astype(BF).reshape(parts, units, unit, 3 * heads * LANES)
    attended_heads, norms = attend_forward(start, length, qkv, heads, head_dim)
    attended = lax.all_to_all(
        attended_heads.reshape(parts, count, mine), "blk", split_axis=0, concat_axis=0, tiled=True
    )
    output_heads = output_full.reshape(parts, mine, width)
    branch_one = by_unit(
        jnp.einsum("pti,pio->to", attended, output_heads, preferred_element_type=F32) + output_bias_full
    )
    middle = source + gate_one * branch_one
    normal_two, inverse_two = layer_norm(middle)
    modulated_two = by_row((normal_two * (1.0 + scale_two) + shift_two).astype(BF))
    expanded = dot(modulated_two, expand_full) + expand_bias_full
    gelu_tanh = partial(jax.nn.gelu, approximate=True)
    activated = gelu_tanh(expanded).astype(BF)
    branch_two = by_unit(dot(activated, shrink_full) + shrink_bias_full)
    whole = middle + gate_two * branch_two
    whole_low = by_row(whole.astype(BF))
    pre_one = dot(whole_low, inner_full) + inner_bias_full
    first = jax.nn.silu(pre_one).astype(BF)
    pre_two = dot(first, middle_full) + middle_bias_full
    second = jax.nn.silu(pre_two).astype(BF)
    aligned = dot(second, outer_full) + outer_bias_full
    target = targets.astype(F32)
    cross = jnp.sum(aligned * target, axis=1)
    aligned_inverse = lax.rsqrt(jnp.sum(aligned * aligned, axis=1) + EPSILON)
    target_inverse = lax.rsqrt(jnp.sum(target * target, axis=1) + EPSILON)
    cosine = cross * aligned_inverse * target_inverse
    grad_aligned = (
        -0.5
        * (
            target * (aligned_inverse * target_inverse)[:, None]
            - (cosine * aligned_inverse * aligned_inverse)[:, None] * aligned
        )
    ).astype(BF)

    def scatter(values):
        return lax.psum_scatter(values, "img", scatter_dimension=0, tiled=True)

    grad_outer = left_product(second, grad_aligned)
    grad_outer_bias = column_sum(grad_aligned)
    grad_pre_two = local_back(jax.nn.silu, pre_two, right_product(grad_aligned, outer_full)).astype(BF)
    grad_middle_weight = left_product(first, grad_pre_two)
    grad_middle_bias = column_sum(grad_pre_two)
    grad_pre_one = local_back(jax.nn.silu, pre_one, right_product(grad_pre_two, middle_full)).astype(BF)
    grad_inner = left_product(whole_low, grad_pre_one)
    grad_inner_bias = column_sum(grad_pre_one)
    early_weights = jnp.concatenate(
        [g.reshape(devices, -1, g.shape[1]) for g in (grad_inner, grad_middle_weight)], axis=1
    )
    early_part = scatter(early_weights.reshape(-1, early_weights.shape[2]))
    grad_whole = by_unit(cotangent.astype(F32)) + by_unit(right_product(grad_pre_one, inner_full))
    grad_gate_two = grad_whole * branch_two
    grad_branch_two = by_row((grad_whole * gate_two).astype(BF))
    grad_shrink = left_product(activated, grad_branch_two)
    grad_shrink_bias = column_sum(grad_branch_two)
    grad_expanded = local_back(gelu_tanh, expanded, right_product(grad_branch_two, shrink_full)).astype(BF)
    grad_expand = left_product(modulated_two, grad_expanded)
    grad_expand_bias = column_sum(grad_expanded)
    grad_mod_two = by_unit(right_product(grad_expanded, expand_full))
    grad_scale_two = grad_mod_two * normal_two
    grad_middle = grad_whole + norm_back(grad_mod_two * (1.0 + scale_two), normal_two, inverse_two)
    grad_gate_one = grad_middle * branch_one
    grad_branch_one = by_row((grad_middle * gate_one).astype(BF))
    grad_output = jnp.einsum("pti,to->pio", attended, grad_branch_one, preferred_element_type=F32)
    grad_output = grad_output.astype(BF).reshape(width, width)
    grad_output_bias = column_sum(grad_branch_one)
    def slot_sum(*values):
        rows = jnp.concatenate([jnp.sum(v, axis=1) for v in values], axis=1)
        return jnp.dot(unit_hot.T, rows, precision=HIGH)

    early_slots = slot_sum(grad_gate_one, grad_mod_two, grad_scale_two, grad_gate_two)
    grad_attended = jnp.einsum("to,pio->pti", grad_branch_one, output_heads, preferred_element_type=F32)
    grad_heads = lax.all_to_all(grad_attended.astype(BF), "blk", split_axis=0, concat_axis=0, tiled=True)
    grad_heads, grad_shrink, grad_expand, grad_output, grad_outer = lax.optimization_barrier(
        (grad_heads, grad_shrink, grad_expand, grad_output, grad_outer)
    )
    grad_heads = grad_heads.reshape(parts, units, unit, mine)
    grad_qkv = attend_backward(start, length, qkv, norms, attended_heads, grad_heads, heads, head_dim).reshape(parts * count, -1)
    grad_tied, early_sum = lax.optimization_barrier((grad_qkv, lax.psum(early_part, "blk")))
    grad_attend = left_product(modulated_group, grad_tied)
    partial_mod_one = right_product(grad_qkv, attend_full).astype(BF)
    qkv_bias = column_sum(grad_qkv[:, : 3 * mine]).reshape(3, 1, mine)
    spread = (jnp.arange(parts) == place_blk).astype(F32)[None, :, None]
    attend_bias_rows = jnp.concatenate([qkv_bias[:1], qkv_bias[2:]]) * spread
    bias_grads = (
        attend_bias_rows,
        grad_output_bias,
        grad_expand_bias,
        grad_shrink_bias,
        grad_inner_bias,
        grad_middle_bias,
        grad_outer_bias,
    )
    bias_rows = jnp.concatenate([b.reshape(devices, -1) for b in bias_grads], axis=1)
    early_width = early_slots.shape[1]
    deep = max(slots, devices)
    early_rows = jnp.concatenate(
        [
            jnp.pad(early_slots, ((0, deep - slots), (0, 0))),
            jnp.pad(bias_rows, ((0, deep - devices), (0, whole_lanes(bias_rows.shape[1]) - bias_rows.shape[1]))),
        ],
        axis=1,
    )
    grads = (grad_outer, grad_attend, grad_output, grad_shrink, grad_expand)
    if (devices, parts) == (8, 4):
        *sums, early = reduce_call(grads, (), 1, early_rows, 640, 1)
    else:
        sums = [scatter(grad) for grad in grads]
        attend_part = lax.all_gather(sums[1], "blk", axis=0, tiled=False)
        sums = list(lax.psum(tuple(sums[:1] + sums[2:]), "blk"))
        sums.insert(1, attend_part)
        early = lax.all_gather(lax.psum(early_rows, "blk"), "img", axis=0, tiled=False)
    outer_sum, attend_parts, output_sum, shrink_sum, expand_sum = sums
    inner_sum, middle_sum = early_sum[: inner_weight.shape[0]], early_sum[inner_weight.shape[0] :]
    attend_sum = assemble(attend_parts, mine)
    grad_mod_one = lax.psum_scatter(partial_mod_one, "blk", scatter_dimension=0, tiled=True)
    grad_mod_one, early = lax.optimization_barrier((grad_mod_one, early))
    early_grad = early[:, :slots, :early_width].reshape(devices * slots, -1)
    grad_mod_one = by_unit(grad_mod_one.astype(F32))
    grad_scale_one = grad_mod_one * normal_one
    grad_source = grad_middle + norm_back(grad_mod_one * (1.0 + scale_one), normal_one, inverse_one)

    late_slots = slot_sum(grad_mod_one, grad_scale_one)
    late_grad = total_call(late_slots, devices, parts, 2).reshape(devices * slots, 2 * width)
    bias_sum = jnp.sum(lax.dynamic_index_in_dim(early, place_img, axis=1, keepdims=False)[:, early_width:], axis=0)
    bias_sums = []
    at = 0
    for bias in biases:
        bias_sums.append(bias_sum[at : at + bias.shape[0]])
        at += bias.shape[0]
    (
        attend_bias_sum,
        output_bias_sum,
        expand_bias_sum,
        shrink_bias_sum,
        inner_bias_sum,
        middle_bias_sum,
        outer_bias_sum,
    ) = bias_sums
    modulation_grad = jnp.concatenate([late_grad, early_grad], axis=1)
    modulate_sum = jnp.dot(silu_condition.astype(F32).T, modulation_grad, precision=HIGH)
    modulate_bias_sum = jnp.sum(modulation_grad, axis=0)
    silu_grad = jnp.dot(modulation_grad, modulate_weight.astype(F32).T, precision=HIGH)
    condition_grad = local_back(jax.nn.silu, condition, silu_grad)
    table_sum = jnp.dot(class_hot.astype(F32).T, condition_grad, precision=HIGH)
    return (
        whole_low,
        by_row(grad_source.astype(BF)),
        table_sum,
        modulate_sum,
        modulate_bias_sum,
        attend_sum.astype(F32),
        attend_bias_sum,
        output_sum.astype(F32),
        output_bias_sum,
        expand_sum.astype(F32),
        expand_bias_sum,
        shrink_sum.astype(F32),
        shrink_bias_sum,
        inner_sum.astype(F32),
        inner_bias_sum,
        middle_sum.astype(F32),
        middle_bias_sum,
        outer_sum.astype(F32),
        outer_bias_sum,
    )


def solution(mesh):
    in_specs = (
        P(("img", "blk"), None),
        P(("img", "blk")),
        P(),
        P(),
        P(("img", "blk"), None),
        P(("img", "blk"), None),
        P(None, "img"),
        P("img", None),
        P(),
        P("img", None),
        P("img"),
        P("img", None),
        P("img"),
        P("img", None),
        P("img"),
        P("img", None),
        P("img"),
        P("img", None),
        P("img"),
        P("img", None),
        P("img"),
        P("img", None),
        P("img"),
    )
    out_specs = (
        P(("img", "blk"), None),
        P(("img", "blk"), None),
        P(None, "img"),
        P("img", None),
        P(),
        P("img", None),
        P("img"),
        P("img", None),
        P("img"),
        P("img", None),
        P("img"),
        P("img", None),
        P("img"),
        P("img", None),
        P("img"),
        P("img", None),
        P("img"),
        P("img", None),
        P("img"),
    )
    return jax.shard_map(
        per_device, mesh=mesh, in_specs=in_specs, out_specs=out_specs, check_vma=False
    )
```

```python
from functools import partial
import math

import jax
import jax.numpy as jnp
from jax import lax
from jax.experimental import pallas as pl
from jax.experimental.pallas import tpu as pltpu
from jax.sharding import PartitionSpec as P

HEADS = 16
SHORT = 256
RATIO = 4
LANES = 128

EPSILON = 1e-06
HIGH = lax.Precision.HIGHEST
BF = jnp.bfloat16
F32 = jnp.float32


def layer_norm(values):
    mean = jnp.mean(values, axis=-1, keepdims=True)
    centered = values - mean
    variance = jnp.mean(centered * centered, axis=-1, keepdims=True)
    inverse = lax.rsqrt(variance + EPSILON)
    return (centered * inverse, inverse)


def norm_back(grad, normal, inverse):
    mean_grad = jnp.mean(grad, axis=-1, keepdims=True)
    mean_cross = jnp.mean(grad * normal, axis=-1, keepdims=True)
    return inverse * (grad - mean_grad - normal * mean_cross)


def local_back(function, point, grad):
    return jax.vjp(function, point)[1](grad)[0]


def left_product(left, right):
    return jnp.einsum("ti,to->io", left, right, preferred_element_type=F32).astype(BF)


def right_product(grad, weight):
    return jnp.einsum("to,io->ti", grad, weight, preferred_element_type=F32)


def column_sum(values):
    return jnp.sum(values.astype(F32), axis=0)


def dot(left, right):
    return jnp.dot(left, right, preferred_element_type=F32)


def dot_general(left, right, contract):
    return lax.dot_general(left, right, ((contract[:1], contract[1:]), ((), ())), preferred_element_type=F32)


def softmax_base(scale):
    return scale * math.log2(math.e)


def attend_forward_kernel(heads, scale, start_ref, length_ref, qkv_ref, pick_ref, out_ref, norm_ref):
    parts, _, unit, _ = qkv_ref.shape
    base = softmax_base(scale)
    u = pl.program_id(0)
    first = start_ref[u]

    def head(which, h, at):
        lane = (which * heads + h) * LANES
        return qkv_ref[:, pl.ds(at, 1), :, lane : lane + LANES].reshape(parts * unit, LANES)

    def work(span):
        outs = []
        lane = lax.broadcasted_iota(jnp.int32, (parts * unit, LANES), 1)
        norms = jnp.zeros((parts * unit, LANES), F32)
        for h in range(heads):
            query = head(0, h, u)
            scores = [dot_general(query, head(1, h, first + j), (1, 1)) for j in range(span)]
            top = scores[0]
            for block in scores[1:]:
                top = jnp.maximum(top, block)
            top = jnp.max(top, axis=1, keepdims=True) * base
            attended = 0.0
            for j in range(span):
                raised = jnp.exp2(scores[j] * base - top).astype(BF)
                attended = attended + dot(raised, head(2, h, first + j))
            total = attended[:, LANES - 1 :]
            norms = jnp.where(lane == h, top + jnp.log2(total), norms)
            outs.append((attended * (1.0 / total)).astype(BF))
        norm_ref[0] = jnp.transpose(norms)[:8]
        packed = dot(jnp.concatenate(outs, axis=1), pick_ref[...]).astype(BF)
        out_ref[...] = packed.reshape(out_ref.shape)

    pl.when(length_ref[u] == 1)(lambda: work(1))
    pl.when(length_ref[u] != 1)(lambda: work(RATIO))


def attend_backward_kernel(
    heads,
    scale,
    start_ref,
    length_ref,
    qkv_ref,
    norm_ref,
    attended_ref,
    grad_ref,
    spread_ref,
    mark_ref,
    pick_ref,
    out_ref,
    dq,
    dk,
    dv,
    keys_across,
):
    parts, units, unit, _ = qkv_ref.shape
    base = softmax_base(scale)
    u = pl.program_id(0)
    first = start_ref[u]

    def head(which, h, at):
        lane = (which * heads + h) * LANES
        return qkv_ref[:, pl.ds(at, 1), :, lane : lane + LANES].reshape(parts * unit, LANES)

    @pl.when(u == 0)
    def _():
        dk[...] = jnp.zeros_like(dk)
        dv[...] = jnp.zeros_like(dv)

        def turn(i, carry):
            for h in range(heads):
                keys_across[i, h] = jnp.transpose(head(1, h, i))
            return carry

        lax.fori_loop(0, units, turn, 0)

    def work(span):
        packed = grad_ref[...].reshape(parts * unit, -1)
        grads = dot(packed, spread_ref[...]).astype(BF)
        product = packed.astype(F32) * attended_ref[...].reshape(parts * unit, -1).astype(F32)
        high = product.astype(BF)
        low = (product - high.astype(F32)).astype(BF)
        offsets = dot_general(mark_ref[...], high, (1, 1)) + dot_general(mark_ref[...], low, (1, 1))
        into = (parts, 1, unit, LANES)
        for h in range(heads):
            at = slice(h * LANES, (h + 1) * LANES)
            grad, query = grads[:, at], head(0, h, u)
            norm, offset = norm_ref[0, h : h + 1, :], offsets[h : h + 1]
            query_grad = 0.0
            for j in range(span):
                key, value = head(1, h, first + j), head(2, h, first + j)
                chance = jnp.exp2(dot_general(key, query, (1, 1)) * base - norm)
                chance_grad = dot_general(value, grad, (1, 1))
                score_grad = (chance * (chance_grad - offset)).astype(BF)
                block = pl.ds(first + j, 1)
                dv[:, block, :, at] += dot(chance.astype(BF), grad).reshape(into)
                dk[:, block, :, at] += dot(score_grad, query).reshape(into)
                query_grad = query_grad + dot(keys_across[first + j, h], score_grad)
            dq[:, pl.ds(u, 1), :, at] = jnp.transpose(query_grad * scale).astype(BF).reshape(into)

    pl.when(length_ref[u] == 1)(lambda: work(1))
    pl.when(length_ref[u] != 1)(lambda: work(RATIO))

    @pl.when(u == units - 1)
    def _():
        def pack(i, carry):
            at = pl.ds(i, 1)
            rows = [dq[:, at], (dk[:, at] * scale).astype(BF), dv[:, at].astype(BF)]
            rows = [row.reshape(parts * unit, -1) for row in rows]
            packed = dot(jnp.concatenate(rows, axis=1), pick_ref[...]).astype(BF)
            out_ref[:, at] = packed.reshape(parts, 1, unit, -1)
            return carry

        lax.fori_loop(0, units, pack, 0)


def whole_lanes(width):
    return -(-width // LANES) * LANES


def picker(heads, head_dim, dtype, width=None):
    row = jnp.arange(heads * LANES)[:, None]
    col = jnp.arange(heads * head_dim if width is None else width)[None, :]
    return ((row // LANES == col // head_dim) & (row % LANES == col % head_dim)).astype(dtype)


def attend_forward(start, length, qkv, heads, head_dim):
    parts, units, unit, lanes = qkv.shape
    width = heads * head_dim
    whole = lambda *shape: pl.BlockSpec(shape, lambda u, *_: (0,) * len(shape))
    return pl.pallas_call(
        partial(attend_forward_kernel, heads, 1.0 / math.sqrt(head_dim)),
        grid_spec=pltpu.PrefetchScalarGridSpec(
            num_scalar_prefetch=2,
            grid=(units,),
            in_specs=[whole(parts, units, unit, lanes), whole(heads * LANES, width)],
            out_specs=[
                pl.BlockSpec((parts, 1, unit, width), lambda u, *_: (0, u, 0, 0)),
                pl.BlockSpec((1, 8, parts * unit), lambda u, *_: (u, 0, 0)),
            ],
        ),
        out_shape=[
            jax.ShapeDtypeStruct((parts, units, unit, width), BF),
            jax.ShapeDtypeStruct((units, 8, parts * unit), F32),
        ],
        compiler_params=pltpu.CompilerParams(vmem_limit_bytes=48 * 2**20),
        cost_estimate=pl.CostEstimate(flops=10 * 2**30, bytes_accessed=16 * 2**20, transcendentals=2**23),
        name="attend_forward",
    )(start, length, qkv, picker(heads, head_dim, BF))


def attend_backward(start, length, qkv, norms, attended, grad, heads, head_dim):
    parts, units, unit, lanes = qkv.shape
    width = heads * head_dim
    whole = lambda *shape: pl.BlockSpec(shape, lambda u, *_: (0,) * len(shape))
    one_unit = pl.BlockSpec((parts, 1, unit, width), lambda u, *_: (0, u, 0, 0))
    pick = picker(heads, head_dim, BF)
    mark = (jnp.arange(8)[:, None] == jnp.arange(width)[None, :] // head_dim).astype(BF)
    return pl.pallas_call(
        partial(attend_backward_kernel, heads, 1.0 / math.sqrt(head_dim)),
        grid_spec=pltpu.PrefetchScalarGridSpec(
            num_scalar_prefetch=2,
            grid=(units,),
            in_specs=[
                whole(parts, units, unit, lanes),
                pl.BlockSpec((1, 8, parts * unit), lambda u, *_: (u, 0, 0)),
                one_unit,
                one_unit,
                whole(width, heads * LANES),
                whole(8, width),
                whole(3 * heads * LANES, whole_lanes(3 * width)),
            ],
            out_specs=whole(parts, units, unit, whole_lanes(3 * width)),
            scratch_shapes=[
                pltpu.VMEM((parts, units, unit, heads * LANES), BF),
                pltpu.VMEM((parts, units, unit, heads * LANES), F32),
                pltpu.VMEM((parts, units, unit, heads * LANES), F32),
                pltpu.VMEM((units, heads, LANES, parts * unit), BF),
            ],
        ),
        out_shape=jax.ShapeDtypeStruct((parts, units, unit, whole_lanes(3 * width)), BF),
        compiler_params=pltpu.CompilerParams(vmem_limit_bytes=56 * 2**20),
        cost_estimate=pl.CostEstimate(flops=2**20, bytes_accessed=2**20, transcendentals=0),
        name="attend_backward",
    )(start, length, qkv, norms, attended, grad, pick.T, mark, picker(3 * heads, head_dim, BF, whole_lanes(3 * width)))


MESH = pl.DeviceIdType.MESH


def add_into(ref, at, other):
    ref[at] = (ref[at].astype(F32) + other.astype(F32)).astype(BF)


def cut_rows(rows, k):
    up = (rows // 2 + 15) // 16 * 16
    return up if k % 2 == 0 else rows - up


def reduce_kernel(chunks, tensors, ready, ring, *refs):
    grads, slots, refs = refs[:tensors], refs[tensors], refs[tensors + 1 :]
    outs, slots_out, scratch = refs[:tensors], refs[tensors], list(refs[tensors + 1 :])
    own, local_sem, send_sem, recv_sem, credit, gathered_parts, slots_line, slots_send, slots_recv = scratch[:9]
    rings = scratch[9:]
    place, z = lax.axis_index("img"), lax.axis_index("blk")
    y, x, c = lax.div(place, 4), lax.rem(lax.div(place, 2), 2), lax.rem(place, 2)
    pair, beside, across = place + 1 - 2 * c, place + 2 - 4 * x, place + 4 - 8 * y
    near, far = z + 1 - 2 * lax.rem(z, 2), 3 - z
    inside = (z == 1) | (z == 2)
    outside = (z == 0) | (z == 3)

    barrier = pltpu.get_barrier_semaphore()
    for step in (1, 2, 3):
        pl.semaphore_signal(barrier, inc=1, device_id={"blk": lax.rem(z + step, 4)}, device_id_type=MESH)
    others = [lax.rem(place + step, 8) for step in range(1, 8)]
    for other in others:
        pl.semaphore_signal(barrier, inc=1, device_id={"img": other}, device_id_type=MESH)
    pl.semaphore_wait(barrier, 10)

    def send(k, which, source, target, where):
        return pltpu.make_async_remote_copy(
            src_ref=source,
            dst_ref=target,
            send_sem=send_sem.at[k, which],
            recv_sem=recv_sem.at[k, which],
            device_id=where,
            device_id_type=MESH,
        )

    def parts_of(k):
        t, row, rows, col, cols, gather = chunks[k]
        return grads[t], outs[t], row, rows, col, cols, gather

    def cut(k):
        return cut_rows(chunks[k][2], k)

    def is_ready(k):
        return chunks[k][0] in ready

    def slot(k):
        _, _, rows, _, cols, _ = chunks[k]
        first = cut(k)
        i = k % ring
        wide = pl.ds(0, cols)
        acc, rx, ry, rx2, ry2, from_near, from_far, total = rings
        return (
            acc.at[i, :, :, pl.ds(0, rows), wide],
            rx.at[i, :, pl.ds(0, first), wide],
            ry.at[i, :, pl.ds(0, rows - first), wide],
            rx2.at[i, pl.ds(0, rows - first), wide],
            ry2.at[i, pl.ds(0, first), wide],
            from_near.at[i, pl.ds(0, rows), wide],
            from_far.at[i, :, pl.ds(0, rows), wide],
            total.at[i, pl.ds(0, rows), wide],
        )

    copies = {}

    def begin(k, which, source, target, where):
        copies[k, which] = send(k, which, source, target, where)
        copies[k, which].start()

    def load(k):
        grad, _, row, rows, col, cols, _ = parts_of(k)
        return pltpu.make_async_copy(
            grad.at[:, :, c, pl.ds(row, rows), pl.ds(col, cols)],
            own.at[summed.index(k) % 2, :, :, pl.ds(0, rows), pl.ds(0, cols)],
            local_sem.at[summed.index(k) % 2],
        )

    count = len(chunks)

    def stage_zero(k):
        grad, _, row, rows, col, cols, _ = parts_of(k)
        if k >= ring:
            pl.semaphore_wait(credit.at[k % ring], 5)
        if is_ready(k):
            return
        begin(k, 0, grad.at[:, :, 1 - c, pl.ds(row, rows), pl.ds(col, cols)], slot(k)[0], {"img": pair})

    for k in range(min(ring, count)):
        stage_zero(k)
    summed = [k for k in range(count) if not is_ready(k)]
    for k in summed[:2]:
        load(k).start()

    wide_chunks = [k for k in range(count) if chunks[k][5]]

    def wide_total(k):
        _, _, rows, _, cols, _ = chunks[k]
        return gathered_parts.at[wide_chunks.index(k), :, pl.ds(0, rows), pl.ds(0, cols)]

    def stage_one(k):
        _, _, _, rows, _, cols, _ = parts_of(k)
        if is_ready(k):
            return
        acc, rx, ry = slot(k)[:3]
        load(k).wait()
        copies[k, 0].wait_recv()
        for i in range(2):
            for j in range(2):
                add_into(acc, (i, j), own[summed.index(k) % 2, i, j, :rows, :cols])
        for later in summed[summed.index(k) + 2 : summed.index(k) + 3]:
            load(later).start()
        first = cut(k)
        begin(k, 1, acc.at[:, 1 - x, pl.ds(0, first)], rx, {"img": beside})
        begin(k, 2, acc.at[1 - y, :, pl.ds(first, rows - first)], ry, {"img": across})

    def stage_two(k):
        if is_ready(k):
            return
        rows = chunks[k][2]
        acc, rx, ry, rx2, ry2 = slot(k)[:5]
        first = cut(k)
        copies[k, 1].wait_recv()
        copies[k, 2].wait_recv()
        copies[k, 1].wait_send()
        copies[k, 2].wait_send()
        for i in range(2):
            add_into(acc, (i, x, slice(0, first)), rx[i])
            add_into(acc, (y, i, slice(first, rows)), ry[i])
        begin(k, 3, acc.at[y, 1 - x, pl.ds(first, rows - first)], rx2, {"img": beside})
        begin(k, 4, acc.at[1 - y, x, pl.ds(0, first)], ry2, {"img": across})

    def stage_three(k):
        _, out, row, rows, col, cols, gather = parts_of(k)
        acc, _, _, rx2, ry2, from_near, from_far, total = slot(k)
        if gather:
            total = wide_total(k)
        if is_ready(k):
            from_far[0] = grads[chunks[k][0]][row : row + rows, col : col + cols]
            copies[k, 5] = send(k, 5, from_far.at[0], from_near, {"blk": near})
            pl.when(outside)(copies[k, 5].start)
            return
        first = cut(k)
        copies[k, 3].wait_recv()
        copies[k, 4].wait_recv()
        low = (acc[y, x, 0:first].astype(F32) + ry2[...].astype(F32)).astype(BF)
        high = (acc[y, x, first:rows].astype(F32) + rx2[...].astype(F32)).astype(BF)
        if gather:
            total[z, 0:first] = low
            total[z, first:rows] = high
            for step in (1, 2, 3):
                begin(k, 4 + step, total.at[z], total.at[z], {"blk": lax.rem(z + step, 4)})
            return
        from_far[0, 0:first] = low
        from_far[0, first:rows] = high
        copies[k, 5] = send(k, 5, from_far.at[0], from_near, {"blk": near})
        pl.when(outside)(copies[k, 5].start)

    def stage_four(k):
        if chunks[k][5]:
            return
        from_near, from_far, total = slot(k)[5:]
        copies[k, 6] = send(k, 6, from_far.at[0], from_far.at[1], {"blk": far})

        @pl.when(inside)
        def _():
            copies[k, 5].wait_recv()
            add_into(from_far, 0, from_near[...])
            copies[k, 6].start()

    def stage_five(k):
        if chunks[k][5]:
            return
        from_near, from_far, total = slot(k)[5:]
        copies[k, 7] = send(k, 7, total, total, {"blk": near})

        @pl.when(inside)
        def _():
            copies[k, 6].wait_recv()
            total[...] = (from_far[0].astype(F32) + from_far[1].astype(F32)).astype(BF)
            copies[k, 7].start()

    def stage_six(k):
        _, out, row, rows, col, cols, gather = parts_of(k)
        total = wide_total(k) if gather else slot(k)[7]
        if gather:
            for step in (1, 2, 3):
                copies[k, 4 + step].wait()
            out[:, row : row + rows, col : col + cols] = total[...]
        else:
            pl.when(outside)(copies[k, 7].wait_recv)
            out[row : row + rows, col : col + cols] = total[...]
            pl.when(outside)(copies[k, 5].wait_send)
            pl.when(inside)(copies[k, 6].wait_send)
            pl.when(inside)(copies[k, 7].wait_send)
        for which in () if is_ready(k) else (0, 3, 4):
            copies[k, which].wait_send()
        if k + ring < count:
            for other in (pair, beside, across):
                pl.semaphore_signal(credit.at[k % ring], inc=1, device_id={"img": other}, device_id_type=MESH)
            for other in (near, far):
                pl.semaphore_signal(credit.at[k % ring], inc=1, device_id={"blk": other}, device_id_type=MESH)

    def slots_copy(which, source, target, where):
        return pltpu.make_async_remote_copy(
            src_ref=source,
            dst_ref=target,
            send_sem=slots_send.at[which],
            recv_sem=slots_recv.at[which],
            device_id=where,
            device_id_type=MESH,
        )

    slots_near = slots_copy(0, slots, slots_line.at[0], {"blk": near})
    slots_far = slots_copy(8, slots_line.at[1], slots_line.at[2], {"blk": far})
    slots_back = slots_copy(9, slots_out.at[place], slots_out.at[place], {"blk": near})
    slots_round = [
        slots_copy(1 + i, slots_out.at[place], slots_out.at[place], {"img": other}) for i, other in enumerate(others)
    ]

    def slots_one():
        pl.when(outside)(slots_near.start)

    def slots_two():
        @pl.when(inside)
        def _():
            slots_near.wait_recv()
            slots_line[1] = slots_line[0] + slots[...]
            slots_far.start()

    def slots_three():
        @pl.when(inside)
        def _():
            slots_far.wait_recv()
            slots_out[place] = slots_line[1] + slots_line[2]
            slots_back.start()

    def slots_four():
        pl.when(outside)(slots_back.wait_recv)
        for copy in slots_round:
            copy.start()

    def slots_five():
        for copy in slots_round:
            copy.wait()
        pl.when(outside)(slots_near.wait_send)
        pl.when(inside)(slots_far.wait_send)
        pl.when(inside)(slots_back.wait_send)

    slots_stages = {0: slots_one, 2: slots_two, 4: slots_three, 6: slots_four, 9: slots_five}
    stages = ((stage_one, 0), (stage_two, 2), (stage_three, 4), (stage_four, 5), (stage_five, 6), (stage_six, 7))
    for step in range(max(count + 7, 10)):
        for stage, behind in stages:
            if 0 <= step - behind < count:
                stage(step - behind)
        if step - 8 >= 0 and step - 8 + ring < count:
            stage_zero(step - 8 + ring)
        if step in slots_stages:
            slots_stages[step]()


def reduce_call(grads, ready, gathered, slots, width, collective_id):
    chunks, shapes = [], []
    for t, grad in enumerate(grads):
        rows, cols = grad.shape[0] // (1 if t in ready else 8), grad.shape[1]
        depth = 144 if rows % 144 == 0 or t in ready else 128
        for row in range(0, rows, depth):
            for col in range(0, cols, width):
                chunks.append((t, row, min(depth, rows - row), col, min(width, cols - col), t == gathered))
        shapes.append(jax.ShapeDtypeStruct((4, rows, cols) if t == gathered else (rows, cols), BF))
    shapes.append(jax.ShapeDtypeStruct((8, *slots.shape), F32))
    n, ring = len(chunks), 12
    deep = max(rows for _, _, rows, _, _, _ in chunks)
    half = (deep // 2 + 15) // 16 * 16
    dma = pltpu.SemaphoreType.DMA
    scratch = [
        pltpu.VMEM((2, 2, 2, deep, width), BF),
        dma((2,)),
        dma((n, 8)),
        dma((n, 8)),
        pltpu.SemaphoreType.REGULAR((ring,)),
        pltpu.VMEM((max(1, sum(g for *_, g in chunks)), 4, deep, width), BF),
        pltpu.VMEM((3, *slots.shape), F32),
        dma((10,)),
        dma((10,)),
    ]
    for shape in (
        (2, 2, deep, width),
        (2, half, width),
        (2, half, width),
        (half, width),
        (half, width),
        (deep, width),
        (2, deep, width),
        (deep, width),
    ):
        scratch.append(pltpu.VMEM((ring, *shape), BF))
    vmem, anywhere = pl.BlockSpec(memory_space=pltpu.VMEM), pl.BlockSpec(memory_space=pl.ANY)
    return pl.pallas_call(
        partial(reduce_kernel, chunks, len(grads), ready, ring),
        out_shape=shapes,
        in_specs=[vmem if t in ready else anywhere for t in range(len(grads))] + [vmem],
        out_specs=[vmem] * (len(grads) + 1),
        scratch_shapes=scratch,
        compiler_params=pltpu.CompilerParams(
            collective_id=collective_id, has_side_effects=True, vmem_limit_bytes=56 * 2**20
        ),
        cost_estimate=pl.CostEstimate(flops=0, bytes_accessed=500 * 2**20, transcendentals=0),
        name=f"reduce_{collective_id}",
    )(
        *(g if t in ready else g.reshape(2, 2, 2, g.shape[0] // 8, g.shape[1]) for t, g in enumerate(grads)),
        slots,
    )


def gather_kernel(chunks, tensors, early, hot_ref, x_ref, share_ref, bias_ref, start_ref, *refs):
    shards, refs = refs[:tensors], refs[tensors:]
    fulls, refs = refs[:tensors], refs[tensors:]
    rows_ref, modulation_ref, bias_out = refs[:3]
    share_got, own_sem, first_send, first_recv, rest_send, rest_recv, bias_send, bias_recv = refs[3:11]
    send_sem, recv_sem, line_send, line_recv, spread_send, spread_recv = refs[11:]
    place, z = lax.axis_index("img"), lax.axis_index("blk")
    y, x, c = lax.div(place, 4), lax.rem(lax.div(place, 2), 2), lax.rem(place, 2)
    step_x, step_y = 2 - 4 * x, 4 - 8 * y
    pair, beside, across = place + 1 - 2 * c, place + step_x, place + step_y
    diagonal = place + step_x + step_y
    devices = share_got.shape[0]
    units, slots = hot_ref.shape
    unit = x_ref.shape[0] // units
    wide = x_ref.shape[1]

    barrier = pltpu.get_barrier_semaphore()
    for step in range(1, devices):
        pl.semaphore_signal(barrier, inc=1, device_id={"img": lax.rem(place + step, devices)}, device_id_type=MESH)
    for step in (1, 2, 3):
        pl.semaphore_signal(barrier, inc=1, device_id={"blk": lax.rem(z + step, 4)}, device_id_type=MESH)
    pl.semaphore_wait(barrier, devices + 2)

    def remote(source, target, send, recv, where):
        return pltpu.make_async_remote_copy(
            src_ref=source,
            dst_ref=target,
            send_sem=send,
            recv_sem=recv,
            device_id=where,
            device_id_type=MESH,
        )

    part = (share_ref.shape[2] - early) // 4
    part_at = pl.multiple_of(early + z * part, LANES)
    first, rest, biases = [], [], []
    for step in range(1, devices):
        to = lax.rem(place + step, devices)
        for copies, lo, size, send, recv in (
            (first, 0, early, first_send, first_recv),
            (rest, part_at, part, rest_send, rest_recv),
        ):
            copies.append(
                remote(
                    share_ref.at[to, :, pl.ds(lo, size)],
                    share_got.at[place, :, pl.ds(lo, size)],
                    send.at[step],
                    recv.at[step],
                    {"img": to},
                )
            )
        biases.append(remote(bias_ref, bias_out.at[place], bias_send.at[step], bias_recv.at[step], {"img": to}))
    for copy in first:
        copy.start()

    copies = {}

    def begin(k, which, block, rows, where):
        t, row, count = chunks[k]
        at = (block, pl.ds(row + rows[0], rows[1]))
        copies[k, which] = remote(
            fulls[t].at[at], fulls[t].at[at], send_sem.at[k, which], recv_sem.at[k, which], where
        )
        copies[k, which].start()

    def begin_own(k, which, where):
        t, row, count = chunks[k]
        source = shards[t].at[pl.ds(row, count)]
        copies[k, which] = remote(
            source, fulls[t].at[place, pl.ds(row, count)], send_sem.at[k, which], recv_sem.at[k, which], where
        )
        copies[k, which].start()

    own = [pltpu.make_async_copy(shards[t], fulls[t].at[place], own_sem.at[t]) for t in range(tensors)]
    def ahead(k):
        if k < len(chunks):
            begin_own(k, 0, {"img": beside})
            begin_own(k, 1, {"img": across})
            begin_own(k, 2, {"img": pair})

    ahead(0)
    for copy in rest + biases:
        copy.start()
    for k in range(1, 3):
        ahead(k)
    for copy in own:
        copy.start()

    share_got[place] = share_ref[place]
    bias_out[place] = bias_ref[...]
    for copy in first:
        copy.wait()

    def modulation_of(lo, size):
        at = pl.ds(lo, size)
        total = share_got[0, :, at]
        for i in range(1, devices):
            total = total + share_got[i, :, at]
        modulation_ref[:, at] = start_ref[:, at] + total

    modulation_of(0, early)
    for u in range(units):
        chosen = hot_ref[u : u + 1, 0:1] * modulation_ref[0:1, 0:early]
        for s in range(1, slots):
            chosen = chosen + hot_ref[u : u + 1, s : s + 1] * modulation_ref[s : s + 1, 0:early]
        at = pl.ds(u * unit, unit)
        values = x_ref[at, :].astype(F32)
        centered = values - jnp.mean(values, axis=1, keepdims=True)
        inverse = lax.rsqrt(jnp.mean(centered * centered, axis=1, keepdims=True) + EPSILON)
        rows_ref[z, at, :] = (centered * inverse * (1.0 + chosen[:, wide:]) + chosen[:, :wide]).astype(BF)

    up = [
        remote(block, block, line_send.at[0, s], line_recv.at[0, s], {"blk": lax.rem(z + 1, 4)})
        for s, block in ((s, rows_ref.at[lax.rem(z - s + 4, 4)]) for s in range(3))
    ]
    down = [
        remote(block, block, line_send.at[1, s], line_recv.at[1, s], {"blk": lax.rem(z + 3, 4)})
        for s, block in ((s, rows_ref.at[lax.rem(z + s, 4)]) for s in range(3))
    ]

    def line_step(s):
        if s > 0:
            pl.when(z >= s)(up[s - 1].wait_recv)
            pl.when(z + s < 4)(down[s - 1].wait_recv)
        if s < 3:
            pl.when((z >= s) & (z < 3))(up[s].start)
            pl.when((z + s < 4) & (z > 0))(down[s].start)

    def cut(k):
        return cut_rows(chunks[k][2], k)

    def relay(k):
        count, half = chunks[k][2], cut(k)
        copies[k, 0].wait_recv()
        begin(k, 3, beside, (0, half), {"img": across})
        begin(k, 5, beside, (0, count), {"img": pair})
        copies[k, 1].wait_recv()
        begin(k, 4, across, (half, count - half), {"img": beside})
        begin(k, 6, across, (0, count), {"img": pair})

    def last(k):
        count, half = chunks[k][2], cut(k)
        copies[k, 3].wait_recv()
        begin(k, 7, diagonal, (0, half), {"img": pair})
        copies[k, 4].wait_recv()
        begin(k, 8, diagonal, (half, count - half), {"img": pair})

    line_step(0)
    for copy in rest:
        copy.wait()
    modulation_of(part_at, part)
    own_part = modulation_ref.at[:, pl.ds(part_at, part)]
    spread = [
        remote(own_part, own_part, spread_send.at[step], spread_recv.at[step], {"blk": lax.rem(z + step, 4)})
        for step in (1, 2, 3)
    ]
    for copy in spread:
        copy.start()
    n = len(chunks)
    for k in range(n + 2):
        if k < n:
            relay(k)
            ahead(k + 3)
        if k >= 2:
            last(k - 2)
        for s in (1, 2):
            if k == 2 * s - 1:
                line_step(s)
    for copy in biases:
        copy.wait()
    line_step(3)
    for copy in spread:
        copy.wait()
    for copy in own:
        copy.wait()
    for k in range(n):
        for which in (0, 1, 3, 4):
            copies[k, which].wait_send()
        copies[k, 2].wait()
        for which in (5, 6, 7, 8):
            copies[k, which].wait()
    for s in range(3):
        pl.when((z >= s) & (z < 3))(up[s].wait_send)
        pl.when((z + s < 4) & (z > 0))(down[s].wait_send)


def gather_call(shards, unit_hot, rows, shares, bias_row, modulate_bias, collective_id):
    devices = shares.shape[0]
    slots, wide = shares.shape[1:]
    chunks = []
    for t, shard in enumerate(shards):
        depth = shard.shape[0]
        for row in range(0, depth, 144):
            chunks.append((t, row, min(144, depth - row)))
    n = len(chunks)
    vmem, anywhere = pl.BlockSpec(memory_space=pltpu.VMEM), pl.BlockSpec(memory_space=pl.ANY)
    dma = pltpu.SemaphoreType.DMA
    first_modulation = jnp.broadcast_to(modulate_bias.astype(F32)[None, :], (slots, wide))
    return pl.pallas_call(
        partial(gather_kernel, chunks, len(shards), 2 * rows.shape[1]),
        out_shape=[jax.ShapeDtypeStruct((devices, *s.shape), BF) for s in shards]
        + [
            jax.ShapeDtypeStruct((4, *rows.shape), BF),
            jax.ShapeDtypeStruct((slots, wide), F32),
            jax.ShapeDtypeStruct((devices, *bias_row.shape), F32),
        ],
        in_specs=[vmem] * 5 + [anywhere] * len(shards),
        out_specs=[anywhere] * len(shards) + [vmem] * 3,
        scratch_shapes=[
            pltpu.VMEM((devices, slots, wide), F32),
            dma((len(shards),)),
            dma((devices,)),
            dma((devices,)),
            dma((devices,)),
            dma((devices,)),
            dma((devices,)),
            dma((devices,)),
            dma((n, 9)),
            dma((n, 9)),
            dma((2, 3)),
            dma((2, 3)),
            dma((4,)),
            dma((4,)),
        ],
        compiler_params=pltpu.CompilerParams(
            collective_id=collective_id, has_side_effects=True, vmem_limit_bytes=48 * 2**20
        ),
        cost_estimate=pl.CostEstimate(flops=0, bytes_accessed=450 * 2**20, transcendentals=0),
        name=f"gather_{collective_id}",
    )(unit_hot, rows, shares, bias_row, first_modulation, *shards)


def pick_kernel(parts, mine, place_ref, weight_ref, out_ref):
    width = parts * mine
    padding = jnp.zeros((weight_ref.shape[0], out_ref.shape[1] - 3 * mine), BF)
    for part in range(parts):

        @pl.when(place_ref[0] == part)
        def _():
            starts = [which * width + part * mine for which in range(3)]
            pieces = [weight_ref[:, start : start + mine] for start in starts]
            out_ref[...] = jnp.concatenate(pieces + [padding], axis=1)


def pick_heads(weight, place, parts, mine):
    return pl.pallas_call(
        partial(pick_kernel, parts, mine),
        out_shape=jax.ShapeDtypeStruct((weight.shape[0], whole_lanes(3 * mine)), BF),
        in_specs=[pl.BlockSpec(memory_space=pltpu.SMEM), pl.BlockSpec(memory_space=pltpu.VMEM)],
        out_specs=pl.BlockSpec(memory_space=pltpu.VMEM),
        compiler_params=pltpu.CompilerParams(vmem_limit_bytes=32 * 2**20),
        name="pick_heads",
    )(place.astype(jnp.int32).reshape(1), weight)


def assemble_kernel(mine, parts_ref, out_ref):
    pieces = [
        parts_ref[part, :, which * mine : (which + 1) * mine].astype(F32)
        for which in range(3)
        for part in range(parts_ref.shape[0])
    ]
    out_ref[...] = jnp.concatenate(pieces, axis=1)


def assemble(parts, mine):
    return pl.pallas_call(
        partial(assemble_kernel, mine),
        out_shape=jax.ShapeDtypeStruct((parts.shape[1], 3 * mine * parts.shape[0]), F32),
        compiler_params=pltpu.CompilerParams(vmem_limit_bytes=32 * 2**20),
        name="assemble",
    )(parts)


def total_kernel(mine_ref, out_ref, lines, line_send, line_recv, send_sem, recv_sem):
    place, z = lax.axis_index("img"), lax.axis_index("blk")
    parts, devices = lines.shape[0], out_ref.shape[0]
    barrier = pltpu.get_barrier_semaphore()
    for step in range(1, parts):
        pl.semaphore_signal(barrier, inc=1, device_id={"blk": lax.rem(z + step, parts)}, device_id_type=MESH)
    for step in range(1, devices):
        pl.semaphore_signal(barrier, inc=1, device_id={"img": lax.rem(place + step, devices)}, device_id_type=MESH)
    pl.semaphore_wait(barrier, parts + devices - 2)

    lines[z] = mine_ref[...]
    copies = [
        pltpu.make_async_remote_copy(
            src_ref=lines.at[z],
            dst_ref=lines.at[z],
            send_sem=line_send.at[step],
            recv_sem=line_recv.at[step],
            device_id={"blk": lax.rem(z + step, parts)},
            device_id_type=MESH,
        )
        for step in range(1, parts)
    ]
    for copy in copies:
        copy.start()
    for copy in copies:
        copy.wait()
    total = lines[0]
    for step in range(1, parts):
        total = total + lines[step]
    out_ref[place] = total
    copies = [
        pltpu.make_async_remote_copy(
            src_ref=out_ref.at[place],
            dst_ref=out_ref.at[place],
            send_sem=send_sem.at[step],
            recv_sem=recv_sem.at[step],
            device_id={"img": lax.rem(place + step, devices)},
            device_id_type=MESH,
        )
        for step in range(1, devices)
    ]
    for copy in copies:
        copy.start()
    for copy in copies:
        copy.wait()


def total_call(mine, devices, parts, collective_id):
    if (devices, parts) != (8, 4):
        return lax.all_gather(lax.psum(mine, "blk"), "img", axis=0, tiled=False)
    return pl.pallas_call(
        total_kernel,
        out_shape=jax.ShapeDtypeStruct((devices, *mine.shape), mine.dtype),
        in_specs=[pl.BlockSpec(memory_space=pltpu.VMEM)],
        out_specs=pl.BlockSpec(memory_space=pltpu.VMEM),
        scratch_shapes=[
            pltpu.VMEM((parts, *mine.shape), mine.dtype),
            pltpu.SemaphoreType.DMA((parts,)),
            pltpu.SemaphoreType.DMA((parts,)),
            pltpu.SemaphoreType.DMA((devices,)),
            pltpu.SemaphoreType.DMA((devices,)),
        ],
        compiler_params=pltpu.CompilerParams(
            collective_id=collective_id, has_side_effects=True, vmem_limit_bytes=32 * 2**20
        ),
        name=f"total_{collective_id}",
    )(mine)


def per_device(
    inputs,
    token_image,
    image_time,
    image_class,
    targets,
    cotangent,
    class_table,
    modulate_weight,
    modulate_bias,
    attend_weight,
    attend_bias,
    output_weight,
    output_bias,
    expand_weight,
    expand_bias,
    shrink_weight,
    shrink_bias,
    inner_weight,
    inner_bias,
    middle_weight,
    middle_bias,
    outer_weight,
    outer_bias,
):
    count, width = inputs.shape
    head_dim = width // HEADS
    columns = class_table.shape[1]
    devices, parts = lax.axis_size("img"), lax.axis_size("blk")
    place_img, place_blk = lax.axis_index("img"), lax.axis_index("blk")
    slots = image_class.shape[0] // devices
    unit = SHORT // parts
    units = count // unit
    heads = HEADS // parts
    mine = heads * head_dim
    half = width // 2

    class_hot = (image_class[:, None] == jnp.arange(class_table.shape[0])[None, :]).astype(BF)
    column = place_img * columns + jnp.arange(columns)
    frequency = jnp.exp(-math.log(10000.0) * (column % half).astype(F32) / half)
    angle = image_time.astype(F32)[:, None] * frequency[None, :]
    condition = dot(class_hot, class_table) + jnp.where(column[None, :] < half, jnp.cos(angle), jnp.sin(angle))
    silu_condition = jax.nn.silu(condition).astype(BF)
    shares = dot(silu_condition, modulate_weight)
    biases = (attend_bias, output_bias, expand_bias, shrink_bias, inner_bias, middle_bias, outer_bias)
    longest = whole_lanes(max(bias.shape[0] for bias in biases))
    bias_row = jnp.stack([jnp.pad(bias.astype(F32), (0, longest - bias.shape[0])) for bias in biases])
    bias_row = jnp.pad(bias_row, ((0, 8 - len(biases)), (0, 0)))
    shares = shares.reshape(devices, slots, -1)

    labels = token_image[::unit]
    same = labels[:, None] == labels[None, :]
    start = jnp.argmax(same, axis=1).astype(jnp.int32)
    length = jnp.sum(same, axis=1).astype(jnp.int32)
    unit_hot = (labels[:, None] == jnp.arange(slots)[None, :]).astype(F32)
    def by_unit(values):
        return values.reshape(units, unit, width)

    def by_row(values):
        return values.reshape(count, width)

    attend_mine = pick_heads(attend_weight, place_blk, parts, mine)

    def gather(shard):
        return lax.all_gather(shard, "img", axis=0, tiled=True)

    source = by_unit(inputs.astype(F32))
    normal_one, inverse_one = layer_norm(source)
    first_weights = (attend_mine, output_weight, expand_weight, outer_weight, shrink_weight)
    if (devices, parts) == (8, 4):
        *fulls, rows_group, modulation, got_bias = gather_call(
            first_weights, unit_hot, inputs, shares, bias_row, modulate_bias, 3
        )
        fulls = [full.reshape(-1, full.shape[2]) for full in fulls]
        modulated_group = rows_group.reshape(parts * count, width)
    else:
        fulls = [gather(shard) for shard in first_weights]
        modulation = modulate_bias.astype(F32)[None, :] + lax.psum_scatter(
            shares.reshape(devices * slots, -1), "img", scatter_dimension=0, tiled=True
        )
        got_bias = lax.all_gather(bias_row, "img", axis=0, tiled=False)
        chosen = jnp.dot(unit_hot, modulation, precision=HIGH)[:, None, : 2 * width]
        modulated_one = normal_one * (1.0 + chosen[:, :, width:]) + chosen[:, :, :width]
        modulated_group = lax.all_gather(by_row(modulated_one.astype(BF)), "blk", axis=0, tiled=True)
    attend_full, output_full, expand_full, outer_full, shrink_full = fulls
    inner_shard, middle_shard, modulated_group = lax.optimization_barrier(
        (inner_weight, middle_weight, modulated_group)
    )
    inner_full, middle_full = gather(inner_shard), gather(middle_shard)
    full_biases = [got_bias[:, i, : bias.shape[0]].reshape(-1) for i, bias in enumerate(biases)]
    (
        attend_bias_full,
        output_bias_full,
        expand_bias_full,
        shrink_bias_full,
        inner_bias_full,
        middle_bias_full,
        outer_bias_full,
    ) = full_biases
    unit_modulation = jnp.dot(unit_hot, modulation, precision=HIGH)
    shift_one, scale_one, gate_one, shift_two, scale_two, gate_two = (
        block[:, None, :] for block in jnp.split(unit_modulation, 6, axis=1)
    )

    def pad_heads(values):
        lead = values.shape[:-1]
        values = values.reshape(*lead, 3 * heads, head_dim)
        values = jnp.pad(values, ((0, 0),) * len(lead) + ((0, 0), (0, LANES - head_dim)))
        return values.reshape(*lead, 3 * heads * LANES)

    bias_mine = lax.dynamic_slice_in_dim(attend_bias_full.reshape(2, parts, mine), place_blk, 1, axis=1)
    bias_mine = jnp.concatenate([bias_mine[0, 0], jnp.zeros((mine,), F32), bias_mine[1, 0]])
    is_value = jnp.arange(3 * heads * LANES) >= 2 * heads * LANES
    is_last = jnp.arange(3 * heads * LANES) % LANES == LANES - 1
    padded_bias = jnp.where(is_value & is_last, 1.0, pad_heads(bias_mine))
    projected = dot(modulated_group, pad_heads(attend_full[:, : 3 * mine])) + padded_bias[None, :]
    qkv = projected.astype(BF).reshape(parts, units, unit, 3 * heads * LANES)
    attended_heads, norms = attend_forward(start, length, qkv, heads, head_dim)
    attended = lax.all_to_all(
        attended_heads.reshape(parts, count, mine), "blk", split_axis=0, concat_axis=0, tiled=True
    )
    output_heads = output_full.reshape(parts, mine, width)
    branch_one = by_unit(
        jnp.einsum("pti,pio->to", attended, output_heads, preferred_element_type=F32) + output_bias_full
    )
    middle = source + gate_one * branch_one
    normal_two, inverse_two = layer_norm(middle)
    modulated_two = by_row((normal_two * (1.0 + scale_two) + shift_two).astype(BF))
    expanded = dot(modulated_two, expand_full) + expand_bias_full
    gelu_tanh = partial(jax.nn.gelu, approximate=True)
    activated = gelu_tanh(expanded).astype(BF)
    branch_two = by_unit(dot(activated, shrink_full) + shrink_bias_full)
    whole = middle + gate_two * branch_two
    whole_low = by_row(whole.astype(BF))
    pre_one = dot(whole_low, inner_full) + inner_bias_full
    first = jax.nn.silu(pre_one).astype(BF)
    pre_two = dot(first, middle_full) + middle_bias_full
    second = jax.nn.silu(pre_two).astype(BF)
    aligned = dot(second, outer_full) + outer_bias_full
    target = targets.astype(F32)
    cross = jnp.sum(aligned * target, axis=1)
    aligned_inverse = lax.rsqrt(jnp.sum(aligned * aligned, axis=1) + EPSILON)
    target_inverse = lax.rsqrt(jnp.sum(target * target, axis=1) + EPSILON)
    cosine = cross * aligned_inverse * target_inverse
    grad_aligned = (
        -0.5
        * (
            target * (aligned_inverse * target_inverse)[:, None]
            - (cosine * aligned_inverse * aligned_inverse)[:, None] * aligned
        )
    ).astype(BF)

    def scatter(values):
        return lax.psum_scatter(values, "img", scatter_dimension=0, tiled=True)

    grad_outer = left_product(second, grad_aligned)
    grad_outer_bias = column_sum(grad_aligned)
    grad_pre_two = local_back(jax.nn.silu, pre_two, right_product(grad_aligned, outer_full)).astype(BF)
    grad_middle_weight = left_product(first, grad_pre_two)
    grad_middle_bias = column_sum(grad_pre_two)
    grad_pre_one = local_back(jax.nn.silu, pre_one, right_product(grad_pre_two, middle_full)).astype(BF)
    grad_inner = left_product(whole_low, grad_pre_one)
    grad_inner_bias = column_sum(grad_pre_one)
    early_weights = jnp.concatenate(
        [g.reshape(devices, -1, g.shape[1]) for g in (grad_inner, grad_middle_weight)], axis=1
    )
    early_part = scatter(early_weights.reshape(-1, early_weights.shape[2]))
    grad_whole = by_unit(cotangent.astype(F32)) + by_unit(right_product(grad_pre_one, inner_full))
    grad_gate_two = grad_whole * branch_two
    grad_branch_two = by_row((grad_whole * gate_two).astype(BF))
    grad_shrink = left_product(activated, grad_branch_two)
    grad_shrink_bias = column_sum(grad_branch_two)
    grad_expanded = local_back(gelu_tanh, expanded, right_product(grad_branch_two, shrink_full)).astype(BF)
    grad_expand = left_product(modulated_two, grad_expanded)
    grad_expand_bias = column_sum(grad_expanded)
    grad_mod_two = by_unit(right_product(grad_expanded, expand_full))
    grad_scale_two = grad_mod_two * normal_two
    grad_middle = grad_whole + norm_back(grad_mod_two * (1.0 + scale_two), normal_two, inverse_two)
    grad_gate_one = grad_middle * branch_one
    grad_branch_one = by_row((grad_middle * gate_one).astype(BF))
    grad_output = jnp.einsum("pti,to->pio", attended, grad_branch_one, preferred_element_type=F32)
    grad_output = grad_output.astype(BF).reshape(width, width)
    grad_output_bias = column_sum(grad_branch_one)
    def slot_sum(*values):
        rows = jnp.concatenate([jnp.sum(v, axis=1) for v in values], axis=1)
        return jnp.dot(unit_hot.T, rows, precision=HIGH)

    early_slots = slot_sum(grad_gate_one, grad_mod_two, grad_scale_two, grad_gate_two)
    grad_attended = jnp.einsum("to,pio->pti", grad_branch_one, output_heads, preferred_element_type=F32)
    grad_heads = lax.all_to_all(grad_attended.astype(BF), "blk", split_axis=0, concat_axis=0, tiled=True)
    grad_heads, grad_shrink, grad_expand, grad_output, grad_outer = lax.optimization_barrier(
        (grad_heads, grad_shrink, grad_expand, grad_output, grad_outer)
    )
    grad_heads = grad_heads.reshape(parts, units, unit, mine)
    grad_qkv = attend_backward(start, length, qkv, norms, attended_heads, grad_heads, heads, head_dim).reshape(parts * count, -1)
    grad_tied, early_sum = lax.optimization_barrier((grad_qkv, lax.psum(early_part, "blk")))
    grad_attend = left_product(modulated_group, grad_tied)
    partial_mod_one = right_product(grad_qkv, attend_full).astype(BF)
    qkv_bias = column_sum(grad_qkv[:, : 3 * mine]).reshape(3, 1, mine)
    spread = (jnp.arange(parts) == place_blk).astype(F32)[None, :, None]
    attend_bias_rows = jnp.concatenate([qkv_bias[:1], qkv_bias[2:]]) * spread
    bias_grads = (
        attend_bias_rows,
        grad_output_bias,
        grad_expand_bias,
        grad_shrink_bias,
        grad_inner_bias,
        grad_middle_bias,
        grad_outer_bias,
    )
    bias_rows = jnp.concatenate([b.reshape(devices, -1) for b in bias_grads], axis=1)
    early_width = early_slots.shape[1]
    deep = max(slots, devices)
    early_rows = jnp.concatenate(
        [
            jnp.pad(early_slots, ((0, deep - slots), (0, 0))),
            jnp.pad(bias_rows, ((0, deep - devices), (0, whole_lanes(bias_rows.shape[1]) - bias_rows.shape[1]))),
        ],
        axis=1,
    )
    grads = (grad_outer, grad_attend, grad_output, grad_shrink, grad_expand)
    if (devices, parts) == (8, 4):
        *sums, early = reduce_call(grads, (), 1, early_rows, 640, 1)
    else:
        sums = [scatter(grad) for grad in grads]
        attend_part = lax.all_gather(sums[1], "blk", axis=0, tiled=False)
        sums = list(lax.psum(tuple(sums[:1] + sums[2:]), "blk"))
        sums.insert(1, attend_part)
        early = lax.all_gather(lax.psum(early_rows, "blk"), "img", axis=0, tiled=False)
    outer_sum, attend_parts, output_sum, shrink_sum, expand_sum = sums
    inner_sum, middle_sum = early_sum[: inner_weight.shape[0]], early_sum[inner_weight.shape[0] :]
    attend_sum = assemble(attend_parts, mine)
    grad_mod_one = lax.psum_scatter(partial_mod_one, "blk", scatter_dimension=0, tiled=True)
    grad_mod_one, early = lax.optimization_barrier((grad_mod_one, early))
    early_grad = early[:, :slots, :early_width].reshape(devices * slots, -1)
    grad_mod_one = by_unit(grad_mod_one.astype(F32))
    grad_scale_one = grad_mod_one * normal_one
    grad_source = grad_middle + norm_back(grad_mod_one * (1.0 + scale_one), normal_one, inverse_one)

    late_slots = slot_sum(grad_mod_one, grad_scale_one)
    late_grad = total_call(late_slots, devices, parts, 2).reshape(devices * slots, 2 * width)
    bias_sum = jnp.sum(lax.dynamic_index_in_dim(early, place_img, axis=1, keepdims=False)[:, early_width:], axis=0)
    bias_sums = []
    at = 0
    for bias in biases:
        bias_sums.append(bias_sum[at : at + bias.shape[0]])
        at += bias.shape[0]
    (
        attend_bias_sum,
        output_bias_sum,
        expand_bias_sum,
        shrink_bias_sum,
        inner_bias_sum,
        middle_bias_sum,
        outer_bias_sum,
    ) = bias_sums
    modulation_grad = jnp.concatenate([late_grad, early_grad], axis=1)
    modulate_sum = jnp.dot(silu_condition.astype(F32).T, modulation_grad, precision=HIGH)
    modulate_bias_sum = jnp.sum(modulation_grad, axis=0)
    silu_grad = jnp.dot(modulation_grad, modulate_weight.astype(F32).T, precision=HIGH)
    condition_grad = local_back(jax.nn.silu, condition, silu_grad)
    table_sum = jnp.dot(class_hot.astype(F32).T, condition_grad, precision=HIGH)
    return (
        whole_low,
        by_row(grad_source.astype(BF)),
        table_sum,
        modulate_sum,
        modulate_bias_sum,
        attend_sum.astype(F32),
        attend_bias_sum,
        output_sum.astype(F32),
        output_bias_sum,
        expand_sum.astype(F32),
        expand_bias_sum,
        shrink_sum.astype(F32),
        shrink_bias_sum,
        inner_sum.astype(F32),
        inner_bias_sum,
        middle_sum.astype(F32),
        middle_bias_sum,
        outer_sum.astype(F32),
        outer_bias_sum,
    )


def solution(mesh):
    in_specs = (
        P(("img", "blk"), None),
        P(("img", "blk")),
        P(),
        P(),
        P(("img", "blk"), None),
        P(("img", "blk"), None),
        P(None, "img"),
        P("img", None),
        P(),
        P("img", None),
        P("img"),
        P("img", None),
        P("img"),
        P("img", None),
        P("img"),
        P("img", None),
        P("img"),
        P("img", None),
        P("img"),
        P("img", None),
        P("img"),
        P("img", None),
        P("img"),
    )
    out_specs = (
        P(("img", "blk"), None),
        P(("img", "blk"), None),
        P(None, "img"),
        P("img", None),
        P(),
        P("img", None),
        P("img"),
        P("img", None),
        P("img"),
        P("img", None),
        P("img"),
        P("img", None),
        P("img"),
        P("img", None),
        P("img"),
        P("img", None),
        P("img"),
        P("img", None),
        P("img"),
    )
    return jax.shard_map(
        per_device, mesh=mesh, in_specs=in_specs, out_specs=out_specs, check_vma=False
    )
```
